32 devices in a mesh: grp: 2 (over y), tp: 4 (over z), dp: 4 (over x, core).
Axes of the slice: x: 2, y: 2, z: 4, core: 2. Of those that a mesh axis runs over, the one named last changes fastest.
Arguments:
- tokens: bfloat16 [1024, 8192], P(('grp', 'dp'), 'tp'), parts along dimension 0, may hold values from -6 to 6
- frozen_up_weight: bfloat16 [8192, 28672], P('dp', 'tp'), may hold values from -0.0625 to 0.0625
- adapter_down: bfloat16 [32, 8192, 64], P('dp', 'tp'), may hold values from -0.0625 to 0.0625
- adapter_up: bfloat16 [32, 64, 28672], P('dp', None, 'tp'), may hold values from -0.03125 to 0.03125
- cotangent: bfloat16 [1024, 28672], P(('grp', 'dp'), 'tp'), parts along dimension 0, may hold values from -0.59765625 to 0.59765625
- block_adapter: int32 [8], P('grp'), parts along dimension 0, may hold values from 0 to 31
- block_length: int32 [8], P('grp'), parts along dimension 0, may hold values from 1 to 128, as said below
- adapter_slot: int32 [32], replicated, may hold values from 0 to 31, each once
Outputs:
- projected: bfloat16 [1024, 28672], P(('grp', 'dp'), 'tp'), parts along dimension 0
- tokens_grad: bfloat16 [1024, 8192], P(('grp', 'dp'), 'tp'), parts along dimension 0
- down_grad: float32 [64, 8192, 64], P(('grp', 'dp'), 'tp'), parts along dimension 0
- up_grad: float32 [64, 64, 28672], P(('grp', 'dp'), None, 'tp'), parts along dimension 0
The draws below stay inside these ranges and needn't reach their ends.
There are 2 independent parts, one for each index of `grp`. The reference program is written for one: setup_inputs(seed, part) draws one part's arguments, and reference() takes and returns one part's arrays. A program takes and returns all parts, laid end to end along the dimension named above; an argument that names none is the same for every part. Nothing has to cross between parts.
Inputs may be any that keep to these rules, and one draw needn't show every extreme that they name: `block_adapter`: each block of 128 tokens serves the one adapter named here. The first block_length[k] tokens of block k are live, the rest are padding; some block is full. A permutation: adapter a's factors and gradients are entry adapter_slot[a] of the stores, held by dp index adapter_slot[a] // 8.
All inputs are finite; a program needn't handle non-finite values.
Results may differ from the reference program's by a relative error of at most 0.0028.
Values may be sent and summed in bfloat16 or wider, within the bound.
No kernel may reach another device: no remote copies, remote signals or barrier semaphores. Data moves between devices by JAX's collectives and lax.ppermute only.
A program may use at most 384 MiB of HBM per device.

```python
import jax
import jax.numpy as jnp
from jax import lax

D = 8192
HIDDEN_UNITS = 28672
RANK = 64
SEGMENT_BLOCK = 128
TOKEN_TOTAL = 512
ADAPTERS = 32
BLOCKS = 4


def draw_block_length(key, part):
    key = jax.random.fold_in(key, 11)
    length_key, full_key = jax.random.split(key)
    lengths = jax.random.randint(length_key, (BLOCKS,), 1, SEGMENT_BLOCK + 1)
    full_block = jax.random.randint(full_key, (), 0, BLOCKS)
    return jnp.where(jnp.arange(BLOCKS) == full_block, SEGMENT_BLOCK, lengths).astype(jnp.int32)


def set_ends(array, stream_key, low, largest):
    spot = [jax.random.randint(jax.random.fold_in(stream_key, axis), (), 0, length) for axis, length in enumerate(array.shape)]
    longest = array.shape.index(max(array.shape))
    neighbour = spot[:longest] + [(spot[longest] + 1) % array.shape[longest]] + spot[longest + 1:]
    return array.at[tuple(spot)].set(low).at[tuple(neighbour)].set(largest)


def block_levels(own_key, extent, pieces, least, top_value):
    factor_of, own = 1.0, jax.random.fold_in(own_key, 6)
    for axis_at, parts in pieces:
        draws = jnp.exp(jax.random.uniform(jax.random.fold_in(own, axis_at), (parts,), jnp.float32, least / len(pieces), top_value / len(pieces)))
        factor_of = factor_of * jnp.repeat(draws, extent[axis_at] // parts).reshape([-1 if axis == axis_at else 1 for axis in range(len(extent))])
    return factor_of


def centred(rng, extent, spread, limit, pieces=(), dtype=jnp.bfloat16):
    values = spread * jax.random.normal(rng, extent, jnp.float32)
    if pieces:
        values = values * block_levels(rng, extent, pieces, -0.22, 0.18)
    return jnp.clip(values, -limit, limit).astype(dtype)


def setup_inputs(seed: int = 0, part: int = 0) -> dict:
    key_of = jax.random.split(jax.random.key(seed), 9)
    part_keys = jax.random.split(jax.random.fold_in(key_of[8], part), 9)
    return {
        "tokens": centred(part_keys[0], (TOKEN_TOTAL, D), 1.0, 6.0, ((0, 4), (1, 4))),
        "frozen_up_weight": centred(key_of[1], (D, HIDDEN_UNITS), D ** -0.5, 0.0625, ((0, 4), (1, 4))),
        "adapter_down": centred(key_of[2], (ADAPTERS, D, RANK), D ** -0.5, 0.0625, ((0, 4), (1, 4))),
        "adapter_up": centred(key_of[3], (ADAPTERS, RANK, HIDDEN_UNITS), HIDDEN_UNITS ** -0.5, 0.03125, ((0, 4), (2, 4))),
        "cotangent": centred(part_keys[4], (TOKEN_TOTAL, HIDDEN_UNITS), 0.1, 0.59765625, ((0, 4), (1, 4))),
        "block_adapter": set_ends(jax.random.randint(part_keys[5], (BLOCKS,), 0, ADAPTERS), jax.random.fold_in(part_keys[5], 1), 0, ADAPTERS - 1).astype(jnp.int32),
        "block_length": draw_block_length(jax.random.fold_in(jax.random.fold_in(key_of[8], part), 71), part),
        "adapter_slot": jax.random.permutation(key_of[7], ADAPTERS).astype(jnp.int32),
    }


adapter_scale = 2.0
highest_precision = lax.Precision.HIGHEST


def reference(tokens, frozen_up_weight, adapter_down, adapter_up, cotangent, block_adapter, block_length, adapter_slot):
    total_blocks = TOKEN_TOTAL // SEGMENT_BLOCK
    slot_ids = adapter_slot[block_adapter]
    live_mask = (lax.broadcasted_iota(jnp.int32, (total_blocks, SEGMENT_BLOCK), 1) < block_length[:, None]).astype(jnp.float32)
    token_blocks = tokens.astype(jnp.float32).reshape(total_blocks, SEGMENT_BLOCK, D) * live_mask[:, :, None]
    cotangent_blocks = cotangent.astype(jnp.float32).reshape(total_blocks, SEGMENT_BLOCK, HIDDEN_UNITS) * live_mask[:, :, None]
    down_sel = adapter_down[slot_ids].astype(jnp.float32)
    up_selection = adapter_up[slot_ids].astype(jnp.float32)
    rank_inner = jnp.einsum("gbd,gdr->gbr", token_blocks, down_sel, precision=highest_precision)
    inner_adapter_product = lax.optimization_barrier(rank_inner.astype(jnp.bfloat16)).astype(jnp.float32)
    adapter_delta = adapter_scale * jnp.einsum("qto,qox->qtx", inner_adapter_product, up_selection, precision=highest_precision)
    projected = (jnp.dot(tokens, frozen_up_weight, preferred_element_type=jnp.float32) + adapter_delta.reshape(TOKEN_TOTAL, HIDDEN_UNITS)).astype(jnp.bfloat16)
    rank_return = adapter_scale * jnp.einsum("axc,akc->axk", cotangent_blocks, up_selection, precision=highest_precision)
    back_b = lax.optimization_barrier(rank_return.astype(jnp.bfloat16)).astype(jnp.float32)
    correction = jnp.einsum("gbr,gdr->gbd", back_b, down_sel, precision=highest_precision)
    tokens_grad = (jnp.dot(cotangent, frozen_up_weight.T, preferred_element_type=jnp.float32) + correction.reshape(TOKEN_TOTAL, D)).astype(jnp.bfloat16)
    up_products = adapter_scale * jnp.einsum("pzy,pzu->pyu", inner_adapter_product, cotangent_blocks, precision=highest_precision)
    down_terms = jnp.einsum("gbd,gbr->gdr", token_blocks, back_b, precision=highest_precision)
    up_grad = jnp.zeros((ADAPTERS, RANK, HIDDEN_UNITS), jnp.float32).at[slot_ids].add(up_products)
    down_grad = jnp.zeros((ADAPTERS, D, RANK), jnp.float32).at[slot_ids].add(down_terms)
    return projected, tokens_grad, down_grad, up_grad
```

```python
import jax
import jax.numpy as jnp
from jax import lax
from jax.sharding import PartitionSpec as P

SEGMENT_BLOCK = 128

adapter_scale = 2.0
CHUNKS = 4


def dot(a, b, contract):
    return lax.dot_general(a, b, ((contract[:1], contract[1:]), ((), ())), preferred_element_type=jnp.float32)


def make_local(groups, shards):
    square = groups == shards
    bits = [1 << n for n in range((groups - 1).bit_length())]

    def swap(x, bit):
        return lax.ppermute(x, "dp", [(d, d ^ bit) for d in range(groups)])

    def gather(x):
        blocks = {0: x}
        for bit in reversed(bits):
            blocks.update({q | bit: swap(block, bit) for q, block in blocks.items()})
        return [blocks[q] for q in range(groups)]

    def transpose(x):
        pairs = [(c * groups + r, (r ^ c) * groups + c) for r in range(groups) for c in range(shards)]
        return lax.ppermute(x, ("tp", "dp"), pairs)

    def untranspose(x):
        pairs = [((r ^ c) * groups + c, c * groups + r) for r in range(groups) for c in range(shards)]
        return lax.ppermute(x, ("tp", "dp"), pairs)

    def local(tokens, weight, adapter_down, adapter_up, cotangent, block_adapter, block_length, adapter_slot):
        rows, width = tokens.shape
        depth, hidden = weight.shape
        per_owner, _, rank = adapter_down.shape
        i, j = lax.axis_index("dp"), lax.axis_index("tp")
        order = jnp.arange(groups, dtype=jnp.int32) ^ i
        match = block_adapter[:, None] == jnp.arange(adapter_slot.shape[0], dtype=jnp.int32)[None, :]
        slots = jnp.sum(jnp.where(match, adapter_slot[None, :], 0), axis=1)[order]
        lengths = block_length[order]
        owned = slots // per_owner == i
        local_ids = slots % per_owner
        live = (lax.broadcasted_iota(jnp.int32, (groups, rows), 1) < lengths[:, None]).astype(jnp.float32)
        down_t = jnp.swapaxes(adapter_down, 1, 2)
        zero = jnp.zeros((), jnp.bfloat16)

        def chosen(store):
            return [
                jnp.where(owned[q], lax.dynamic_index_in_dim(store, local_ids[q], 0, False), zero)
                for q in range(groups)
            ]

        down_sel, up_sel = chosen(down_t), chosen(adapter_up)
        if square:
            all_tokens = lax.all_gather(transpose(tokens), "tp", axis=0, tiled=True)
        else:
            whole = lax.all_gather(lax.all_gather(tokens, "dp", axis=0), "tp", axis=2, tiled=True)
            whole = lax.dynamic_slice_in_dim(whole, i * depth, depth, 2)
            all_tokens = whole[order].reshape(groups * rows, depth)
        token_blocks = gather(tokens)
        cot_blocks = gather(cotangent)
        cot_all = jnp.concatenate(cot_blocks, axis=0)
        tok_all = jnp.concatenate(token_blocks, axis=0)

        parts = list(down_sel)
        held = groups
        for bit in bits:
            parts = [parts[2 * n] + swap(parts[2 * n + 1], bit) for n in range(held // 2)]
            held //= 2
        down_mine = parts[0]

        inner = jnp.stack([dot(token_blocks[q], down_sel[q], (1, 1)) for q in range(groups)])
        inner = lax.psum(inner, "tp") * live[:, :, None]
        inner_b = inner.astype(jnp.bfloat16)
        back = jnp.stack([dot(cot_blocks[q], up_sel[q], (1, 1)) for q in range(groups)])
        back = lax.psum(back[order], ("tp", "dp"))[order] * (adapter_scale * live)[:, :, None]
        back_b = back.astype(jnp.bfloat16)

        one_hot = (local_ids[:, None] == jnp.arange(per_owner, dtype=jnp.int32)[None, :]) & owned[:, None]

        def spread(x):
            wide = jnp.where(one_hot[:, None, :, None], x[:, :, None, :], zero)
            return wide.reshape(groups * rows, per_owner * rank)

        inner_wide = spread(inner_b) * jnp.bfloat16(adapter_scale)
        back_wide = spread(back_b)
        up_flat = adapter_up.reshape(per_owner * rank, hidden)

        total = dot(cot_all, weight, (1, 1))
        if square:
            total = lax.psum_scatter(total, "tp", scatter_dimension=0, tiled=True)
            mine = lax.dynamic_index_in_dim(back_b, j, 0, False)
            total = total + dot(mine, transpose(down_mine), (1, 0))
            tokens_grad = untranspose(total.astype(jnp.bfloat16))
        else:
            placed = jnp.zeros((groups, rows, groups, depth), jnp.float32)
            placed = lax.dynamic_update_slice_in_dim(
                placed, total.reshape(groups, rows, 1, depth)[order], i, 2
            )
            placed = lax.psum_scatter(placed, "dp", scatter_dimension=0, tiled=False)
            placed = placed.reshape(rows, groups * depth)
            placed = lax.psum_scatter(placed, "tp", scatter_dimension=1, tiled=True)
            tokens_grad = (placed + dot(back_b[0], down_mine, (1, 0))).astype(jnp.bfloat16)

        pieces = CHUNKS if hidden % (CHUNKS * 128) == 0 else 1
        step = hidden // pieces
        outs = []
        for n in range(pieces):
            cols = slice(n * step, (n + 1) * step)
            part = dot(all_tokens, weight[:, cols], (1, 0)) + dot(inner_wide, up_flat[:, cols], (1, 0))
            parts = [part[q * rows : (q + 1) * rows] for q in range(groups)]
            held = groups
            for bit in bits:
                sent = [parts[2 * m + 1] for m in range(held // 2)]
                if bit == bits[-1]:
                    sent = [x.astype(jnp.bfloat16) for x in sent]
                parts = [parts[2 * m] + swap(sent[m], bit).astype(jnp.float32) for m in range(held // 2)]
                held //= 2
            outs.append(parts[0].astype(jnp.bfloat16))
        projected = jnp.concatenate(outs, axis=1)

        up_grad = dot(inner_wide, cot_all, (0, 0)).reshape(per_owner, rank, hidden)
        down_grad = dot(back_wide, tok_all, (0, 0)).reshape(per_owner, rank, width)
        return projected, tokens_grad, jnp.swapaxes(down_grad, 1, 2), up_grad

    return local


def solution(mesh):
    placed = (
        P(("grp", "dp"), "tp"),
        P("dp", "tp"),
        P("dp", "tp", None),
        P("dp", None, "tp"),
        P(("grp", "dp"), "tp"),
        P("grp"),
        P("grp"),
        P(),
    )
    return jax.shard_map(
        make_local(mesh.shape["dp"], mesh.shape["tp"]),
        mesh=mesh,
        in_specs=placed,
        out_specs=(
            P(("grp", "dp"), "tp"),
            P(("grp", "dp"), "tp"),
            P(("grp", "dp"), "tp", None),
            P(("grp", "dp"), None, "tp"),
        ),
        check_vma=False,
    )
```

```python
import functools

import jax
import jax.numpy as jnp
from jax import lax
from jax.experimental import pallas as pl
from jax.experimental.pallas import tpu as pltpu
from jax.sharding import PartitionSpec as P

SEGMENT_BLOCK = 128

adapter_scale = 2.0
CORE, CHIP = 1, 2
PLACE_BLOCK = (0, 2, 3, 1)
BLOCK_PLACE = (0, 3, 1, 2)
VMEM = 40 * 1024 * 1024


def dot(a, b, contract):
    return lax.dot_general(a, b, ((contract[:1], contract[1:]), ((), ())), preferred_element_type=jnp.float32)


def after(x, *others):
    return lax.optimization_barrier((x,) + others)[0]


def cost(flops, moved):
    return pl.CostEstimate(flops=flops, bytes_accessed=moved, transcendentals=0)


def project(first, second, wide, weight, up_flat, start, stop, block):
    rows, depth = first.shape
    span = wide.shape[1]
    count = (stop - start) // block
    base = start // block

    def kernel(a_ref, b_ref, wide_ref, w_ref, up_ref, keep_ref, send_ref, lhs):
        @pl.when(pl.program_id(0) == 0)
        def _():
            lhs[:rows] = a_ref[...]
            lhs[rows:] = b_ref[...]

        total = dot(lhs[...], w_ref[...], (1, 0)) + dot(wide_ref[...], up_ref[...], (1, 0))
        keep_ref[...] = total[:rows]
        send_ref[...] = total[rows:]

    whole = lambda n: (0, 0)
    return pl.pallas_call(
        kernel,
        grid=(count,),
        in_specs=[
            pl.BlockSpec((rows, depth), whole),
            pl.BlockSpec((rows, depth), whole),
            pl.BlockSpec((2 * rows, span), whole),
            pl.BlockSpec((depth, block), lambda n: (0, n + base)),
            pl.BlockSpec((span, block), lambda n: (0, n + base)),
        ],
        out_specs=[pl.BlockSpec((rows, block), lambda n: (0, n))] * 2,
        out_shape=[jax.ShapeDtypeStruct((rows, stop - start), jnp.float32)] * 2,
        scratch_shapes=[pltpu.VMEM((2 * rows, depth), first.dtype)],
        compiler_params=pltpu.CompilerParams(vmem_limit_bytes=VMEM),
        cost_estimate=cost(4 * rows * (depth + span) * (stop - start), 2 * (depth + span + 4 * rows) * (stop - start)),
        name="project",
    )(first, second, wide, weight, up_flat)


def return_grad(first, second, weight):
    rows, hidden = first.shape
    depth = weight.shape[0]
    block = 256

    def kernel(a_ref, b_ref, w_ref, out_ref, lhs):
        @pl.when(pl.program_id(0) == 0)
        def _():
            lhs[:rows] = a_ref[...]
            lhs[rows:] = b_ref[...]

        out_ref[...] = dot(lhs[...], w_ref[...], (1, 1))

    whole = lambda n: (0, 0)
    return pl.pallas_call(
        kernel,
        grid=(depth // block,),
        in_specs=[
            pl.BlockSpec((rows, hidden), whole),
            pl.BlockSpec((rows, hidden), whole),
            pl.BlockSpec((block, hidden), lambda n: (n, 0)),
        ],
        out_specs=pl.BlockSpec((2 * rows, block), lambda n: (0, n)),
        out_shape=jax.ShapeDtypeStruct((2 * rows, depth), jnp.float32),
        scratch_shapes=[pltpu.VMEM((2 * rows, hidden), first.dtype)],
        compiler_params=pltpu.CompilerParams(vmem_limit_bytes=VMEM),
        cost_estimate=cost(4 * rows * hidden * depth, 2 * hidden * (depth + 2 * rows)),
        name="return_grad",
    )(first, second, weight)


def rank_back(up_flat, blocks, one_hot, rank):
    span, hidden = up_flat.shape
    rows = blocks[0].shape[0]
    groups = len(blocks)
    block = 1024
    slots = span // rank

    def kernel(up_ref, *refs):
        cots, hot_ref, out_ref, total = refs[:groups], refs[groups], refs[groups + 1], refs[groups + 2]
        n = pl.program_id(0)

        @pl.when(n == 0)
        def _():
            total[...] = jnp.zeros_like(total)

        cot = jnp.concatenate([c[...] for c in cots], axis=0)
        total[...] += dot(up_ref[...], cot, (1, 1))

        @pl.when(n == pl.num_programs(0) - 1)
        def _():
            acc = jnp.zeros((rank, groups * rows), jnp.float32)
            for s in range(slots):
                part = slice(s * rank, (s + 1) * rank)
                acc += total[part] * hot_ref[s : s + 1, :]
            out_ref[...] = acc

    return pl.pallas_call(
        kernel,
        grid=(hidden // block,),
        in_specs=[pl.BlockSpec((span, block), lambda n: (0, n))]
        + [pl.BlockSpec((rows, block), lambda n: (0, n))] * groups
        + [pl.BlockSpec((slots, groups * rows), lambda n: (0, 0))],
        out_specs=pl.BlockSpec((rank, groups * rows), lambda n: (0, 0)),
        out_shape=jax.ShapeDtypeStruct((rank, groups * rows), jnp.float32),
        scratch_shapes=[pltpu.VMEM((span, groups * rows), jnp.float32)],
        compiler_params=pltpu.CompilerParams(vmem_limit_bytes=VMEM),
        cost_estimate=cost(2 * span * groups * rows * hidden, 2 * hidden * (span + groups * rows)),
        name="rank_back",
    )(up_flat, *blocks, one_hot)


def slot_grad(wide_t, blocks, block):
    span = wide_t.shape[0]
    rows, columns = blocks[0].shape
    groups = len(blocks)

    def kernel(wide_ref, *refs):
        values = jnp.concatenate([c[...] for c in refs[:groups]], axis=0)
        refs[groups][...] = dot(wide_ref[...], values, (1, 0))

    return pl.pallas_call(
        kernel,
        grid=(columns // block,),
        in_specs=[pl.BlockSpec((span, groups * rows), lambda n: (0, 0))]
        + [pl.BlockSpec((rows, block), lambda n: (0, n))] * groups,
        out_specs=pl.BlockSpec((span, block), lambda n: (0, n)),
        out_shape=jax.ShapeDtypeStruct((span, columns), jnp.float32),
        compiler_params=pltpu.CompilerParams(vmem_limit_bytes=VMEM),
        cost_estimate=cost(2 * span * groups * rows * columns, (4 * span + 2 * groups * rows) * columns),
        name="slot_grad",
    )(wide_t, *blocks)


def block_facts(block_adapter, block_length, adapter_slot, order, rows, per_owner, i):
    match = block_adapter[:, None] == jnp.arange(adapter_slot.shape[0], dtype=jnp.int32)[None, :]
    slots = jnp.sum(jnp.where(match, adapter_slot[None, :], 0), axis=1)[order]
    lengths = block_length[order]
    owned = slots // per_owner == i
    local_ids = slots % per_owner
    groups = order.shape[0]
    live = (lax.broadcasted_iota(jnp.int32, (groups, rows), 1) < lengths[:, None]).astype(jnp.float32)
    return owned, local_ids, live


def chosen(store, owned, local_ids):
    zero = jnp.zeros((), store.dtype)
    return [
        jnp.where(owned[q], lax.dynamic_index_in_dim(store, local_ids[q], 0, False), zero)
        for q in range(owned.shape[0])
    ]


def local_square(
    tokens, weight, adapter_down, adapter_up, cotangent, block_adapter, block_length, adapter_slot
):
    groups = shards = 4
    rows, width = tokens.shape
    depth, hidden = weight.shape
    per_owner, _, rank = adapter_down.shape
    span = per_owner * rank
    i, j = lax.axis_index("dp"), lax.axis_index("tp")
    order = jnp.arange(groups, dtype=jnp.int32) ^ i

    def swap(x, bit):
        return lax.ppermute(x, "dp", [(d, d ^ bit) for d in range(groups)])

    def along(x, pairs):
        return lax.ppermute(x, "tp", pairs)

    def turn(x, sources):
        pairs = [(c * groups + r, z * groups + d) for (r, c), (d, z) in sources]
        return lax.ppermute(x, ("tp", "dp"), pairs)

    everyone = [(r, c) for r in range(groups) for c in range(shards)]
    near = [(r, c) for r, c in everyone if r // CHIP == c // CHIP]

    tok_x = swap(tokens, CHIP)
    cot_c = swap(cotangent, CORE)
    cot_x = swap(after(cotangent, tok_x), CHIP)
    tok_c, tok_xc = swap(tokens, CORE), swap(tok_x, CORE)
    cot_xc = swap(cot_x, CORE)
    toks, cots = [tokens, tok_c, tok_x, tok_xc], [cotangent, cot_c, cot_x, cot_xc]

    owned, local_ids, live = block_facts(
        block_adapter, block_length, adapter_slot, order, rows, per_owner, i
    )
    one_hot = (jnp.arange(per_owner, dtype=jnp.int32)[:, None] == local_ids[None, :]) & owned[None, :]
    hot = jnp.repeat(one_hot.astype(jnp.float32), rows, axis=1)
    live_row = live.reshape(1, groups * rows)

    mid, low = (j == 1) | (j == 2), j < 2
    far = turn(tok_x, [((r, c), (c, BLOCK_PLACE[r ^ CHIP ^ c])) for r, c in near])
    own = turn(after(tokens, tok_x), [((r, c), (c, BLOCK_PLACE[r ^ c])) for r, c in near])
    grad01 = return_grad(after(cotangent, tok_x), cot_c, weight)
    far = after(far, grad01)

    def pair(a, b):
        return jnp.where(low, a, b), jnp.where(low, b, a)

    across = along(far, [(1, 2), (2, 1)])
    out = along(far, [(1, 0), (2, 3)])
    onward = along(across, [(1, 0), (2, 3)])
    rows2, rows3 = pair(jnp.where(mid, far, out), jnp.where(mid, across, onward))
    own = after(own, across)
    hop = along(own, [(0, 1), (3, 2)])
    skip = along(own, [(0, 2), (3, 1)])
    last = along(skip, [(2, 3), (1, 0)])
    rows0, rows1 = pair(jnp.where(mid, hop, own), jnp.where(mid, skip, last))

    down_sel = chosen(jnp.swapaxes(adapter_down, 1, 2), owned, local_ids)
    down_near = swap(jnp.stack([down_sel[1], down_sel[3]]), CORE)
    down_far = swap(down_sel[2] + down_near[1], CHIP)
    down_mine = turn(
        down_sel[0] + down_near[0] + down_far, [((r, c), (c, BLOCK_PLACE[r ^ c])) for r, c in everyone]
    )

    def total_tp(x):
        for bit in (1, 2):
            x = x + along(x, [(z, z ^ bit) for z in range(shards)])
        return x

    def spread(x):
        hot_b = hot.astype(jnp.bfloat16)
        return (hot_b[:, None, :] * x[None, :, :]).reshape(span, groups * rows)

    inner = jnp.concatenate([dot(down_sel[q], toks[q], (1, 1)) for q in range(groups)], axis=1)
    inner_b = (total_tp(inner) * live_row).astype(jnp.bfloat16)
    inner_wide = spread(inner_b * jnp.bfloat16(adapter_scale))
    inner_rows = inner_wide.T
    up_flat = adapter_up.reshape(span, hidden)

    block = 512
    steps = hidden // block
    pieces = 4 if steps >= 4 else 1
    edges = [(-(-steps * n // pieces)) * block for n in range(pieces + 1)]
    crossing, waiting = [], []

    def cross(point):
        keep, send = waiting.pop(0)
        summed = (after(keep, point) + swap(send, CORE)).astype(jnp.bfloat16)
        crossing.append(swap(summed, CHIP))
        return summed

    point = rows2
    for a, b in zip(edges, edges[1:]):
        waiting.append(project(after(rows2, point), rows3, inner_rows[2 * rows :], weight, up_flat, a, b, block))
        point = waiting[-1][0]
        if len(waiting) > 1:
            point = cross(point)
    grad01 = after(grad01, point)
    point = cross(point)
    grad23 = return_grad(after(cot_x, point), cot_xc, weight)

    def grad_block(both, at):
        return lax.dynamic_slice_in_dim(both, at * rows, rows, 0)

    b16 = jnp.bfloat16
    second = (j >= 2).astype(jnp.int32)
    early = [
        along(grad_block(grad01, second), [(1, 0), (2, 3)]),
        along(grad_block(grad01, 1 - second).astype(b16), [(2, 0), (1, 3)]),
        along(grad_block(grad01, 1 - second).astype(b16), [(3, 0), (0, 3)]),
    ]
    late = [
        along(grad_block(grad23, second), [(0, 1), (3, 2)]),
        along(grad_block(grad23, 1 - second).astype(b16), [(2, 1), (1, 2)]),
        along(grad_block(grad23, 1 - second).astype(b16), [(3, 1), (0, 2)]),
    ]

    back = rank_back(after(up_flat, grad23), cots, hot, rank)
    back_b = (total_tp(back) * (adapter_scale * live_row)).astype(b16)
    shared = [back_b[:, q * rows : (q + 1) * rows] for q in range(groups)]
    for bit in (CORE, CHIP):
        got = swap(jnp.stack(shared), bit)
        shared = [shared[q] + got[q ^ bit] for q in range(groups)]
    q_mine = jnp.asarray(PLACE_BLOCK, jnp.int32)[j]
    back_mine = lax.dynamic_index_in_dim(jnp.stack(shared), q_mine, 0, False)

    total = jnp.where(mid, grad_block(grad23, second), grad_block(grad01, second))
    for part in early + late:
        total = total + part.astype(jnp.float32)
    total = total + dot(back_mine, down_mine, (0, 0))
    tokens_grad = turn(
        total.astype(b16), [((c, BLOCK_PLACE[r ^ c]), (r, c)) for r, c in everyone]
    )

    keep, send = project(after(rows0, back), rows1, inner_rows[: 2 * rows], weight, up_flat, 0, hidden, block)
    mine = keep + swap(send, CORE)
    projected = jnp.concatenate(
        [
            (mine[:, a:b] + part.astype(jnp.float32)).astype(b16)
            for a, b, part in zip(edges, edges[1:], crossing)
        ],
        axis=1,
    )

    up_grad = slot_grad(after(inner_wide, keep), cots, 1024).reshape(per_owner, rank, hidden)
    down_grad = slot_grad(spread(back_b), toks, 1024).reshape(per_owner, rank, width)
    return projected, tokens_grad, jnp.swapaxes(down_grad, 1, 2), up_grad


def local_any(
    groups, tokens, weight, adapter_down, adapter_up, cotangent, block_adapter, block_length, adapter_slot
):
    bits = [1 << n for n in range((groups - 1).bit_length())]

    def swap(x, bit):
        return lax.ppermute(x, "dp", [(d, d ^ bit) for d in range(groups)])

    def gather(x):
        blocks = {0: x}
        for bit in reversed(bits):
            blocks.update({q | bit: swap(block, bit) for q, block in blocks.items()})
        return jnp.stack([blocks[q] for q in range(groups)])

    def combine(parts):
        for bit in bits:
            parts = [a + swap(b, bit) for a, b in zip(parts[::2], parts[1::2])]
        return parts[0]

    rows, width = tokens.shape
    depth, hidden = weight.shape
    per_owner, _, rank = adapter_down.shape
    i = lax.axis_index("dp")
    order = jnp.arange(groups, dtype=jnp.int32) ^ i
    owned, local_ids, live = block_facts(
        block_adapter, block_length, adapter_slot, order, rows, per_owner, i
    )
    down_sel = chosen(adapter_down, owned, local_ids)
    up_sel = chosen(adapter_up, owned, local_ids)
    all_tokens = lax.all_gather(lax.all_gather(tokens, "dp", axis=0), "tp", axis=2, tiled=True)
    all_tokens = lax.dynamic_slice_in_dim(all_tokens, i * depth, depth, 2)[order]
    all_tokens = all_tokens.reshape(groups * rows, depth)
    toks, cots = gather(tokens), gather(cotangent)
    tok_all, cot_all = toks.reshape(-1, width), cots.reshape(-1, hidden)
    down_mine = combine(down_sel)
    inner = jnp.stack([dot(toks[q], down_sel[q], (1, 0)) for q in range(groups)])
    inner_b = (lax.psum(inner, "tp") * live[:, :, None]).astype(jnp.bfloat16)
    back = jnp.stack([dot(cots[q], up_sel[q], (1, 1)) for q in range(groups)])
    back = lax.psum(back[order], ("tp", "dp"))[order] * (adapter_scale * live)[:, :, None]
    back_b = back.astype(jnp.bfloat16)
    one_hot = (local_ids[:, None] == jnp.arange(per_owner, dtype=jnp.int32)[None, :]) & owned[:, None]

    def spread(x):
        wide = jnp.where(one_hot[:, None, :, None], x[:, :, None, :], jnp.zeros((), x.dtype))
        return wide.reshape(groups * rows, per_owner * rank)

    inner_wide = spread(inner_b) * jnp.bfloat16(adapter_scale)
    total = dot(cot_all, weight, (1, 1)).reshape(groups, rows, 1, depth)[order]
    placed = jnp.zeros((groups, rows, groups, depth), jnp.float32)
    placed = lax.dynamic_update_slice_in_dim(placed, total, i, 2)
    placed = lax.psum_scatter(placed, "dp", scatter_dimension=0, tiled=False)
    placed = placed.reshape(rows, groups * depth)
    placed = lax.psum_scatter(placed, "tp", scatter_dimension=1, tiled=True)
    tokens_grad = (placed + dot(back_b[0], down_mine, (1, 1))).astype(jnp.bfloat16)
    part = dot(all_tokens, weight, (1, 0)) + dot(inner_wide, adapter_up.reshape(-1, hidden), (1, 0))
    projected = combine(list(part.reshape(groups, rows, hidden))).astype(jnp.bfloat16)
    up_grad = dot(inner_wide, cot_all, (0, 0)).reshape(per_owner, rank, hidden)
    down_grad = dot(spread(back_b), tok_all, (0, 0)).reshape(per_owner, rank, width)
    return projected, tokens_grad, jnp.swapaxes(down_grad, 1, 2), up_grad


def solution(mesh):
    placed = (
        P(("grp", "dp"), "tp"),
        P("dp", "tp"),
        P("dp", "tp", None),
        P("dp", None, "tp"),
        P(("grp", "dp"), "tp"),
        P("grp"),
        P("grp"),
        P(),
    )
    groups, shards = mesh.shape["dp"], mesh.shape["tp"]
    square = groups == shards == 4
    return jax.shard_map(
        local_square if square else functools.partial(local_any, groups),
        mesh=mesh,
        in_specs=placed,
        out_specs=(
            P(("grp", "dp"), "tp"),
            P(("grp", "dp"), "tp"),
            P(("grp", "dp"), "tp", None),
            P(("grp", "dp"), None, "tp"),
        ),
        check_vma=False,
    )
```

```python
import functools

import jax
import jax.numpy as jnp
from jax import lax
from jax.experimental import pallas as pl
from jax.experimental.pallas import tpu as pltpu
from jax.sharding import PartitionSpec as P

SEGMENT_BLOCK = 128

adapter_scale = 2.0
CORE, CHIP = 1, 2
VMEM = 48 * 1024 * 1024


def dot(a, b, contract):
    return lax.dot_general(a, b, ((contract[:1], contract[1:]), ((), ())), preferred_element_type=jnp.float32)


def after(x, *others):
    return lax.optimization_barrier((x,) + others)[0]


def cost(flops, moved):
    return pl.CostEstimate(flops=flops // 256, bytes_accessed=moved // 256, transcendentals=0)


def project(tokens, wide, weight, up_flat, start, stop, block):
    rows, depth = tokens.shape
    span = wide.shape[1]
    quarter = rows // 4
    base = start // block

    def kernel(tok_ref, wide_ref, w_ref, up_ref, keep_ref, send_ref):
        total = dot(tok_ref[...], w_ref[...], (1, 0)) + dot(wide_ref[...], up_ref[...], (1, 0))
        keep_ref[0] = total[:quarter]
        send_ref[0] = total[quarter : 2 * quarter]
        keep_ref[1] = total[2 * quarter : 3 * quarter]
        send_ref[1] = total[3 * quarter :]

    whole = lambda n: (0, 0)
    return pl.pallas_call(
        kernel,
        grid=((stop - start) // block,),
        in_specs=[
            pl.BlockSpec((rows, depth), whole),
            pl.BlockSpec((rows, span), whole),
            pl.BlockSpec((depth, block), lambda n: (0, n + base)),
            pl.BlockSpec((span, block), lambda n: (0, n + base)),
        ],
        out_specs=[pl.BlockSpec((2, quarter, block), lambda n: (0, 0, n))] * 2,
        out_shape=[jax.ShapeDtypeStruct((2, quarter, stop - start), jnp.float32)] * 2,
        compiler_params=pltpu.CompilerParams(vmem_limit_bytes=VMEM),
        cost_estimate=cost(2 * rows * (depth + span) * (stop - start), (2 * depth + 2 * span + 4 * rows) * (stop - start)),
        name="project",
    )(tokens, wide, weight, up_flat)


def return_grad(first, second, weight, half, sums=()):
    rows, hidden = first.shape
    depth = weight.shape[0]
    block = 512

    def kernel(a_ref, b_ref, w_ref, *refs):
        out_ref, sums_ref, rhs = refs[-3:]

        @pl.when(pl.program_id(0) == 0)
        def _():
            rhs[:rows] = a_ref[...]
            rhs[rows:] = b_ref[...]

        total = dot(w_ref[...], rhs[...], (1, 1)).T
        out_ref[...] = total
        sums_ref[...] = total.astype(sums_ref.dtype)

    whole = lambda n: (0, 0)
    return pl.pallas_call(
        kernel,
        grid=(depth // block,),
        in_specs=[
            pl.BlockSpec((rows, hidden), whole),
            pl.BlockSpec((rows, hidden), whole),
            pl.BlockSpec((block, hidden), lambda n: (n, 0)),
        ]
        + [pl.BlockSpec(memory_space=pl.ANY)] * len(sums),
        out_specs=[
            pl.BlockSpec((2 * rows, block), lambda n: (0, n)),
            pl.BlockSpec((2 * rows, block), lambda n: (half, n)),
        ],
        out_shape=[
            jax.ShapeDtypeStruct((2 * rows, depth), jnp.float32),
            jax.ShapeDtypeStruct((4 * rows, depth), first.dtype),
        ],
        input_output_aliases={3: 1} if sums else {},
        scratch_shapes=[pltpu.VMEM((2 * rows, hidden), first.dtype)],
        compiler_params=pltpu.CompilerParams(vmem_limit_bytes=VMEM),
        cost_estimate=cost(4 * rows * hidden * depth, 2 * hidden * (depth + 2 * rows)),
        name="return_grad",
    )(first, second, weight, *sums)


def rank_sum(facts, flat, blocks, places, rank, scale, block):
    span, columns = flat.shape
    rows = blocks[0].shape[0]
    count = len(blocks)
    slots = span // rank
    groups = facts.shape[0] // 2

    def kernel(facts_ref, flat_ref, *refs):
        out_ref, total = refs[count], refs[count + 1]
        n = pl.program_id(0)
        values = jnp.concatenate([c[...] for c in refs[:count]], axis=0)
        product = dot(flat_ref[...], values, (1, 1))

        @pl.when(n == 0)
        def _():
            total[...] = product

        @pl.when(n > 0)
        def _():
            total[...] += product

        @pl.when(n == pl.num_programs(0) - 1)
        def _():
            for at, place in enumerate(places):
                acc = jnp.zeros((rank, rows), jnp.float32)
                for s in range(slots):
                    part = total[s * rank : (s + 1) * rank, at * rows : (at + 1) * rows]
                    acc = jnp.where(facts_ref[place] == s, part, acc)
                alive = lax.broadcasted_iota(jnp.int32, (rank, rows), 1) < facts_ref[groups + place]
                out_ref[:, at * rows : (at + 1) * rows] = jnp.where(alive, acc * scale, 0.0)

    return pl.pallas_call(
        kernel,
        grid=(columns // block,),
        in_specs=[pl.BlockSpec(memory_space=pltpu.SMEM), pl.BlockSpec((span, block), lambda n: (0, n))]
        + [pl.BlockSpec((rows, block), lambda n: (0, n))] * count,
        out_specs=pl.BlockSpec((rank, count * rows), lambda n: (0, 0)),
        out_shape=jax.ShapeDtypeStruct((rank, count * rows), jnp.float32),
        scratch_shapes=[pltpu.VMEM((span, count * rows), jnp.float32)],
        compiler_params=pltpu.CompilerParams(vmem_limit_bytes=VMEM),
        cost_estimate=cost(2 * span * count * rows * columns, 2 * columns * (span + count * rows)),
        name="rank_sum",
    )(facts, flat, *blocks)


def spread(facts, here, there, slots, scale):
    rank, tokens = here.shape
    groups = facts.shape[0] // 2
    rows = tokens // groups

    def kernel(facts_ref, a_ref, b_ref, wide_ref, turned_ref, sum_ref):
        x = (a_ref[...] + b_ref[...]).astype(jnp.bfloat16)
        sum_ref[...] = x
        x = x.astype(jnp.float32) * scale
        for q in range(groups):
            part = x[:, q * rows : (q + 1) * rows]
            for s in range(slots):
                value = jnp.where(facts_ref[q] == s, part, 0.0)
                wide_ref[s * rank : (s + 1) * rank, q * rows : (q + 1) * rows] = value.astype(jnp.bfloat16)
        turned_ref[...] = wide_ref[...].astype(jnp.float32).T.astype(jnp.bfloat16)

    return pl.pallas_call(
        kernel,
        in_specs=[pl.BlockSpec(memory_space=pltpu.SMEM)] + [pl.BlockSpec(memory_space=pltpu.VMEM)] * 2,
        out_specs=[pl.BlockSpec(memory_space=pltpu.VMEM)] * 3,
        out_shape=[
            jax.ShapeDtypeStruct((slots * rank, tokens), jnp.bfloat16),
            jax.ShapeDtypeStruct((tokens, slots * rank), jnp.bfloat16),
            jax.ShapeDtypeStruct((rank, tokens), jnp.bfloat16),
        ],
        compiler_params=pltpu.CompilerParams(vmem_limit_bytes=VMEM),
        cost_estimate=cost(0, 8 * slots * rank * tokens),
        name="spread",
    )(facts, here, there)


def slot_grad(wide_t, blocks, block):
    span = wide_t.shape[0]
    rows, columns = blocks[0].shape
    groups = len(blocks)

    def kernel(wide_ref, *refs):
        values = jnp.concatenate([c[...] for c in refs[:groups]], axis=0)
        refs[groups][...] = dot(wide_ref[...], values, (1, 0))

    return pl.pallas_call(
        kernel,
        grid=(columns // block,),
        in_specs=[pl.BlockSpec((span, groups * rows), lambda n: (0, 0))]
        + [pl.BlockSpec((rows, block), lambda n: (0, n))] * groups,
        out_specs=pl.BlockSpec((span, block), lambda n: (0, n)),
        out_shape=jax.ShapeDtypeStruct((span, columns), jnp.float32),
        compiler_params=pltpu.CompilerParams(vmem_limit_bytes=VMEM),
        cost_estimate=cost(2 * span * groups * rows * columns, (4 * span + 2 * groups * rows) * columns),
        name="slot_grad",
    )(wide_t, *blocks)


def block_facts(block_adapter, block_length, adapter_slot, order, rows, per_owner, i):
    match = block_adapter[:, None] == jnp.arange(adapter_slot.shape[0], dtype=jnp.int32)[None, :]
    slots = jnp.sum(jnp.where(match, adapter_slot[None, :], 0), axis=1)[order]
    lengths = block_length[order]
    owned = slots // per_owner == i
    local_ids = slots % per_owner
    groups = order.shape[0]
    live = (lax.broadcasted_iota(jnp.int32, (groups, rows), 1) < lengths[:, None]).astype(jnp.float32)
    return owned, local_ids, live


def chosen(store, owned, local_ids):
    zero = jnp.zeros((), store.dtype)
    return [
        jnp.where(owned[q], lax.dynamic_index_in_dim(store, local_ids[q], 0, False), zero)
        for q in range(owned.shape[0])
    ]


def own_facts(block_adapter, block_length, adapter_slot, groups, per_owner, i):
    place = jnp.arange(groups, dtype=jnp.int32)
    at = ((place[:, None] ^ i) == place[None, :]).astype(jnp.int32)
    named = jnp.sum(at * block_adapter[None, :], axis=1)
    match = named[:, None] == jnp.arange(adapter_slot.shape[0], dtype=jnp.int32)[None, :]
    slots = jnp.sum(jnp.where(match, adapter_slot[None, :], 0), axis=1)
    here = slots - i * per_owner
    here = jnp.where((here >= 0) & (here < per_owner), here, -1)
    return jnp.concatenate([here, jnp.sum(at * block_length[None, :], axis=1)])


def local_square(
    tokens, weight, adapter_down, adapter_up, cotangent, block_adapter, block_length, adapter_slot
):
    groups = shards = 4
    rows, width = tokens.shape
    depth, hidden = weight.shape
    per_owner, _, rank = adapter_down.shape
    span = per_owner * rank
    b16 = jnp.bfloat16
    i, j = lax.axis_index("dp"), lax.axis_index("tp")

    def swap(x, bit):
        return lax.ppermute(x, "dp", [(d, d ^ bit) for d in range(groups)])

    def along(x, bit):
        return lax.ppermute(x, "tp", [(z, z ^ bit) for z in range(shards)])

    forth = [(c * groups + r, (r ^ c) * groups + c) for r in range(groups) for c in range(shards)]
    back_again = [(b, a) for a, b in forth]

    def turn(x, pairs):
        return lax.ppermute(x, ("tp", "dp"), pairs)

    turned = turn(tokens, forth)
    tok_x = swap(tokens, CHIP)
    cot_c = swap(cotangent, CORE)
    facts = own_facts(block_adapter, block_length, adapter_slot, groups, per_owner, i)
    down_flat = jnp.swapaxes(adapter_down, 1, 2).reshape(span, width)
    up_flat = adapter_up.reshape(span, hidden)

    def chosen(q):
        at = jnp.maximum(facts[q], 0) * rank
        return jnp.where(facts[q] >= 0, lax.dynamic_slice_in_dim(down_flat, at, rank, 0), jnp.zeros((), b16))

    all_tokens = lax.all_gather(turned, "tp", axis=0, tiled=True)
    cot_x = swap(after(cotangent, tok_x, turned), CHIP)

    mixed = swap(jnp.concatenate([tokens, after(tok_x, turned), chosen(1), chosen(3)], axis=0), CORE)
    toks = [tokens, mixed[:rows], tok_x, mixed[rows : 2 * rows]]
    down_x = swap(chosen(2) + mixed[2 * rows + rank :], CHIP)
    inner = rank_sum(facts, down_flat, toks, (0, 1, 2, 3), rank, 1.0, width)
    inner = inner + along(inner, 1)
    down_mine = turn(chosen(0) + mixed[2 * rows : 2 * rows + rank] + down_x, forth)
    inner_wide, inner_rows, _ = spread(facts, after(inner, down_mine), along(inner, 2), per_owner, adapter_scale)

    grad01, parts = return_grad(after(cotangent, inner_rows), cot_c, weight, 0)
    back01 = rank_sum(facts, after(up_flat, grad01), [cotangent, cot_c], (0, 1), rank, adapter_scale, 1024)
    all_tokens = after(all_tokens, back01)
    cot_xc = swap(after(cot_x, all_tokens), CORE)
    grad23, parts = return_grad(cot_x, cot_xc, weight, 1, (parts,))
    parts = lax.all_to_all(parts.reshape(shards, rows, depth), "tp", 0, 0, tiled=True)
    back23 = rank_sum(facts, after(up_flat, grad23), [cot_x, cot_xc], (2, 3), rank, adapter_scale, 1024)
    back = jnp.concatenate([back01, back23], axis=1)

    def grad_block(q):
        low = lax.dynamic_slice_in_dim(grad01, (q & 1) * rows, rows, 0)
        high = lax.dynamic_slice_in_dim(grad23, (q & 1) * rows, rows, 0)
        return jnp.where(q < 2, low, high)

    def share(x, got, bit):
        return x + jnp.concatenate([got[:, (q ^ bit) * rows : ((q ^ bit) + 1) * rows] for q in range(groups)], axis=1)

    block = 512
    steps = hidden // block
    pieces = 4
    edges = [(-(-steps * n // pieces)) * block for n in range(pieces + 1)]
    kept, sent, got_c, got_x, done = [], [], [], [], []

    def make(n, *points):
        keep, send = project(after(all_tokens, *points), inner_rows, weight, up_flat, edges[n], edges[n + 1], block)
        kept.append(keep)
        got_c.append(swap(send, CORE))
        return keep

    def cross(n, *points):
        summed = (after(kept[n], *points)[1] + got_c[n][1]).astype(b16)
        got_x.append(swap(summed, CHIP))
        return summed

    def finish(n, *points):
        done.append((after(kept[n], *points)[0] + got_c[n][0] + got_x[n].astype(jnp.float32)).astype(b16))
        return done[-1]

    point = make(0, back23)
    back = back + along(back, 1)
    point = make(1, point, back)
    back_wide, _, back_b = spread(facts, after(back, point), along(back, 2), per_owner, 1.0)
    point = cross(0, back_b)
    point = make(2, point)
    back_b = share(after(back_b, point), swap(back_b, CORE), CORE)
    point = cross(1, back_b)
    point = finish(0, point)
    point = make(3, point)
    back_b = share(after(back_b, point), swap(back_b, CHIP), CHIP)
    point = cross(2, back_b)
    point = finish(1, point)
    down_wide = slot_grad(after(back_wide, point), toks, 1024)
    point = cross(3, down_wide)
    up_wide = slot_grad(after(inner_wide, point), [cotangent, cot_c, cot_x, cot_xc], 1024)
    point = finish(2, up_wide)

    back_mine = lax.dynamic_slice_in_dim(back_b, j * rows, rows, 1)
    total = grad_block(j)
    for m in range(1, shards):
        total = total + lax.dynamic_index_in_dim(parts, j ^ m, 0, False).astype(jnp.float32)
    total = total + dot(after(back_mine, point), down_mine, (0, 0))
    tokens_grad = turn(total.astype(b16), back_again)
    finish(3, total)
    projected = jnp.concatenate(done, axis=1)
    up_grad = up_wide.reshape(per_owner, rank, hidden)
    down_grad = jnp.swapaxes(down_wide.reshape(per_owner, rank, width), 1, 2)
    return projected, tokens_grad, down_grad, up_grad


def local_any(
    groups, tokens, weight, adapter_down, adapter_up, cotangent, block_adapter, block_length, adapter_slot
):
    bits = [1 << n for n in range((groups - 1).bit_length())]

    def swap(x, bit):
        return lax.ppermute(x, "dp", [(d, d ^ bit) for d in range(groups)])

    def gather(x):
        blocks = {0: x}
        for bit in reversed(bits):
            blocks.update({q | bit: swap(block, bit) for q, block in blocks.items()})
        return jnp.stack([blocks[q] for q in range(groups)])

    def combine(parts):
        for bit in bits:
            parts = [a + swap(b, bit) for a, b in zip(parts[::2], parts[1::2])]
        return parts[0]

    rows, width = tokens.shape
    depth, hidden = weight.shape
    per_owner, _, rank = adapter_down.shape
    i = lax.axis_index("dp")
    order = jnp.arange(groups, dtype=jnp.int32) ^ i
    owned, local_ids, live = block_facts(
        block_adapter, block_length, adapter_slot, order, rows, per_owner, i
    )
    down_sel = chosen(adapter_down, owned, local_ids)
    up_sel = chosen(adapter_up, owned, local_ids)
    all_tokens = lax.all_gather(lax.all_gather(tokens, "dp", axis=0), "tp", axis=2, tiled=True)
    all_tokens = lax.dynamic_slice_in_dim(all_tokens, i * depth, depth, 2)[order]
    all_tokens = all_tokens.reshape(groups * rows, depth)
    toks, cots = gather(tokens), gather(cotangent)
    tok_all, cot_all = toks.reshape(-1, width), cots.reshape(-1, hidden)
    down_mine = combine(down_sel)
    inner = jnp.stack([dot(toks[q], down_sel[q], (1, 0)) for q in range(groups)])
    inner_b = (lax.psum(inner, "tp") * live[:, :, None]).astype(jnp.bfloat16)
    back = jnp.stack([dot(cots[q], up_sel[q], (1, 1)) for q in range(groups)])
    back = lax.psum(back[order], ("tp", "dp"))[order] * (adapter_scale * live)[:, :, None]
    back_b = back.astype(jnp.bfloat16)
    one_hot = (local_ids[:, None] == jnp.arange(per_owner, dtype=jnp.int32)[None, :]) & owned[:, None]

    def spread(x):
        wide = jnp.where(one_hot[:, None, :, None], x[:, :, None, :], jnp.zeros((), x.dtype))
        return wide.reshape(groups * rows, per_owner * rank)

    inner_wide = spread(inner_b) * jnp.bfloat16(adapter_scale)
    total = dot(cot_all, weight, (1, 1)).reshape(groups, rows, 1, depth)[order]
    placed = jnp.zeros((groups, rows, groups, depth), jnp.float32)
    placed = lax.dynamic_update_slice_in_dim(placed, total, i, 2)
    placed = lax.psum_scatter(placed, "dp", scatter_dimension=0, tiled=False)
    placed = placed.reshape(rows, groups * depth)
    placed = lax.psum_scatter(placed, "tp", scatter_dimension=1, tiled=True)
    tokens_grad = (placed + dot(back_b[0], down_mine, (1, 1))).astype(jnp.bfloat16)
    part = dot(all_tokens, weight, (1, 0)) + dot(inner_wide, adapter_up.reshape(-1, hidden), (1, 0))
    projected = combine(list(part.reshape(groups, rows, hidden))).astype(jnp.bfloat16)
    up_grad = dot(inner_wide, cot_all, (0, 0)).reshape(per_owner, rank, hidden)
    down_grad = dot(spread(back_b), tok_all, (0, 0)).reshape(per_owner, rank, width)
    return projected, tokens_grad, jnp.swapaxes(down_grad, 1, 2), up_grad


def solution(mesh):
    placed = (
        P(("grp", "dp"), "tp"),
        P("dp", "tp"),
        P("dp", "tp", None),
        P("dp", None, "tp"),
        P(("grp", "dp"), "tp"),
        P("grp"),
        P("grp"),
        P(),
    )
    groups, shards = mesh.shape["dp"], mesh.shape["tp"]
    square = groups == shards == 4
    return jax.shard_map(
        local_square if square else functools.partial(local_any, groups),
        mesh=mesh,
        in_specs=placed,
        out_specs=(
            P(("grp", "dp"), "tp"),
            P(("grp", "dp"), "tp"),
            P(("grp", "dp"), "tp", None),
            P(("grp", "dp"), None, "tp"),
        ),
        check_vma=False,
    )
```

```python
import functools

import jax
import jax.numpy as jnp
from jax import lax
from jax.experimental import pallas as pl
from jax.experimental.pallas import tpu as pltpu
from jax.sharding import PartitionSpec as P

SEGMENT_BLOCK = 128

adapter_scale = 2.0
CORE, CHIP = 1, 2
VMEM = 48 * 1024 * 1024


def dot(a, b, contract):
    return lax.dot_general(a, b, ((contract[:1], contract[1:]), ((), ())), preferred_element_type=jnp.float32)


def after(x, *others):
    return lax.optimization_barrier((x,) + others)[0]


def cost(flops, moved):
    return pl.CostEstimate(flops=flops // 256, bytes_accessed=moved // 256, transcendentals=0)


def project(facts, near, far, wide, weight, up_flat, start, stop, block):
    _, rows, depth = near.shape
    groups = 4
    span = wide.shape[1]
    base = start // block

    def kernel(facts_ref, near_ref, far_ref, wide_ref, w_ref, up_ref, keep_ref, send_ref, lhs):
        @pl.when(pl.program_id(0) == 0)
        def _():
            for m in range(groups):
                at = pl.multiple_of((facts_ref[2 * groups] ^ m) * rows, rows)
                lhs[pl.ds(at, rows)] = (far_ref if m & 1 else near_ref)[m >> 1]

        total = dot(lhs[...], w_ref[...], (1, 0)) + dot(wide_ref[...], up_ref[...], (1, 0))
        keep_ref[0] = total[:rows]
        send_ref[0] = total[rows : 2 * rows]
        keep_ref[1] = total[2 * rows : 3 * rows]
        send_ref[1] = total[3 * rows :]

    whole = lambda n: (0, 0, 0)
    return pl.pallas_call(
        kernel,
        grid=((stop - start) // block,),
        in_specs=[
            pl.BlockSpec(memory_space=pltpu.SMEM),
            pl.BlockSpec((2, rows, depth), whole),
            pl.BlockSpec((2, rows, depth), whole),
            pl.BlockSpec((groups * rows, span), lambda n: (0, 0)),
            pl.BlockSpec((depth, block), lambda n: (0, n + base)),
            pl.BlockSpec((span, block), lambda n: (0, n + base)),
        ],
        out_specs=[pl.BlockSpec((2, rows, block), lambda n: (0, 0, n))] * 2,
        out_shape=[jax.ShapeDtypeStruct((2, rows, stop - start), jnp.float32)] * 2,
        scratch_shapes=[pltpu.VMEM((groups * rows, depth), near.dtype)],
        compiler_params=pltpu.CompilerParams(vmem_limit_bytes=VMEM),
        cost_estimate=cost(2 * groups * rows * (depth + span) * (stop - start), 2 * (depth + span + 2 * groups * rows) * (stop - start)),
        name="project",
    )(facts, near, far, wide, weight, up_flat)


def return_grad(first, second, weight, half, start, stop, sums=()):
    rows, hidden = first.shape
    depth = weight.shape[0]
    block = 256
    base = start // block

    def kernel(a_ref, b_ref, w_ref, *refs):
        out_ref, sums_ref, rhs = refs[-3:]

        @pl.when(pl.program_id(0) == 0)
        def _():
            rhs[:rows] = a_ref[...]
            rhs[rows:] = b_ref[...]

        total = dot(w_ref[...], rhs[...], (1, 1)).T
        out_ref[...] = total
        sums_ref[...] = total.astype(sums_ref.dtype)

    whole = lambda n: (0, 0)
    return pl.pallas_call(
        kernel,
        grid=((stop - start) // block,),
        in_specs=[
            pl.BlockSpec((rows, hidden), whole),
            pl.BlockSpec((rows, hidden), whole),
            pl.BlockSpec((block, hidden), lambda n: (n + base, 0)),
        ]
        + [pl.BlockSpec(memory_space=pl.ANY)] * len(sums),
        out_specs=[
            pl.BlockSpec((2 * rows, block), lambda n: (0, n)),
            pl.BlockSpec((2 * rows, block), lambda n: (half, n + base)),
        ],
        out_shape=[
            jax.ShapeDtypeStruct((2 * rows, stop - start), jnp.float32),
            jax.ShapeDtypeStruct((4 * rows, depth), first.dtype),
        ],
        input_output_aliases={3: 1} if sums else {},
        scratch_shapes=[pltpu.VMEM((2 * rows, hidden), first.dtype)],
        compiler_params=pltpu.CompilerParams(vmem_limit_bytes=VMEM),
        cost_estimate=cost(4 * rows * hidden * (stop - start), 2 * hidden * (stop - start + 2 * rows)),
        name="return_grad",
    )(first, second, weight, *sums)


def rank_back(facts, store, blocks, places, block):
    _, rank, columns = store.shape
    rows = blocks[0].shape[0]
    count = len(blocks)
    groups = facts.shape[0] // 2

    def kernel(facts_ref, *refs):
        slots, values, out_ref, total = refs[:count], refs[count : 2 * count], refs[-2], refs[-1]
        n = pl.program_id(0)
        left = jnp.concatenate([r[0] for r in slots], axis=0)
        right = jnp.concatenate([r[...] for r in values], axis=0)
        product = dot(left, right, (1, 1))

        @pl.when(n == 0)
        def _():
            total[...] = product

        @pl.when(n > 0)
        def _():
            total[...] += product

        @pl.when(n == pl.num_programs(0) - 1)
        def _():
            for at, place in enumerate(places):
                part = total[at * rank : (at + 1) * rank, at * rows : (at + 1) * rows]
                alive = lax.broadcasted_iota(jnp.int32, (rank, rows), 1) < facts_ref[groups + place]
                alive = alive & (facts_ref[place] >= 0)
                out_ref[:, at * rows : (at + 1) * rows] = jnp.where(alive, part * adapter_scale, 0.0)

    def chosen_slot(place):
        return lambda n, facts_ref: (jnp.maximum(facts_ref[place], 0), 0, n)

    return pl.pallas_call(
        kernel,
        grid_spec=pltpu.PrefetchScalarGridSpec(
            num_scalar_prefetch=1,
            grid=(columns // block,),
            in_specs=[pl.BlockSpec((1, rank, block), chosen_slot(place)) for place in places]
            + [pl.BlockSpec((rows, block), lambda n, facts_ref: (0, n))] * count,
            out_specs=pl.BlockSpec((rank, count * rows), lambda n, facts_ref: (0, 0)),
            scratch_shapes=[pltpu.VMEM((count * rank, count * rows), jnp.float32)],
        ),
        out_shape=jax.ShapeDtypeStruct((rank, count * rows), jnp.float32),
        compiler_params=pltpu.CompilerParams(vmem_limit_bytes=VMEM),
        cost_estimate=cost(2 * count * rank * count * rows * columns, 2 * columns * count * (rank + rows)),
        name="rank_back",
    )(facts, *[store] * count, *blocks)


def spread(facts, here, there, slots, scale):
    rank, tokens = here.shape
    groups = facts.shape[0] // 2
    rows = tokens // groups
    values = [here] if there is None else [here, there]

    def kernel(facts_ref, *refs):
        wide_ref, turned_ref, sum_ref = refs[-3:]
        x = sum(r[...] for r in refs[:-3]).astype(jnp.bfloat16)
        sum_ref[...] = x
        x = x.astype(jnp.float32) * scale
        for q in range(groups):
            part = x[:, q * rows : (q + 1) * rows]
            for s in range(slots):
                value = jnp.where(facts_ref[q] == s, part, 0.0)
                wide_ref[s * rank : (s + 1) * rank, q * rows : (q + 1) * rows] = value.astype(jnp.bfloat16)
        turned_ref[...] = wide_ref[...].astype(jnp.float32).T.astype(jnp.bfloat16)

    return pl.pallas_call(
        kernel,
        in_specs=[pl.BlockSpec(memory_space=pltpu.SMEM)] + [pl.BlockSpec(memory_space=pltpu.VMEM)] * len(values),
        out_specs=[pl.BlockSpec(memory_space=pltpu.VMEM)] * 3,
        out_shape=[
            jax.ShapeDtypeStruct((slots * rank, tokens), jnp.bfloat16),
            jax.ShapeDtypeStruct((tokens, slots * rank), jnp.bfloat16),
            jax.ShapeDtypeStruct((rank, tokens), jnp.bfloat16),
        ],
        compiler_params=pltpu.CompilerParams(vmem_limit_bytes=VMEM),
        cost_estimate=cost(0, 8 * slots * rank * tokens),
        name="spread",
    )(facts, *values)


def slot_grad(wide_t, blocks, block):
    span = wide_t.shape[0]
    rows, columns = blocks[0].shape
    groups = len(blocks)

    def kernel(wide_ref, *refs):
        values = jnp.concatenate([c[...] for c in refs[:groups]], axis=0)
        refs[groups][...] = dot(wide_ref[...], values, (1, 0))

    return pl.pallas_call(
        kernel,
        grid=(columns // block,),
        in_specs=[pl.BlockSpec((span, groups * rows), lambda n: (0, 0))]
        + [pl.BlockSpec((rows, block), lambda n: (0, n))] * groups,
        out_specs=pl.BlockSpec((span, block), lambda n: (0, n)),
        out_shape=jax.ShapeDtypeStruct((span, columns), jnp.float32),
        compiler_params=pltpu.CompilerParams(vmem_limit_bytes=VMEM),
        cost_estimate=cost(2 * span * groups * rows * columns, (4 * span + 2 * groups * rows) * columns),
        name="slot_grad",
    )(wide_t, *blocks)


def block_facts(block_adapter, block_length, adapter_slot, order, rows, per_owner, i):
    match = block_adapter[:, None] == jnp.arange(adapter_slot.shape[0], dtype=jnp.int32)[None, :]
    slots = jnp.sum(jnp.where(match, adapter_slot[None, :], 0), axis=1)[order]
    lengths = block_length[order]
    owned = slots // per_owner == i
    local_ids = slots % per_owner
    groups = order.shape[0]
    live = (lax.broadcasted_iota(jnp.int32, (groups, rows), 1) < lengths[:, None]).astype(jnp.float32)
    return owned, local_ids, live


def chosen(store, owned, local_ids):
    zero = jnp.zeros((), store.dtype)
    return [
        jnp.where(owned[q], lax.dynamic_index_in_dim(store, local_ids[q], 0, False), zero)
        for q in range(owned.shape[0])
    ]


def choose(block_adapter, block_length, adapter_slot, here, store):
    slots, rank, width = store.shape
    groups = block_adapter.shape[0]

    def block_of(step):
        return jnp.clip(jnp.where(step < 2, 2 * step + 1, 6 - 2 * step), 0, groups - 1)

    def slot_of(q, adapter_ref, slot_ref, here_ref):
        return slot_ref[adapter_ref[q ^ here_ref[0]]] - here_ref[0] * slots

    def kernel(adapter_ref, length_ref, slot_ref, here_ref, store_ref, near_ref, rest_ref, facts_ref):
        step = pl.program_id(0)

        @pl.when(step == 0)
        def _():
            for q in range(groups):
                at = slot_of(q, adapter_ref, slot_ref, here_ref)
                facts_ref[q] = jnp.where((at >= 0) & (at < slots), at, -1)
                facts_ref[groups + q] = length_ref[q ^ here_ref[0]]
            facts_ref[2 * groups] = here_ref[1]

        at = slot_of(block_of(step), adapter_ref, slot_ref, here_ref)
        value = store_ref[0] * ((at >= 0) & (at < slots)).astype(store_ref.dtype)

        @pl.when(step < 2)
        def _():
            near_ref[...] = value

        @pl.when(step >= 2)
        def _():
            rest_ref[...] = value

    def stored(step, adapter_ref, length_ref, slot_ref, here_ref):
        at = slot_of(block_of(step), adapter_ref, slot_ref, here_ref)
        return jnp.clip(at, 0, slots - 1), 0, 0

    return pl.pallas_call(
        kernel,
        grid_spec=pltpu.PrefetchScalarGridSpec(
            num_scalar_prefetch=4,
            grid=(groups,),
            in_specs=[pl.BlockSpec((1, rank, width), stored)],
            out_specs=[
                pl.BlockSpec((rank, width), lambda step, *refs: (jnp.minimum(step, 1), 0)),
                pl.BlockSpec((rank, width), lambda step, *refs: (jnp.maximum(step - 2, 0), 0)),
                pl.BlockSpec(memory_space=pltpu.SMEM),
            ],
        ),
        out_shape=[jax.ShapeDtypeStruct((2 * rank, width), store.dtype)] * 2
        + [jax.ShapeDtypeStruct((2 * groups + 1,), jnp.int32)],
        compiler_params=pltpu.CompilerParams(vmem_limit_bytes=VMEM),
        cost_estimate=cost(0, 8 * rank * width * groups),
        name="choose",
    )(block_adapter, block_length, adapter_slot, here, store)


def local_square(
    tokens, weight, adapter_down, adapter_up, cotangent, block_adapter, block_length, adapter_slot
):
    groups = shards = 4
    rows, width = tokens.shape
    depth, hidden = weight.shape
    per_owner, _, rank = adapter_down.shape
    span = per_owner * rank
    b16 = jnp.bfloat16
    i, j = lax.axis_index("dp"), lax.axis_index("tp")

    def swap(x, bit):
        return lax.ppermute(x, "dp", [(d, d ^ bit) for d in range(groups)])

    def along(x, bit):
        return lax.ppermute(x, "tp", [(z, z ^ bit) for z in range(shards)])

    forth = [(c * groups + r, (r ^ c) * groups + c) for r in range(groups) for c in range(shards)]
    back_again = [(b, a) for a, b in forth]

    def turn(x, pairs):
        return lax.ppermute(x, ("tp", "dp"), pairs)

    turned = turn(tokens, forth)
    cot_c = swap(cotangent, CORE)
    here = jnp.stack([i, j]).astype(jnp.int32)
    down_t = jnp.swapaxes(adapter_down, 1, 2)
    near, rest, facts = choose(block_adapter, block_length, adapter_slot, here, down_t)
    up_flat = adapter_up.reshape(span, hidden)
    half = depth // 2

    near = swap(near, CORE)
    down_x = swap(rest[:rank] + near[rank:], CHIP)
    cot_x = swap(after(cotangent, near), CHIP)
    down_own = rest[rank:] + near[:rank] + down_x
    inner = dot(down_own, after(tokens, turned), (1, 1))

    grad01, parts = return_grad(after(cotangent, inner), cot_c, weight, 0, 0, half)
    inner = inner + after(along(inner, 1), grad01)
    tok_2 = along(after(turned, inner), 2)
    more01, parts = return_grad(after(cotangent, inner, turned), cot_c, weight, 0, half, depth, (parts,))
    inner = inner + after(along(inner, 2), more01)
    inner = jnp.where(lax.broadcasted_iota(jnp.int32, (rank, rows), 1) < facts[groups], inner, 0.0).astype(b16)
    back01 = rank_back(facts, after(adapter_up, inner), [cotangent, cot_c], (0, 1), hidden // 4)
    inner = jnp.concatenate([inner, swap(inner, CORE)], axis=1)
    tok_near = jnp.stack([turned, after(tok_2, back01)])
    tok_far = along(tok_near, 1)

    cot_xc = swap(after(cot_x, tok_near), CORE)
    tok_x = swap(after(tokens, cot_x), CHIP)
    inner = jnp.concatenate([inner, swap(after(inner, cot_x), CHIP)], axis=1)
    back23 = rank_back(facts, adapter_up, [cot_x, cot_xc], (2, 3), hidden // 4)
    back = jnp.concatenate([back01, back23], axis=1)
    grad23, parts = return_grad(after(cot_x, back), cot_xc, weight, 1, 0, half, (parts,))
    back = after(back, grad23) + along(back, 1)
    more23, parts = return_grad(after(cot_x, back), cot_xc, weight, 1, half, depth, (parts,))
    back_wide, _, back_b = spread(facts, after(back, more23), along(back, 2), per_owner, 1.0)
    parts = after(parts, back_b).reshape(shards, rows, depth)
    parts = [lax.all_to_all(x, "tp", 0, 0, tiled=True) for x in (parts[:, :, :half], parts[:, :, half:])]
    mixed = swap(jnp.concatenate([tokens, after(tok_x, back_b)], axis=0), CORE)
    toks = [tokens, mixed[:rows], tok_x, mixed[rows:]]
    down_mine = turn(after(down_own, cot_x), forth)
    inner_wide, inner_rows, _ = spread(facts, after(inner, back_b), None, per_owner, adapter_scale)

    def grad_block(q):
        halves = [
            [lax.dynamic_slice_in_dim(x, (q & 1) * rows, rows, 0) for x in both]
            for both in ((grad01, grad23), (more01, more23))
        ]
        return jnp.concatenate([jnp.where(q < 2, low, high) for low, high in halves], axis=1)

    def share(x, got, bit):
        return x + jnp.concatenate([got[:, (q ^ bit) * rows : ((q ^ bit) + 1) * rows] for q in range(groups)], axis=1)

    block = 512
    steps = hidden // block
    pieces = 4
    edges = [(-(-steps * n // pieces)) * block for n in range(pieces + 1)]
    kept, sent, got_c, got_x, done = [], [], [], [], []

    def make(n, *points):
        keep, send = project(facts, after(tok_near, *points), tok_far, inner_rows, weight, up_flat, edges[n], edges[n + 1], block)
        kept.append(keep)
        got_c.append(swap(send, CORE))
        return keep

    def cross(n, *points):
        summed = (after(kept[n], *points)[1] + got_c[n][1]).astype(b16)
        got_x.append(swap(summed, CHIP))
        return summed

    def finish(n, *points):
        done.append((after(kept[n], *points)[0] + got_c[n][0] + got_x[n].astype(jnp.float32)).astype(b16))
        return done[-1]

    point = make(0, tok_x, down_mine)
    back_b = share(after(back_b, point), swap(back_b, CORE), CORE)
    point = make(1, back_b)
    back_b = share(after(back_b, point), swap(back_b, CHIP), CHIP)
    point = cross(0, back_b)
    point = make(2, point, mixed, parts[0])
    point = cross(1, point)
    point = finish(0, point)
    point = make(3, point)
    point = cross(2, point)
    point = finish(1, point)
    down_wide = slot_grad(after(back_wide, point), toks, 1024)
    point = cross(3, down_wide)
    back_mine = lax.dynamic_slice_in_dim(back_b, j * rows, rows, 1)
    total = after(grad_block(j), point, parts[1])
    for m in range(1, shards):
        total = total + jnp.concatenate(
            [lax.dynamic_index_in_dim(x, j ^ m, 0, False).astype(jnp.float32) for x in parts], axis=1
        )
    total = (total + dot(back_mine, down_mine, (0, 0))).astype(b16)
    tokens_grad = turn(total, back_again)
    up_wide = slot_grad(after(inner_wide, total), [cotangent, cot_c, cot_x, cot_xc], 1024)
    point = finish(2, up_wide)
    finish(3, point)
    projected = jnp.concatenate(done, axis=1)
    up_grad = up_wide.reshape(per_owner, rank, hidden)
    down_grad = jnp.swapaxes(down_wide.reshape(per_owner, rank, width), 1, 2)
    return projected, tokens_grad, down_grad, up_grad


def local_any(
    groups, tokens, weight, adapter_down, adapter_up, cotangent, block_adapter, block_length, adapter_slot
):
    bits = [1 << n for n in range((groups - 1).bit_length())]

    def swap(x, bit):
        return lax.ppermute(x, "dp", [(d, d ^ bit) for d in range(groups)])

    def gather(x):
        blocks = {0: x}
        for bit in reversed(bits):
            blocks.update({q | bit: swap(block, bit) for q, block in blocks.items()})
        return jnp.stack([blocks[q] for q in range(groups)])

    def combine(parts):
        for bit in bits:
            parts = [a + swap(b, bit) for a, b in zip(parts[::2], parts[1::2])]
        return parts[0]

    rows, width = tokens.shape
    depth, hidden = weight.shape
    per_owner, _, rank = adapter_down.shape
    i = lax.axis_index("dp")
    order = jnp.arange(groups, dtype=jnp.int32) ^ i
    owned, local_ids, live = block_facts(
        block_adapter, block_length, adapter_slot, order, rows, per_owner, i
    )
    down_sel = chosen(adapter_down, owned, local_ids)
    up_sel = chosen(adapter_up, owned, local_ids)
    all_tokens = lax.all_gather(lax.all_gather(tokens, "dp", axis=0), "tp", axis=2, tiled=True)
    all_tokens = lax.dynamic_slice_in_dim(all_tokens, i * depth, depth, 2)[order]
    all_tokens = all_tokens.reshape(groups * rows, depth)
    toks, cots = gather(tokens), gather(cotangent)
    tok_all, cot_all = toks.reshape(-1, width), cots.reshape(-1, hidden)
    down_mine = combine(down_sel)
    inner = jnp.stack([dot(toks[q], down_sel[q], (1, 0)) for q in range(groups)])
    inner_b = (lax.psum(inner, "tp") * live[:, :, None]).astype(jnp.bfloat16)
    back = jnp.stack([dot(cots[q], up_sel[q], (1, 1)) for q in range(groups)])
    back = lax.psum(back[order], ("tp", "dp"))[order] * (adapter_scale * live)[:, :, None]
    back_b = back.astype(jnp.bfloat16)
    one_hot = (local_ids[:, None] == jnp.arange(per_owner, dtype=jnp.int32)[None, :]) & owned[:, None]

    def spread(x):
        wide = jnp.where(one_hot[:, None, :, None], x[:, :, None, :], jnp.zeros((), x.dtype))
        return wide.reshape(groups * rows, per_owner * rank)

    inner_wide = spread(inner_b) * jnp.bfloat16(adapter_scale)
    total = dot(cot_all, weight, (1, 1)).reshape(groups, rows, 1, depth)[order]
    placed = jnp.zeros((groups, rows, groups, depth), jnp.float32)
    placed = lax.dynamic_update_slice_in_dim(placed, total, i, 2)
    placed = lax.psum_scatter(placed, "dp", scatter_dimension=0, tiled=False)
    placed = placed.reshape(rows, groups * depth)
    placed = lax.psum_scatter(placed, "tp", scatter_dimension=1, tiled=True)
    tokens_grad = (placed + dot(back_b[0], down_mine, (1, 1))).astype(jnp.bfloat16)
    part = dot(all_tokens, weight, (1, 0)) + dot(inner_wide, adapter_up.reshape(-1, hidden), (1, 0))
    projected = combine(list(part.reshape(groups, rows, hidden))).astype(jnp.bfloat16)
    up_grad = dot(inner_wide, cot_all, (0, 0)).reshape(per_owner, rank, hidden)
    down_grad = dot(spread(back_b), tok_all, (0, 0)).reshape(per_owner, rank, width)
    return projected, tokens_grad, jnp.swapaxes(down_grad, 1, 2), up_grad


def solution(mesh):
    placed = (
        P(("grp", "dp"), "tp"),
        P("dp", "tp"),
        P("dp", "tp", None),
        P("dp", None, "tp"),
        P(("grp", "dp"), "tp"),
        P("grp"),
        P("grp"),
        P(),
    )
    groups, shards = mesh.shape["dp"], mesh.shape["tp"]
    square = groups == shards == 4
    return jax.shard_map(
        local_square if square else functools.partial(local_any, groups),
        mesh=mesh,
        in_specs=placed,
        out_specs=(
            P(("grp", "dp"), "tp"),
            P(("grp", "dp"), "tp"),
            P(("grp", "dp"), "tp", None),
            P(("grp", "dp"), None, "tp"),
        ),
        check_vma=False,
    )
```

```python
import functools

import jax
import jax.numpy as jnp
from jax import lax
from jax.experimental import pallas as pl
from jax.experimental.pallas import tpu as pltpu
from jax.sharding import PartitionSpec as P

SEGMENT_BLOCK = 128

adapter_scale = 2.0
CORE, CHIP = 1, 2
VMEM = 48 * 1024 * 1024


def dot(a, b, contract):
    return lax.dot_general(a, b, ((contract[:1], contract[1:]), ((), ())), preferred_element_type=jnp.float32)


def after(x, *others):
    return lax.optimization_barrier((x,) + others)[0]


def cost(flops, moved, share=16):
    return pl.CostEstimate(flops=flops // share, bytes_accessed=moved // share, transcendentals=0)


def project(facts, near, far, wide, weight, up_flat, start, stop, block):
    _, rows, depth = near.shape
    groups = 4
    span = wide.shape[1]
    base = start // block

    def kernel(facts_ref, near_ref, far_ref, wide_ref, w_ref, up_ref, keep_ref, send_ref, lhs):
        @pl.when(pl.program_id(0) == 0)
        def _():
            for m in range(groups):
                at = pl.multiple_of((facts_ref[2 * groups] ^ m) * rows, rows)
                lhs[pl.ds(at, rows)] = (far_ref if m & 1 else near_ref)[m >> 1]

        total = dot(lhs[...], w_ref[...], (1, 0)) + dot(wide_ref[...], up_ref[...], (1, 0))
        keep_ref[0] = total[:rows]
        send_ref[0] = total[rows : 2 * rows]
        keep_ref[1] = total[2 * rows : 3 * rows]
        send_ref[1] = total[3 * rows :]

    whole = lambda n: (0, 0, 0)
    return pl.pallas_call(
        kernel,
        grid=((stop - start) // block,),
        in_specs=[
            pl.BlockSpec(memory_space=pltpu.SMEM),
            pl.BlockSpec((2, rows, depth), whole),
            pl.BlockSpec((2, rows, depth), whole),
            pl.BlockSpec((groups * rows, span), lambda n: (0, 0)),
            pl.BlockSpec((depth, block), lambda n: (0, n + base)),
            pl.BlockSpec((span, block), lambda n: (0, n + base)),
        ],
        out_specs=[pl.BlockSpec((2, rows, block), lambda n: (0, 0, n))] * 2,
        out_shape=[jax.ShapeDtypeStruct((2, rows, stop - start), jnp.float32)] * 2,
        scratch_shapes=[pltpu.VMEM((groups * rows, depth), near.dtype)],
        compiler_params=pltpu.CompilerParams(vmem_limit_bytes=VMEM),
        cost_estimate=cost(2 * groups * rows * (depth + span) * (stop - start), 2 * (depth + span + 2 * groups * rows) * (stop - start), 1),
        name="project",
    )(facts, near, far, wide, weight, up_flat)


def return_grad(first, second, weight, half, start, stop, sums=()):
    rows, hidden = first.shape
    depth = weight.shape[0]
    block = 256
    base = start // block

    def kernel(a_ref, b_ref, w_ref, *refs):
        out_ref, sums_ref, rhs = refs[-3:]

        @pl.when(pl.program_id(0) == 0)
        def _():
            rhs[:rows] = a_ref[...]
            rhs[rows:] = b_ref[...]

        total = dot(w_ref[...], rhs[...], (1, 1)).T
        out_ref[...] = total
        sums_ref[...] = total.astype(sums_ref.dtype)

    whole = lambda n: (0, 0)
    return pl.pallas_call(
        kernel,
        grid=((stop - start) // block,),
        in_specs=[
            pl.BlockSpec((rows, hidden), whole),
            pl.BlockSpec((rows, hidden), whole),
            pl.BlockSpec((block, hidden), lambda n: (n + base, 0)),
        ]
        + [pl.BlockSpec(memory_space=pl.ANY)] * len(sums),
        out_specs=[
            pl.BlockSpec((2 * rows, block), lambda n: (0, n)),
            pl.BlockSpec((2 * rows, block), lambda n: (half, n + base)),
        ],
        out_shape=[
            jax.ShapeDtypeStruct((2 * rows, stop - start), jnp.float32),
            jax.ShapeDtypeStruct((4 * rows, depth), first.dtype),
        ],
        input_output_aliases={3: 1} if sums else {},
        scratch_shapes=[pltpu.VMEM((2 * rows, hidden), first.dtype)],
        compiler_params=pltpu.CompilerParams(vmem_limit_bytes=VMEM),
        cost_estimate=cost(4 * rows * hidden * (stop - start), 2 * hidden * (stop - start + 2 * rows)),
        name="return_grad",
    )(first, second, weight, *sums)


def rank_back(facts, store, blocks, places, block):
    _, rank, columns = store.shape
    rows = blocks[0].shape[0]
    count = len(blocks)
    groups = facts.shape[0] // 2

    def kernel(facts_ref, *refs):
        slots, values, out_ref, total = refs[:count], refs[count : 2 * count], refs[-2], refs[-1]
        n = pl.program_id(0)
        left = jnp.concatenate([r[0] for r in slots], axis=0)
        right = jnp.concatenate([r[...] for r in values], axis=0)
        product = dot(left, right, (1, 1))

        @pl.when(n == 0)
        def _():
            total[...] = product

        @pl.when(n > 0)
        def _():
            total[...] += product

        @pl.when(n == pl.num_programs(0) - 1)
        def _():
            for at, place in enumerate(places):
                part = total[at * rank : (at + 1) * rank, at * rows : (at + 1) * rows]
                alive = lax.broadcasted_iota(jnp.int32, (rank, rows), 1) < facts_ref[groups + place]
                alive = alive & (facts_ref[place] >= 0)
                out_ref[:, at * rows : (at + 1) * rows] = jnp.where(alive, part * adapter_scale, 0.0)

    def chosen_slot(place):
        return lambda n, facts_ref: (jnp.maximum(facts_ref[place], 0), 0, n)

    return pl.pallas_call(
        kernel,
        grid_spec=pltpu.PrefetchScalarGridSpec(
            num_scalar_prefetch=1,
            grid=(columns // block,),
            in_specs=[pl.BlockSpec((1, rank, block), chosen_slot(place)) for place in places]
            + [pl.BlockSpec((rows, block), lambda n, facts_ref: (0, n))] * count,
            out_specs=pl.BlockSpec((rank, count * rows), lambda n, facts_ref: (0, 0)),
            scratch_shapes=[pltpu.VMEM((count * rank, count * rows), jnp.float32)],
        ),
        out_shape=jax.ShapeDtypeStruct((rank, count * rows), jnp.float32),
        compiler_params=pltpu.CompilerParams(vmem_limit_bytes=VMEM),
        cost_estimate=cost(2 * count * rank * count * rows * columns, 2 * columns * count * (rank + rows)),
        name="rank_back",
    )(facts, *[store] * count, *blocks)


def spread(facts, here, there, slots, scale):
    rank, tokens = here.shape
    groups = facts.shape[0] // 2
    rows = tokens // groups
    values = [here] if there is None else [here, there]

    def kernel(facts_ref, *refs):
        wide_ref, turned_ref, sum_ref = refs[-3:]
        x = sum(r[...] for r in refs[:-3]).astype(jnp.bfloat16)
        sum_ref[...] = x
        x = x.astype(jnp.float32) * scale
        for q in range(groups):
            part = x[:, q * rows : (q + 1) * rows]
            for s in range(slots):
                value = jnp.where(facts_ref[q] == s, part, 0.0)
                wide_ref[s * rank : (s + 1) * rank, q * rows : (q + 1) * rows] = value.astype(jnp.bfloat16)
        turned_ref[...] = wide_ref[...].astype(jnp.float32).T.astype(jnp.bfloat16)

    return pl.pallas_call(
        kernel,
        in_specs=[pl.BlockSpec(memory_space=pltpu.SMEM)] + [pl.BlockSpec(memory_space=pltpu.VMEM)] * len(values),
        out_specs=[pl.BlockSpec(memory_space=pltpu.VMEM)] * 3,
        out_shape=[
            jax.ShapeDtypeStruct((slots * rank, tokens), jnp.bfloat16),
            jax.ShapeDtypeStruct((tokens, slots * rank), jnp.bfloat16),
            jax.ShapeDtypeStruct((rank, tokens), jnp.bfloat16),
        ],
        compiler_params=pltpu.CompilerParams(vmem_limit_bytes=VMEM),
        cost_estimate=cost(0, 8 * slots * rank * tokens),
        name="spread",
    )(facts, *values)


def slot_grad(wide_t, blocks, block):
    span = wide_t.shape[0]
    rows, columns = blocks[0].shape
    groups = len(blocks)

    def kernel(wide_ref, *refs):
        values = jnp.concatenate([c[...] for c in refs[:groups]], axis=0)
        refs[groups][...] = dot(wide_ref[...], values, (1, 0))

    return pl.pallas_call(
        kernel,
        grid=(columns // block,),
        in_specs=[pl.BlockSpec((span, groups * rows), lambda n: (0, 0))]
        + [pl.BlockSpec((rows, block), lambda n: (0, n))] * groups,
        out_specs=pl.BlockSpec((span, block), lambda n: (0, n)),
        out_shape=jax.ShapeDtypeStruct((span, columns), jnp.float32),
        compiler_params=pltpu.CompilerParams(vmem_limit_bytes=VMEM),
        cost_estimate=cost(2 * span * groups * rows * columns, (4 * span + 2 * groups * rows) * columns, 1),
        name="slot_grad",
    )(wide_t, *blocks)


def block_facts(block_adapter, block_length, adapter_slot, order, rows, per_owner, i):
    match = block_adapter[:, None] == jnp.arange(adapter_slot.shape[0], dtype=jnp.int32)[None, :]
    slots = jnp.sum(jnp.where(match, adapter_slot[None, :], 0), axis=1)[order]
    lengths = block_length[order]
    owned = slots // per_owner == i
    local_ids = slots % per_owner
    groups = order.shape[0]
    live = (lax.broadcasted_iota(jnp.int32, (groups, rows), 1) < lengths[:, None]).astype(jnp.float32)
    return owned, local_ids, live


def chosen(store, owned, local_ids):
    zero = jnp.zeros((), store.dtype)
    return [
        jnp.where(owned[q], lax.dynamic_index_in_dim(store, local_ids[q], 0, False), zero)
        for q in range(owned.shape[0])
    ]


def choose(block_adapter, block_length, adapter_slot, here, store):
    slots, rank, width = store.shape
    groups = block_adapter.shape[0]

    def block_of(step):
        return jnp.clip(jnp.where(step < 2, 2 * step + 1, 6 - 2 * step), 0, groups - 1)

    def slot_of(q, adapter_ref, slot_ref, here_ref):
        return slot_ref[adapter_ref[q ^ here_ref[0]]] - here_ref[0] * slots

    def kernel(adapter_ref, length_ref, slot_ref, here_ref, store_ref, near_ref, rest_ref, facts_ref):
        step = pl.program_id(0)

        @pl.when(step == 0)
        def _():
            for q in range(groups):
                at = slot_of(q, adapter_ref, slot_ref, here_ref)
                facts_ref[q] = jnp.where((at >= 0) & (at < slots), at, -1)
                facts_ref[groups + q] = length_ref[q ^ here_ref[0]]
            facts_ref[2 * groups] = here_ref[1]

        at = slot_of(block_of(step), adapter_ref, slot_ref, here_ref)
        value = store_ref[0] * ((at >= 0) & (at < slots)).astype(store_ref.dtype)

        @pl.when(step < 2)
        def _():
            near_ref[...] = value

        @pl.when(step >= 2)
        def _():
            rest_ref[...] = value

    def stored(step, adapter_ref, length_ref, slot_ref, here_ref):
        at = slot_of(block_of(step), adapter_ref, slot_ref, here_ref)
        return jnp.clip(at, 0, slots - 1), 0, 0

    return pl.pallas_call(
        kernel,
        grid_spec=pltpu.PrefetchScalarGridSpec(
            num_scalar_prefetch=4,
            grid=(groups,),
            in_specs=[pl.BlockSpec((1, rank, width), stored)],
            out_specs=[
                pl.BlockSpec((rank, width), lambda step, *refs: (jnp.minimum(step, 1), 0)),
                pl.BlockSpec((rank, width), lambda step, *refs: (jnp.maximum(step - 2, 0), 0)),
                pl.BlockSpec(memory_space=pltpu.SMEM),
            ],
        ),
        out_shape=[jax.ShapeDtypeStruct((2 * rank, width), store.dtype)] * 2
        + [jax.ShapeDtypeStruct((2 * groups + 1,), jnp.int32)],
        compiler_params=pltpu.CompilerParams(vmem_limit_bytes=VMEM),
        cost_estimate=cost(0, 8 * rank * width * groups),
        name="choose",
    )(block_adapter, block_length, adapter_slot, here, store)


def local_square(
    tokens, weight, adapter_down, adapter_up, cotangent, block_adapter, block_length, adapter_slot
):
    groups = shards = 4
    rows, width = tokens.shape
    depth, hidden = weight.shape
    per_owner, _, rank = adapter_down.shape
    span = per_owner * rank
    b16 = jnp.bfloat16
    i, j = lax.axis_index("dp"), lax.axis_index("tp")

    def swap(x, bit):
        return lax.ppermute(x, "dp", [(d, d ^ bit) for d in range(groups)])

    def along(x, bit):
        return lax.ppermute(x, "tp", [(z, z ^ bit) for z in range(shards)])

    forth = [(c * groups + r, (r ^ c) * groups + c) for r in range(groups) for c in range(shards)]
    back_again = [(b, a) for a, b in forth]

    def turn(x, pairs):
        return lax.ppermute(x, ("tp", "dp"), pairs)

    turned = turn(tokens, forth)
    cot_c = swap(cotangent, CORE)
    here = jnp.stack([i, j]).astype(jnp.int32)
    down_t = jnp.swapaxes(adapter_down, 1, 2)
    near, rest, facts = choose(block_adapter, block_length, adapter_slot, here, down_t)
    up_flat = adapter_up.reshape(span, hidden)
    half = depth // 2

    near = swap(near, CORE)
    down_x = swap(rest[:rank] + near[rank:], CHIP)
    cot_x = swap(after(cotangent, down_x), CHIP)
    down_own = rest[rank:] + near[:rank] + down_x
    inner = dot(down_own, after(tokens, turned), (1, 1))

    grad01, parts = return_grad(after(cotangent, inner), cot_c, weight, 0, 0, half)
    inner = inner + after(along(inner, 1), grad01)
    tok_2 = along(after(turned, inner), 2)
    more01, parts = return_grad(after(cotangent, inner, turned), cot_c, weight, 0, half, depth, (parts,))
    inner = inner + after(along(inner, 2), more01)
    inner = jnp.where(lax.broadcasted_iota(jnp.int32, (rank, rows), 1) < facts[groups], inner, 0.0).astype(b16)
    back01 = rank_back(facts, after(adapter_up, inner), [cotangent, cot_c], (0, 1), hidden // 4)
    inner = jnp.concatenate([inner, swap(inner, CORE)], axis=1)
    tok_near = jnp.stack([turned, after(tok_2, back01)])
    tok_far = along(tok_near, 1)

    cot_xc = swap(after(cot_x, tok_near), CORE)
    tok_x = swap(after(tokens, cot_x), CHIP)
    inner = jnp.concatenate([inner, swap(after(inner, cot_x), CHIP)], axis=1)
    back23 = rank_back(facts, adapter_up, [cot_x, cot_xc], (2, 3), hidden // 4)
    back = jnp.concatenate([back01, back23], axis=1)
    grad23, parts = return_grad(after(cot_x, back), cot_xc, weight, 1, 0, half, (parts,))
    back = after(back, grad23) + along(back, 1)
    more23, parts = return_grad(after(cot_x, back), cot_xc, weight, 1, half, depth, (parts,))
    back_wide, _, back_b = spread(facts, after(back, more23), along(back, 2), per_owner, 1.0)
    parts = after(parts, back_b).reshape(shards, rows, depth)
    parts = [lax.all_to_all(x, "tp", 0, 0, tiled=True) for x in (parts[:, :, :half], parts[:, :, half:])]
    mixed = swap(jnp.concatenate([tokens, after(tok_x, back_b)], axis=0), CORE)
    toks = [tokens, mixed[:rows], tok_x, mixed[rows:]]
    down_mine = turn(after(down_own, cot_x), forth)
    inner_wide, inner_rows, _ = spread(facts, after(inner, back_b), None, per_owner, adapter_scale)

    def grad_block(q):
        halves = [
            [lax.dynamic_slice_in_dim(x, (q & 1) * rows, rows, 0) for x in both]
            for both in ((grad01, grad23), (more01, more23))
        ]
        return jnp.concatenate([jnp.where(q < 2, low, high) for low, high in halves], axis=1)

    def share(x, got, bit):
        return x + jnp.concatenate([got[:, (q ^ bit) * rows : ((q ^ bit) + 1) * rows] for q in range(groups)], axis=1)

    block = 512
    steps = hidden // block
    pieces = 4
    edges = [(-(-steps * n // pieces)) * block for n in range(pieces + 1)]
    kept, sent, got_c, got_x, done = [], [], [], [], []

    def make(n, *points):
        keep, send = project(facts, after(tok_near, *points), tok_far, inner_rows, weight, up_flat, edges[n], edges[n + 1], block)
        kept.append(keep)
        got_c.append(swap(send, CORE))
        return keep

    def cross(n, *points):
        summed = (after(kept[n], *points)[1] + got_c[n][1]).astype(b16)
        got_x.append(swap(summed, CHIP))
        return summed

    def finish(n, *points):
        done.append((after(kept[n], *points)[0] + got_c[n][0] + got_x[n].astype(jnp.float32)).astype(b16))
        return done[-1]

    point = make(0, tok_x, down_mine)
    back_b = share(after(back_b, point), swap(back_b, CORE), CORE)
    point = make(1, back_b)
    back_b = share(after(back_b, point), swap(back_b, CHIP), CHIP)
    point = cross(0, back_b)
    point = make(2, point, mixed, parts[0])
    point = finish(0, point)
    point = cross(1, point)
    point = make(3, point)
    point = finish(1, point)
    point = cross(2, point)
    point = cross(3, point)
    up_wide = slot_grad(after(inner_wide, point), [cotangent, cot_c, cot_x, cot_xc], 1024)
    point = finish(2, up_wide)
    back_mine = lax.dynamic_slice_in_dim(back_b, j * rows, rows, 1)
    total = after(grad_block(j), point, parts[1])
    for m in range(1, shards):
        total = total + jnp.concatenate(
            [lax.dynamic_index_in_dim(x, j ^ m, 0, False).astype(jnp.float32) for x in parts], axis=1
        )
    total = (total + dot(back_mine, down_mine, (0, 0))).astype(b16)
    tokens_grad = turn(total, back_again)
    down_wide = slot_grad(after(back_wide, total), toks, 1024)
    finish(3, down_wide)
    projected = jnp.concatenate(done, axis=1)
    up_grad = up_wide.reshape(per_owner, rank, hidden)
    down_grad = jnp.swapaxes(down_wide.reshape(per_owner, rank, width), 1, 2)
    return projected, tokens_grad, down_grad, up_grad


def local_any(
    groups, tokens, weight, adapter_down, adapter_up, cotangent, block_adapter, block_length, adapter_slot
):
    bits = [1 << n for n in range((groups - 1).bit_length())]

    def swap(x, bit):
        return lax.ppermute(x, "dp", [(d, d ^ bit) for d in range(groups)])

    def gather(x):
        blocks = {0: x}
        for bit in reversed(bits):
            blocks.update({q | bit: swap(block, bit) for q, block in blocks.items()})
        return jnp.stack([blocks[q] for q in range(groups)])

    def combine(parts):
        for bit in bits:
            parts = [a + swap(b, bit) for a, b in zip(parts[::2], parts[1::2])]
        return parts[0]

    rows, width = tokens.shape
    depth, hidden = weight.shape
    per_owner, _, rank = adapter_down.shape
    i = lax.axis_index("dp")
    order = jnp.arange(groups, dtype=jnp.int32) ^ i
    owned, local_ids, live = block_facts(
        block_adapter, block_length, adapter_slot, order, rows, per_owner, i
    )
    down_sel = chosen(adapter_down, owned, local_ids)
    up_sel = chosen(adapter_up, owned, local_ids)
    all_tokens = lax.all_gather(lax.all_gather(tokens, "dp", axis=0), "tp", axis=2, tiled=True)
    all_tokens = lax.dynamic_slice_in_dim(all_tokens, i * depth, depth, 2)[order]
    all_tokens = all_tokens.reshape(groups * rows, depth)
    toks, cots = gather(tokens), gather(cotangent)
    tok_all, cot_all = toks.reshape(-1, width), cots.reshape(-1, hidden)
    down_mine = combine(down_sel)
    inner = jnp.stack([dot(toks[q], down_sel[q], (1, 0)) for q in range(groups)])
    inner_b = (lax.psum(inner, "tp") * live[:, :, None]).astype(jnp.bfloat16)
    back = jnp.stack([dot(cots[q], up_sel[q], (1, 1)) for q in range(groups)])
    back = lax.psum(back[order], ("tp", "dp"))[order] * (adapter_scale * live)[:, :, None]
    back_b = back.astype(jnp.bfloat16)
    one_hot = (local_ids[:, None] == jnp.arange(per_owner, dtype=jnp.int32)[None, :]) & owned[:, None]

    def spread(x):
        wide = jnp.where(one_hot[:, None, :, None], x[:, :, None, :], jnp.zeros((), x.dtype))
        return wide.reshape(groups * rows, per_owner * rank)

    inner_wide = spread(inner_b) * jnp.bfloat16(adapter_scale)
    total = dot(cot_all, weight, (1, 1)).reshape(groups, rows, 1, depth)[order]
    placed = jnp.zeros((groups, rows, groups, depth), jnp.float32)
    placed = lax.dynamic_update_slice_in_dim(placed, total, i, 2)
    placed = lax.psum_scatter(placed, "dp", scatter_dimension=0, tiled=False)
    placed = placed.reshape(rows, groups * depth)
    placed = lax.psum_scatter(placed, "tp", scatter_dimension=1, tiled=True)
    tokens_grad = (placed + dot(back_b[0], down_mine, (1, 1))).astype(jnp.bfloat16)
    part = dot(all_tokens, weight, (1, 0)) + dot(inner_wide, adapter_up.reshape(-1, hidden), (1, 0))
    projected = combine(list(part.reshape(groups, rows, hidden))).astype(jnp.bfloat16)
    up_grad = dot(inner_wide, cot_all, (0, 0)).reshape(per_owner, rank, hidden)
    down_grad = dot(spread(back_b), tok_all, (0, 0)).reshape(per_owner, rank, width)
    return projected, tokens_grad, jnp.swapaxes(down_grad, 1, 2), up_grad


def solution(mesh):
    placed = (
        P(("grp", "dp"), "tp"),
        P("dp", "tp"),
        P("dp", "tp", None),
        P("dp", None, "tp"),
        P(("grp", "dp"), "tp"),
        P("grp"),
        P("grp"),
        P(),
    )
    groups, shards = mesh.shape["dp"], mesh.shape["tp"]
    square = groups == shards == 4
    return jax.shard_map(
        local_square if square else functools.partial(local_any, groups),
        mesh=mesh,
        in_specs=placed,
        out_specs=(
            P(("grp", "dp"), "tp"),
            P(("grp", "dp"), "tp"),
            P(("grp", "dp"), "tp", None),
            P(("grp", "dp"), None, "tp"),
        ),
        check_vma=False,
    )
```

```python
import functools

import jax
import jax.numpy as jnp
from jax import lax
from jax.experimental import pallas as pl
from jax.experimental.pallas import tpu as pltpu
from jax.sharding import PartitionSpec as P

SEGMENT_BLOCK = 128

adapter_scale = 2.0
CORE, CHIP = 1, 2
VMEM = 36 * 1024 * 1024


def dot(a, b, contract):
    return lax.dot_general(a, b, ((contract[:1], contract[1:]), ((), ())), preferred_element_type=jnp.float32)


def after(x, *others):
    return lax.optimization_barrier((x,) + others)[0]


def cost(flops, moved, share=16):
    return pl.CostEstimate(flops=flops // share // 8, bytes_accessed=moved // share // 8, transcendentals=0)


def project(facts, pieces, wide, weight, up_flat, start, stop, block):
    rows2, depth = pieces[0][0].shape
    rows = rows2 // 2
    groups, ways = 4, len(pieces[0])
    span = wide.shape[1]
    base = start // block
    token_arrays = [x for piece in pieces for x in piece]

    def kernel(facts_ref, *refs):
        tok_refs = refs[: 2 * ways]
        wide_ref, w_ref, up_ref, keep_ref, send_ref, lhs = refs[2 * ways :]

        @pl.when(pl.program_id(0) == 0)
        def _():
            for way in range(ways):

                @pl.when(facts_ref[2 * groups] == way)
                def _():
                    for n in range(2):
                        lhs[n * rows : (n + 1) * rows] = tok_refs[n * ways + way][:rows]
                        lhs[(n + 2) * rows : (n + 3) * rows] = tok_refs[n * ways + way][rows:]

        total = dot(lhs[...], w_ref[...], (1, 0)) + dot(wide_ref[...], up_ref[...], (1, 0))
        keep_ref[0] = total[:rows]
        send_ref[0] = total[rows : 2 * rows]
        keep_ref[1] = total[2 * rows : 3 * rows]
        send_ref[1] = total[3 * rows :]

    whole = lambda n: (0, 0)
    return pl.pallas_call(
        kernel,
        grid=((stop - start) // block,),
        in_specs=[pl.BlockSpec(memory_space=pltpu.SMEM)]
        + [pl.BlockSpec((rows2, depth), whole)] * (2 * ways)
        + [
            pl.BlockSpec((groups * rows, span), whole),
            pl.BlockSpec((depth, block), lambda n: (0, n + base)),
            pl.BlockSpec((span, block), lambda n: (0, n + base)),
        ],
        out_specs=[pl.BlockSpec((2, rows, block), lambda n: (0, 0, n))] * 2,
        out_shape=[jax.ShapeDtypeStruct((2, rows, stop - start), jnp.float32)] * 2,
        scratch_shapes=[pltpu.VMEM((groups * rows, depth), token_arrays[0].dtype)],
        compiler_params=pltpu.CompilerParams(vmem_limit_bytes=VMEM),
        cost_estimate=cost(2 * groups * rows * (depth + span) * (stop - start), 2 * (depth + span + 2 * groups * rows) * (stop - start), 1),
        name="project",
    )(facts, *token_arrays, wide, weight, up_flat)


def return_grad(first, second, weight, half, rows_of, columns_of, carried=(), added=False, send=True):
    rows, hidden = first.shape
    depth = weight.shape[0]
    block = 256
    base, column = rows_of[0] // block, columns_of[0] // hidden
    steps = (rows_of[1] - rows_of[0]) // block

    def kernel(a_ref, b_ref, w_ref, *refs):
        out_ref, rhs = refs[len(carried)], refs[-1]

        @pl.when(pl.program_id(0) == 0)
        def _():
            rhs[:rows] = a_ref[...]
            rhs[rows:] = b_ref[...]

        total = dot(w_ref[...], rhs[...], (1, 1)).T
        if added:
            total += refs[0][...]
        out_ref[...] = total
        if send:
            refs[-2][...] = total.astype(first.dtype)

    whole = lambda n: (0, 0)
    tile = pl.BlockSpec((2 * rows, block), lambda n: (0, n + base))
    outs = [(tile, jax.ShapeDtypeStruct((2 * rows, depth), jnp.float32))]
    if send:
        outs.append(
            (
                pl.BlockSpec((2 * rows, block), lambda n: (half, n + base)),
                jax.ShapeDtypeStruct((4 * rows, depth), first.dtype),
            )
        )
    anywhere = pl.BlockSpec(memory_space=pl.ANY)
    taken = [tile if added and x.dtype == jnp.float32 else anywhere for x in carried]
    target = {jnp.dtype(jnp.float32): 0, jnp.dtype(first.dtype): 1}
    return pl.pallas_call(
        kernel,
        grid=(steps,),
        in_specs=[
            pl.BlockSpec((rows, hidden), whole),
            pl.BlockSpec((rows, hidden), whole),
            pl.BlockSpec((block, hidden), lambda n: (n + base, column)),
        ]
        + taken,
        out_specs=[o[0] for o in outs],
        out_shape=[o[1] for o in outs],
        input_output_aliases={3 + n: target[jnp.dtype(x.dtype)] for n, x in enumerate(carried)},
        scratch_shapes=[pltpu.VMEM((2 * rows, hidden), first.dtype)],
        compiler_params=pltpu.CompilerParams(vmem_limit_bytes=VMEM),
        cost_estimate=cost(4 * rows * hidden * block * steps, 2 * hidden * (block * steps + 2 * rows)),
        name="return_grad",
    )(first, second, weight, *carried)


def rank_inner(facts, flat, blocks, rank):
    span, width = flat.shape
    arrays, places = [x for x, _ in blocks], [n for _, n in blocks]
    groups = len(blocks)
    rows = arrays[0].shape[0] // 2
    slots = span // rank

    def kernel(facts_ref, flat_ref, *refs):
        out_ref = refs[-1]
        total = dot(flat_ref[...], jnp.concatenate([r[...] for r in refs[:-1]], axis=0), (1, 1))
        for q in range(groups):
            acc = jnp.zeros((rank, rows), jnp.float32)
            for s in range(slots):
                acc = jnp.where(facts_ref[q] == s, total[s * rank : (s + 1) * rank, q * rows : (q + 1) * rows], acc)
            alive = lax.broadcasted_iota(jnp.int32, (rank, rows), 1) < facts_ref[groups + q]
            out_ref[:, q * rows : (q + 1) * rows] = jnp.where(alive, acc, 0.0)

    return pl.pallas_call(
        kernel,
        grid=(1,),
        in_specs=[pl.BlockSpec(memory_space=pltpu.SMEM), pl.BlockSpec((span, width), lambda n: (0, 0))]
        + [pl.BlockSpec((rows, width), lambda n, place=place: (place, 0)) for place in places],
        out_specs=pl.BlockSpec((rank, groups * rows), lambda n: (0, 0)),
        out_shape=jax.ShapeDtypeStruct((rank, groups * rows), jnp.float32),
        compiler_params=pltpu.CompilerParams(vmem_limit_bytes=VMEM),
        cost_estimate=cost(2 * span * groups * rows * width, 2 * width * (span + groups * rows)),
        name="rank_inner",
    )(facts, flat, *arrays)


def rank_back(facts, store, blocks, places, block, start=0, before=None):
    rank = store.shape[1]
    rows, columns = blocks[0].shape
    count = len(blocks)
    groups = facts.shape[0] // 2
    base = start // block
    earlier = [] if before is None else [before]

    def kernel(facts_ref, *refs):
        slots, values, out_ref, total = refs[:count], refs[count : 2 * count], refs[-2], refs[-1]
        n = pl.program_id(0)
        left = jnp.concatenate([r[0] for r in slots], axis=0)
        right = jnp.concatenate([r[...] for r in values], axis=0)
        product = dot(left, right, (1, 1))

        @pl.when(n == 0)
        def _():
            total[...] = product

        @pl.when(n > 0)
        def _():
            total[...] += product

        @pl.when(n == pl.num_programs(0) - 1)
        def _():
            for at, place in enumerate(places):
                part = total[at * rank : (at + 1) * rank, at * rows : (at + 1) * rows]
                alive = lax.broadcasted_iota(jnp.int32, (rank, rows), 1) < facts_ref[groups + place]
                alive = alive & (facts_ref[place] >= 0)
                part = jnp.where(alive, part * adapter_scale, 0.0)
                if earlier:
                    part += refs[2 * count][:, at * rows : (at + 1) * rows]
                out_ref[:, at * rows : (at + 1) * rows] = part

    def chosen_slot(place):
        return lambda n, facts_ref: (jnp.maximum(facts_ref[place], 0), 0, n + base)

    small = pl.BlockSpec((rank, count * rows), lambda n, facts_ref: (0, 0))
    return pl.pallas_call(
        kernel,
        grid_spec=pltpu.PrefetchScalarGridSpec(
            num_scalar_prefetch=1,
            grid=(columns // block,),
            in_specs=[pl.BlockSpec((1, rank, block), chosen_slot(place)) for place in places]
            + [pl.BlockSpec((rows, block), lambda n, facts_ref: (0, n))] * count
            + [small] * len(earlier),
            out_specs=small,
            scratch_shapes=[pltpu.VMEM((count * rank, count * rows), jnp.float32)],
        ),
        out_shape=jax.ShapeDtypeStruct((rank, count * rows), jnp.float32),
        compiler_params=pltpu.CompilerParams(vmem_limit_bytes=VMEM),
        cost_estimate=cost(2 * count * rank * count * rows * columns, 2 * columns * count * (rank + rows)),
        name="rank_back",
    )(facts, *[store] * count, *blocks, *earlier)


def spread(facts, here, there, slots, scale):
    rank, tokens = here.shape
    groups = facts.shape[0] // 2
    rows = tokens // groups
    values = [here] if there is None else [here, there]

    def kernel(facts_ref, *refs):
        wide_ref, turned_ref, sum_ref = refs[-3:]
        x = sum(r[...] for r in refs[:-3]).astype(jnp.bfloat16)
        sum_ref[...] = x
        x = x.astype(jnp.float32) * scale
        for q in range(groups):
            part = x[:, q * rows : (q + 1) * rows]
            for s in range(slots):
                value = jnp.where(facts_ref[q] == s, part, 0.0)
                wide_ref[s * rank : (s + 1) * rank, q * rows : (q + 1) * rows] = value.astype(jnp.bfloat16)
        turned_ref[...] = wide_ref[...].astype(jnp.float32).T.astype(jnp.bfloat16)

    return pl.pallas_call(
        kernel,
        in_specs=[pl.BlockSpec(memory_space=pltpu.SMEM)] + [pl.BlockSpec(memory_space=pltpu.VMEM)] * len(values),
        out_specs=[pl.BlockSpec(memory_space=pltpu.VMEM)] * 3,
        out_shape=[
            jax.ShapeDtypeStruct((slots * rank, tokens), jnp.bfloat16),
            jax.ShapeDtypeStruct((tokens, slots * rank), jnp.bfloat16),
            jax.ShapeDtypeStruct((rank, tokens), jnp.bfloat16),
        ],
        compiler_params=pltpu.CompilerParams(vmem_limit_bytes=VMEM),
        cost_estimate=cost(0, 8 * slots * rank * tokens),
        name="spread",
    )(facts, *values)


def slot_grad(wide_t, blocks, block):
    span, tokens = wide_t.shape
    groups = len(blocks)
    rows = tokens // groups
    columns = sum(x.shape[1] for x in blocks[0][0])
    arrays, specs = [], []
    for parts, place in blocks:
        first = 0
        for x in parts:
            count = x.shape[1] // block
            specs.append(
                pl.BlockSpec((rows, block), lambda n, a=first, b=count - 1, place=place: (place, jnp.clip(n - a, 0, b)))
            )
            arrays.append(x)
            first += count

    def kernel(wide_ref, *refs):
        n = pl.program_id(0)
        values, at = [], 0
        for parts, _ in blocks:
            value, first = refs[at][...], parts[0].shape[1] // block
            for more, x in enumerate(parts[1:], 1):
                value = jnp.where(n >= first, refs[at + more][...], value)
                first += x.shape[1] // block
            values.append(value)
            at += len(parts)
        refs[-1][...] = dot(wide_ref[...], jnp.concatenate(values, axis=0), (1, 0))

    return pl.pallas_call(
        kernel,
        grid=(columns // block,),
        in_specs=[pl.BlockSpec((span, tokens), lambda n: (0, 0))] + specs,
        out_specs=pl.BlockSpec((span, block), lambda n: (0, n)),
        out_shape=jax.ShapeDtypeStruct((span, columns), jnp.float32),
        compiler_params=pltpu.CompilerParams(vmem_limit_bytes=VMEM),
        cost_estimate=cost(2 * span * tokens * columns, (4 * span + 2 * tokens) * columns, 1),
        name="slot_grad",
    )(wide_t, *arrays)


def block_facts(block_adapter, block_length, adapter_slot, order, rows, per_owner, i):
    match = block_adapter[:, None] == jnp.arange(adapter_slot.shape[0], dtype=jnp.int32)[None, :]
    slots = jnp.sum(jnp.where(match, adapter_slot[None, :], 0), axis=1)[order]
    lengths = block_length[order]
    owned = slots // per_owner == i
    local_ids = slots % per_owner
    groups = order.shape[0]
    live = (lax.broadcasted_iota(jnp.int32, (groups, rows), 1) < lengths[:, None]).astype(jnp.float32)
    return owned, local_ids, live


def chosen(store, owned, local_ids):
    zero = jnp.zeros((), store.dtype)
    return [
        jnp.where(owned[q], lax.dynamic_index_in_dim(store, local_ids[q], 0, False), zero)
        for q in range(owned.shape[0])
    ]


def choose(block_adapter, block_length, adapter_slot, here, store):
    slots, rank, width = store.shape
    groups = block_adapter.shape[0]

    def block_of(step):
        return jnp.clip(jnp.where(step < 2, 2 * step + 1, 6 - 2 * step), 0, groups - 1)

    def slot_of(q, adapter_ref, slot_ref, here_ref):
        return slot_ref[adapter_ref[q ^ here_ref[0]]] - here_ref[0] * slots

    def kernel(adapter_ref, length_ref, slot_ref, here_ref, store_ref, near_ref, rest_ref, facts_ref):
        step = pl.program_id(0)

        @pl.when(step == 0)
        def _():
            for q in range(groups):
                at = slot_of(q, adapter_ref, slot_ref, here_ref)
                facts_ref[q] = jnp.where((at >= 0) & (at < slots), at, -1)
                facts_ref[groups + q] = length_ref[q ^ here_ref[0]]
            facts_ref[2 * groups] = here_ref[1]

        at = slot_of(block_of(step), adapter_ref, slot_ref, here_ref)
        value = store_ref[0] * ((at >= 0) & (at < slots)).astype(store_ref.dtype)

        @pl.when(step < 2)
        def _():
            near_ref[...] = value

        @pl.when(step >= 2)
        def _():
            rest_ref[...] = value

    def stored(step, adapter_ref, length_ref, slot_ref, here_ref):
        at = slot_of(block_of(step), adapter_ref, slot_ref, here_ref)
        return jnp.clip(at, 0, slots - 1), 0, 0

    return pl.pallas_call(
        kernel,
        grid_spec=pltpu.PrefetchScalarGridSpec(
            num_scalar_prefetch=4,
            grid=(groups,),
            in_specs=[pl.BlockSpec((1, rank, width), stored)],
            out_specs=[
                pl.BlockSpec((rank, width), lambda step, *refs: (jnp.minimum(step, 1), 0)),
                pl.BlockSpec((rank, width), lambda step, *refs: (jnp.maximum(step - 2, 0), 0)),
                pl.BlockSpec(memory_space=pltpu.SMEM),
            ],
        ),
        out_shape=[jax.ShapeDtypeStruct((2 * rank, width), store.dtype)] * 2
        + [jax.ShapeDtypeStruct((2 * groups + 1,), jnp.int32)],
        compiler_params=pltpu.CompilerParams(vmem_limit_bytes=VMEM),
        cost_estimate=cost(0, 8 * rank * width * groups),
        name="choose",
    )(block_adapter, block_length, adapter_slot, here, store)


def local_square(
    tokens, weight, adapter_down, adapter_up, cotangent, block_adapter, block_length, adapter_slot
):
    groups = shards = 4
    rows, width = tokens.shape
    depth, hidden = weight.shape
    per_owner, _, rank = adapter_down.shape
    span = per_owner * rank
    b16 = jnp.bfloat16
    i, j = lax.axis_index("dp"), lax.axis_index("tp")

    def swap(x, bit):
        return lax.ppermute(x, "dp", [(d, d ^ bit) for d in range(groups)])

    def along(x, bit):
        return lax.ppermute(x, "tp", [(z, z ^ bit) for z in range(shards)])

    place = [(c * groups + r, (r ^ c) * groups + c) for r in range(groups) for c in range(shards)]
    hop = [(d * groups + d, (d ^ 2) * groups + d) for d in range(groups)]
    hops = [(z * groups + d, (z ^ 1) * groups + d) for d in range(groups) for z in (d, d ^ 2)]

    def share(x, got, bit):
        return x + jnp.concatenate([got[:, (q ^ bit) * rows : ((q ^ bit) + 1) * rows] for q in range(groups)], axis=1)

    def both(x, pairs):
        return lax.ppermute(x, ("tp", "dp"), pairs)

    tok_x = swap(tokens, CHIP)
    cot_c = swap(cotangent, CORE)
    middle = hidden // 2
    cot_a = swap(after(cotangent[:, :middle], tok_x), CHIP)
    cot_b = swap(after(cotangent[:, middle:], tok_x), CHIP)
    far = i ^ j
    here = jnp.stack([i, jnp.minimum(jnp.where(far == 2, 1, 2 * (far & 1)), 2)]).astype(jnp.int32)
    down_t = jnp.swapaxes(adapter_down, 1, 2)
    near, rest, facts = choose(block_adapter, block_length, adapter_slot, here, down_t)
    up_flat = adapter_up.reshape(span, hidden)
    half = depth // 2

    even = jnp.concatenate([tokens, after(tok_x, facts)], axis=0)
    odd = swap(even, CORE)
    even_far = both(even, hop)
    grad01, parts = return_grad(after(cotangent, even), cot_c, weight, 0, (0, depth), (0, hidden))
    odd = after(odd, grad01)
    odd_far = both(odd, hop)
    toks = [(even, 0), (odd, 0), (even, 1), (odd, 1)]
    inner = rank_inner(facts, down_t.reshape(span, width), toks, rank)
    cot_ac = swap(after(cot_a, inner), CORE)
    back01 = rank_back(facts, after(adapter_up, inner, cot_a), [cotangent, cot_c], (0, 1), hidden // 4)
    inner = after(inner, back01) + along(inner, 1)
    inner_far = along(inner, 2)
    even_mid = jnp.where(i == j, even, after(even_far, inner))
    even_all = both(even_mid, hops)
    near = swap(after(near, cot_a), CORE)
    grad23, = return_grad(
        after(cot_a, even_mid), cot_ac, weight, 1, (0, depth), (0, middle), send=False
    )
    back23 = rank_back(facts, after(adapter_up, grad23), [cot_a, cot_ac], (2, 3), hidden // 4)
    cot_bc = swap(after(cot_b, back23), CORE)
    odd_mid = jnp.where(i == j, odd, after(odd_far, back23, cot_b))
    odd_all = both(odd_mid, hops)
    down_x = rest[:rank] + near[rank:]
    grad23, parts = return_grad(
        after(cot_b, odd_mid, even_all, down_x), cot_bc, weight, 1, (0, depth), (middle, hidden), (grad23, parts), added=True
    )
    back23 = rank_back(facts, after(adapter_up, grad23), [cot_b, cot_bc], (2, 3), hidden // 4, middle, back23)
    back = jnp.concatenate([back01, back23], axis=1)
    back = back + along(back, 1)
    down_x = swap(after(down_x, cot_b), CHIP)
    back_wide, _, back_b = spread(facts, after(back, down_x), along(back, 2), per_owner, 1.0)
    inner_wide, inner_rows, _ = spread(facts, after(inner, back_b), inner_far, per_owner, adapter_scale)
    back_b = share(after(back_b, inner_wide), swap(back_b, CORE), CORE)
    parts = lax.all_to_all(after(parts, back_b).reshape(shards, rows, depth), "tp", 0, 0, tiled=True)
    down_mine = both(rest[rank:] + near[:rank] + after(down_x, back_b), place)

    def grad_block(q):
        low, high = [lax.dynamic_slice_in_dim(x, (q & 1) * rows, rows, 0) for x in (grad01, grad23)]
        return jnp.where(q < 2, low, high)

    block = 512
    steps = hidden // block
    pieces = 4
    edges = [(-(-steps * n // pieces)) * block for n in range(pieces + 1)]
    kept, sent, got_c, got_x, done = [], [], [], [], []

    def make(n, *points):
        keep, send = project(facts, [(even, even_far, even_all), (odd, odd_far, after(odd_all, *points))], inner_rows, weight, up_flat, edges[n], edges[n + 1], block)
        kept.append(keep)
        got_c.append(swap(send, CORE))
        return keep

    def cross(n, *points):
        summed = (after(kept[n], *points)[1] + got_c[n][1]).astype(b16)
        got_x.append(swap(summed, CHIP))
        return summed

    def finish(n, *points):
        done.append((after(kept[n], *points)[0] + got_c[n][0] + got_x[n].astype(jnp.float32)).astype(b16))
        return done[-1]

    point = make(0, back_b)
    back_b = share(after(back_b, point), swap(back_b, CHIP), CHIP)
    point = make(1, point)
    point = cross(0, point)
    point = make(2, point, down_mine, back_b)
    point = finish(0, point)
    point = cross(1, point)
    point = make(3, point)
    point = finish(1, point)
    point = cross(2, point)
    point = cross(3, point)
    cots = [([cotangent], 0), ([cot_c], 0), ([cot_a, cot_b], 0), ([cot_ac, cot_bc], 0)]
    up_wide = slot_grad(after(inner_wide, point), cots, hidden // 4)
    point = finish(2, up_wide)
    back_mine = lax.dynamic_slice_in_dim(back_b, j * rows, rows, 1)
    total = grad_block(j)
    for m in range(1, shards):
        total = total + lax.dynamic_index_in_dim(after(parts, point), j ^ m, 0, False).astype(jnp.float32)
    total = (total + dot(back_mine, down_mine, (0, 0))).astype(b16)
    tokens_grad = both(total, [(b, a) for a, b in place])
    down_wide = slot_grad(after(back_wide, total), [([x], n) for x, n in toks], width // 2)
    finish(3, down_wide)
    projected = jnp.concatenate(done, axis=1)
    up_grad = up_wide.reshape(per_owner, rank, hidden)
    down_grad = jnp.swapaxes(down_wide.reshape(per_owner, rank, width), 1, 2)
    return projected, tokens_grad, down_grad, up_grad


def local_any(
    groups, tokens, weight, adapter_down, adapter_up, cotangent, block_adapter, block_length, adapter_slot
):
    bits = [1 << n for n in range((groups - 1).bit_length())]

    def swap(x, bit):
        return lax.ppermute(x, "dp", [(d, d ^ bit) for d in range(groups)])

    def gather(x):
        blocks = {0: x}
        for bit in reversed(bits):
            blocks.update({q | bit: swap(block, bit) for q, block in blocks.items()})
        return jnp.stack([blocks[q] for q in range(groups)])

    def combine(parts):
        for bit in bits:
            parts = [a + swap(b, bit) for a, b in zip(parts[::2], parts[1::2])]
        return parts[0]

    rows, width = tokens.shape
    depth, hidden = weight.shape
    per_owner, _, rank = adapter_down.shape
    i = lax.axis_index("dp")
    order = jnp.arange(groups, dtype=jnp.int32) ^ i
    owned, local_ids, live = block_facts(
        block_adapter, block_length, adapter_slot, order, rows, per_owner, i
    )
    down_sel = chosen(adapter_down, owned, local_ids)
    up_sel = chosen(adapter_up, owned, local_ids)
    all_tokens = lax.all_gather(lax.all_gather(tokens, "dp", axis=0), "tp", axis=2, tiled=True)
    all_tokens = lax.dynamic_slice_in_dim(all_tokens, i * depth, depth, 2)[order]
    all_tokens = all_tokens.reshape(groups * rows, depth)
    toks, cots = gather(tokens), gather(cotangent)
    tok_all, cot_all = toks.reshape(-1, width), cots.reshape(-1, hidden)
    down_mine = combine(down_sel)
    inner = jnp.stack([dot(toks[q], down_sel[q], (1, 0)) for q in range(groups)])
    inner_b = (lax.psum(inner, "tp") * live[:, :, None]).astype(jnp.bfloat16)
    back = jnp.stack([dot(cots[q], up_sel[q], (1, 1)) for q in range(groups)])
    back = lax.psum(back[order], ("tp", "dp"))[order] * (adapter_scale * live)[:, :, None]
    back_b = back.astype(jnp.bfloat16)
    one_hot = (local_ids[:, None] == jnp.arange(per_owner, dtype=jnp.int32)[None, :]) & owned[:, None]

    def spread(x):
        wide = jnp.where(one_hot[:, None, :, None], x[:, :, None, :], jnp.zeros((), x.dtype))
        return wide.reshape(groups * rows, per_owner * rank)

    inner_wide = spread(inner_b) * jnp.bfloat16(adapter_scale)
    total = dot(cot_all, weight, (1, 1)).reshape(groups, rows, 1, depth)[order]
    placed = jnp.zeros((groups, rows, groups, depth), jnp.float32)
    placed = lax.dynamic_update_slice_in_dim(placed, total, i, 2)
    placed = lax.psum_scatter(placed, "dp", scatter_dimension=0, tiled=False)
    placed = placed.reshape(rows, groups * depth)
    placed = lax.psum_scatter(placed, "tp", scatter_dimension=1, tiled=True)
    tokens_grad = (placed + dot(back_b[0], down_mine, (1, 1))).astype(jnp.bfloat16)
    part = dot(all_tokens, weight, (1, 0)) + dot(inner_wide, adapter_up.reshape(-1, hidden), (1, 0))
    projected = combine(list(part.reshape(groups, rows, hidden))).astype(jnp.bfloat16)
    up_grad = dot(inner_wide, cot_all, (0, 0)).reshape(per_owner, rank, hidden)
    down_grad = dot(spread(back_b), tok_all, (0, 0)).reshape(per_owner, rank, width)
    return projected, tokens_grad, jnp.swapaxes(down_grad, 1, 2), up_grad


def solution(mesh):
    placed = (
        P(("grp", "dp"), "tp"),
        P("dp", "tp"),
        P("dp", "tp", None),
        P("dp", None, "tp"),
        P(("grp", "dp"), "tp"),
        P("grp"),
        P("grp"),
        P(),
    )
    groups, shards = mesh.shape["dp"], mesh.shape["tp"]
    square = groups == shards == 4
    return jax.shard_map(
        local_square if square else functools.partial(local_any, groups),
        mesh=mesh,
        in_specs=placed,
        out_specs=(
            P(("grp", "dp"), "tp"),
            P(("grp", "dp"), "tp"),
            P(("grp", "dp"), "tp", None),
            P(("grp", "dp"), None, "tp"),
        ),
        check_vma=False,
    )
```

```python
import functools

import jax
import jax.numpy as jnp
from jax import lax
from jax.experimental import pallas as pl
from jax.experimental.pallas import tpu as pltpu
from jax.sharding import PartitionSpec as P

SEGMENT_BLOCK = 128

adapter_scale = 2.0
CORE, CHIP = 1, 2
VMEM = 36 * 1024 * 1024


def dot(a, b, contract):
    return lax.dot_general(a, b, ((contract[:1], contract[1:]), ((), ())), preferred_element_type=jnp.float32)


def after(x, *others):
    return lax.optimization_barrier((x,) + others)[0]


def cost(flops, moved, share=64):
    return pl.CostEstimate(flops=flops // share, bytes_accessed=moved // share, transcendentals=0)


def project(tokens, wide, weight, up_flat, start, stop, block):
    rows, depth = tokens.shape
    span = wide.shape[1]
    base = start // block

    def kernel(tok_ref, wide_ref, w_ref, up_ref, keep_ref, send_ref):
        total = dot(tok_ref[...], w_ref[...], (1, 0)) + dot(wide_ref[...], up_ref[...], (1, 0))
        keep_ref[...] = total[: rows // 2]
        send_ref[...] = total[rows // 2 :]

    whole = lambda n: (0, 0)
    return pl.pallas_call(
        kernel,
        grid=((stop - start) // block,),
        in_specs=[
            pl.BlockSpec((rows, depth), whole),
            pl.BlockSpec((rows, span), whole),
            pl.BlockSpec((depth, block), lambda n: (0, n + base)),
            pl.BlockSpec((span, block), lambda n: (0, n + base)),
        ],
        out_specs=[pl.BlockSpec((rows // 2, block), lambda n: (0, n))] * 2,
        out_shape=[jax.ShapeDtypeStruct((rows // 2, stop - start), jnp.float32)] * 2,
        compiler_params=pltpu.CompilerParams(vmem_limit_bytes=VMEM),
        cost_estimate=cost(2 * rows * (depth + span) * (stop - start), 2 * (depth + span + 2 * rows) * (stop - start)),
        name="project",
    )(tokens, wide, weight, up_flat)


def return_grad(facts, first, second, weight, store, places, features, units, block, before=(), grads=None, finish=True):
    rows, hidden = first.shape
    depth, rank = weight.shape[0], store.shape[1]
    groups = facts.shape[0] // 2
    count, part = features[1] - features[0], features[0] // (features[1] - features[0])
    base, half = units[0] // block, places[0] // 2
    grads = tuple(grads or ())

    def kernel(facts_ref, a_ref, b_ref, w_ref, up_a_ref, up_b_ref, *refs):
        before_refs = refs[: len(before)]
        outs, (total, ranks) = refs[len(before) + len(grads) : -2], refs[-2:]
        n = pl.program_id(0)
        rhs = jnp.concatenate([a_ref[...], b_ref[...]], axis=0)
        product = dot(w_ref[...], rhs, (1, 1))
        ranked = dot(jnp.concatenate([up_a_ref[0], up_b_ref[0]], axis=0), rhs, (1, 1))

        @pl.when(n == 0)
        def _():
            total[...] = product + before_refs[0][...] if before else product
            ranks[...] = ranked

        @pl.when(n > 0)
        def _():
            total[...] += product
            ranks[...] += ranked

        @pl.when(n == pl.num_programs(0) - 1)
        def _():
            for at, place in enumerate(places):
                value = ranks[at * rank : (at + 1) * rank, at * rows : (at + 1) * rows]
                alive = lax.broadcasted_iota(jnp.int32, (rank, rows), 1) < facts_ref[groups + place]
                alive = alive & (facts_ref[place] >= 0)
                value = jnp.where(alive, value * adapter_scale, 0.0)
                if before:
                    value += before_refs[1][:, at * rows : (at + 1) * rows]
                outs[0][:, at * rows : (at + 1) * rows] = value
            if finish:
                for m in range(0, count, 256):
                    turned = total[m : m + 256].T
                    outs[1][:, m : m + 256] = turned
                    outs[2][:, m : m + 256] = turned.astype(first.dtype)
            else:
                outs[1][...] = total[...]

    def chosen_slot(place):
        return lambda n, facts_ref: (jnp.maximum(facts_ref[place], 0), 0, n + base)

    whole = lambda n, facts_ref: (0, 0)
    outs = [(pl.BlockSpec((rank, 2 * rows), whole), jax.ShapeDtypeStruct((rank, 2 * rows), jnp.float32))]
    if finish:
        outs += [
            (
                pl.BlockSpec((2 * rows, count), lambda n, facts_ref: (0, part)),
                jax.ShapeDtypeStruct((2 * rows, depth), jnp.float32),
            ),
            (
                pl.BlockSpec((2 * rows, count), lambda n, facts_ref: (half, part)),
                jax.ShapeDtypeStruct((4 * rows, depth), first.dtype),
            ),
        ]
    else:
        outs += [(pl.BlockSpec((count, 2 * rows), whole), jax.ShapeDtypeStruct((count, 2 * rows), jnp.float32))]
    at = 6 + len(before)
    return pl.pallas_call(
        kernel,
        grid_spec=pltpu.PrefetchScalarGridSpec(
            num_scalar_prefetch=1,
            grid=(hidden // block,),
            in_specs=[
                pl.BlockSpec((rows, block), lambda n, facts_ref: (0, n)),
                pl.BlockSpec((rows, block), lambda n, facts_ref: (0, n)),
                pl.BlockSpec((count, block), lambda n, facts_ref: (part, n + base)),
                *[pl.BlockSpec((1, rank, block), chosen_slot(place)) for place in places],
                *[pl.BlockSpec(x.shape, whole) for x in before],
                *[pl.BlockSpec(memory_space=pl.ANY)] * len(grads),
            ],
            out_specs=[o[0] for o in outs],
            scratch_shapes=[
                pltpu.VMEM((count, 2 * rows), jnp.float32),
                pltpu.VMEM((2 * rank, 2 * rows), jnp.float32),
            ],
        ),
        out_shape=[o[1] for o in outs],
        input_output_aliases={at + n: (1 if x.dtype == jnp.float32 else 2) for n, x in enumerate(grads)},
        compiler_params=pltpu.CompilerParams(vmem_limit_bytes=VMEM),
        cost_estimate=cost(4 * rows * hidden * count, 2 * hidden * (count + 2 * rows)),
        name="return_grad",
    )(facts, first, second, weight, store, store, *before, *grads)


def rank_inner(facts, flat, blocks, rank):
    span, width = flat.shape
    arrays, places = [x for x, _ in blocks], [n for _, n in blocks]
    groups = len(blocks)
    rows = arrays[0].shape[0] // 2
    slots = span // rank

    def kernel(facts_ref, flat_ref, *refs):
        out_ref = refs[-1]
        total = dot(flat_ref[...], jnp.concatenate([r[...] for r in refs[:-1]], axis=0), (1, 1))
        for q in range(groups):
            acc = jnp.zeros((rank, rows), jnp.float32)
            for s in range(slots):
                acc = jnp.where(facts_ref[q] == s, total[s * rank : (s + 1) * rank, q * rows : (q + 1) * rows], acc)
            alive = lax.broadcasted_iota(jnp.int32, (rank, rows), 1) < facts_ref[groups + q]
            out_ref[:, q * rows : (q + 1) * rows] = jnp.where(alive, acc, 0.0)

    return pl.pallas_call(
        kernel,
        grid=(1,),
        in_specs=[pl.BlockSpec(memory_space=pltpu.SMEM), pl.BlockSpec((span, width), lambda n: (0, 0))]
        + [pl.BlockSpec((rows, width), lambda n, place=place: (place, 0)) for place in places],
        out_specs=pl.BlockSpec((rank, groups * rows), lambda n: (0, 0)),
        out_shape=jax.ShapeDtypeStruct((rank, groups * rows), jnp.float32),
        compiler_params=pltpu.CompilerParams(vmem_limit_bytes=VMEM),
        cost_estimate=cost(2 * span * groups * rows * width, 2 * width * (span + groups * rows)),
        name="rank_inner",
    )(facts, flat, *arrays)


def spread(facts, here, there, slots, scale):
    rank, tokens = here.shape
    groups = facts.shape[0] // 2
    rows = tokens // groups
    values = [here] if there is None else [here, there]

    def kernel(facts_ref, *refs):
        wide_ref, turned_ref, sum_ref = refs[-3:]
        x = sum(r[...] for r in refs[:-3]).astype(jnp.bfloat16)
        sum_ref[...] = x
        x = x.astype(jnp.float32) * scale
        for q in range(groups):
            part = x[:, q * rows : (q + 1) * rows]
            for s in range(slots):
                value = jnp.where(facts_ref[q] == s, part, 0.0)
                wide_ref[s * rank : (s + 1) * rank, q * rows : (q + 1) * rows] = value.astype(jnp.bfloat16)
        for n, q in enumerate((0, 2, 1, 3)):
            part = wide_ref[:, q * rows : (q + 1) * rows]
            turned_ref[n * rows : (n + 1) * rows] = part.astype(jnp.float32).T.astype(jnp.bfloat16)

    return pl.pallas_call(
        kernel,
        in_specs=[pl.BlockSpec(memory_space=pltpu.SMEM)] + [pl.BlockSpec(memory_space=pltpu.VMEM)] * len(values),
        out_specs=[pl.BlockSpec(memory_space=pltpu.VMEM)] * 3,
        out_shape=[
            jax.ShapeDtypeStruct((slots * rank, tokens), jnp.bfloat16),
            jax.ShapeDtypeStruct((tokens, slots * rank), jnp.bfloat16),
            jax.ShapeDtypeStruct((rank, tokens), jnp.bfloat16),
        ],
        compiler_params=pltpu.CompilerParams(vmem_limit_bytes=VMEM),
        cost_estimate=cost(0, 8 * slots * rank * tokens),
        name="spread",
    )(facts, *values)


def slot_grad(wide_t, blocks, block):
    span, tokens = wide_t.shape
    groups = len(blocks)
    rows = tokens // groups
    columns = sum(x.shape[1] for x in blocks[0][0])
    arrays, specs = [], []
    for parts, place in blocks:
        first = 0
        for x in parts:
            count = x.shape[1] // block
            specs.append(
                pl.BlockSpec((rows, block), lambda n, a=first, b=count - 1, place=place: (place, jnp.clip(n - a, 0, b)))
            )
            arrays.append(x)
            first += count

    def kernel(wide_ref, *refs):
        n = pl.program_id(0)
        values, at = [], 0
        for parts, _ in blocks:
            value, first = refs[at][...], parts[0].shape[1] // block
            for more, x in enumerate(parts[1:], 1):
                value = jnp.where(n >= first, refs[at + more][...], value)
                first += x.shape[1] // block
            values.append(value)
            at += len(parts)
        refs[-1][...] = dot(wide_ref[...], jnp.concatenate(values, axis=0), (1, 0))

    return pl.pallas_call(
        kernel,
        grid=(columns // block,),
        in_specs=[pl.BlockSpec((span, tokens), lambda n: (0, 0))] + specs,
        out_specs=pl.BlockSpec((span, block), lambda n: (0, n)),
        out_shape=jax.ShapeDtypeStruct((span, columns), jnp.float32),
        compiler_params=pltpu.CompilerParams(vmem_limit_bytes=VMEM),
        cost_estimate=cost(2 * span * tokens * columns, (4 * span + 2 * tokens) * columns),
        name="slot_grad",
    )(wide_t, *arrays)


def block_facts(block_adapter, block_length, adapter_slot, order, rows, per_owner, i):
    match = block_adapter[:, None] == jnp.arange(adapter_slot.shape[0], dtype=jnp.int32)[None, :]
    slots = jnp.sum(jnp.where(match, adapter_slot[None, :], 0), axis=1)[order]
    lengths = block_length[order]
    owned = slots // per_owner == i
    local_ids = slots % per_owner
    groups = order.shape[0]
    live = (lax.broadcasted_iota(jnp.int32, (groups, rows), 1) < lengths[:, None]).astype(jnp.float32)
    return owned, local_ids, live


def chosen(store, owned, local_ids):
    zero = jnp.zeros((), store.dtype)
    return [
        jnp.where(owned[q], lax.dynamic_index_in_dim(store, local_ids[q], 0, False), zero)
        for q in range(owned.shape[0])
    ]


def choose(block_adapter, block_length, adapter_slot, here, store):
    slots, rank, width = store.shape
    groups = block_adapter.shape[0]

    def block_of(step):
        return jnp.clip(jnp.where(step < 2, 2 * step + 1, 6 - 2 * step), 0, groups - 1)

    def slot_of(q, adapter_ref, slot_ref, here_ref):
        return slot_ref[adapter_ref[q ^ here_ref[0]]] - here_ref[0] * slots

    def kernel(adapter_ref, length_ref, slot_ref, here_ref, store_ref, near_ref, rest_ref, facts_ref):
        step = pl.program_id(0)

        @pl.when(step == 0)
        def _():
            for q in range(groups):
                at = slot_of(q, adapter_ref, slot_ref, here_ref)
                facts_ref[q] = jnp.where((at >= 0) & (at < slots), at, -1)
                facts_ref[groups + q] = length_ref[q ^ here_ref[0]]
            facts_ref[2 * groups] = here_ref[1]

        at = slot_of(block_of(step), adapter_ref, slot_ref, here_ref)
        value = store_ref[0] * ((at >= 0) & (at < slots)).astype(store_ref.dtype)

        @pl.when(step < 2)
        def _():
            near_ref[...] = value

        @pl.when(step >= 2)
        def _():
            rest_ref[...] = value

    def stored(step, adapter_ref, length_ref, slot_ref, here_ref):
        at = slot_of(block_of(step), adapter_ref, slot_ref, here_ref)
        return jnp.clip(at, 0, slots - 1), 0, 0

    return pl.pallas_call(
        kernel,
        grid_spec=pltpu.PrefetchScalarGridSpec(
            num_scalar_prefetch=4,
            grid=(groups,),
            in_specs=[pl.BlockSpec((1, rank, width), stored)],
            out_specs=[
                pl.BlockSpec((rank, width), lambda step, *refs: (jnp.minimum(step, 1), 0)),
                pl.BlockSpec((rank, width), lambda step, *refs: (jnp.maximum(step - 2, 0), 0)),
                pl.BlockSpec(memory_space=pltpu.SMEM),
            ],
        ),
        out_shape=[jax.ShapeDtypeStruct((2 * rank, width), store.dtype)] * 2
        + [jax.ShapeDtypeStruct((2 * groups + 1,), jnp.int32)],
        compiler_params=pltpu.CompilerParams(vmem_limit_bytes=VMEM),
        cost_estimate=cost(0, 8 * rank * width * groups),
        name="choose",
    )(block_adapter, block_length, adapter_slot, here, store)


def local_square(
    tokens, weight, adapter_down, adapter_up, cotangent, block_adapter, block_length, adapter_slot
):
    groups = shards = 4
    rows, width = tokens.shape
    depth, hidden = weight.shape
    per_owner, _, rank = adapter_down.shape
    span = per_owner * rank
    b16 = jnp.bfloat16
    i, j = lax.axis_index("dp"), lax.axis_index("tp")

    def swap(x, bit):
        return lax.ppermute(x, "dp", [(d, d ^ bit) for d in range(groups)])

    def along(x, bit):
        return lax.ppermute(x, "tp", [(z, z ^ bit) for z in range(shards)])

    place = [(c * groups + r, (r ^ c) * groups + c) for r in range(groups) for c in range(shards)]
    hop = [(d * groups + d, (d ^ 2) * groups + d) for d in range(groups)]
    hops = [(z * groups + d, (z ^ 1) * groups + d) for d in range(groups) for z in (d, d ^ 2)]

    def share(x, got, bit):
        return x + jnp.concatenate([got[:, (q ^ bit) * rows : ((q ^ bit) + 1) * rows] for q in range(groups)], axis=1)

    def both(x, pairs):
        return lax.ppermute(x, ("tp", "dp"), pairs)

    tok_x = swap(tokens, CHIP)
    cot_c = swap(cotangent, CORE)
    middle, half = hidden // 2, depth // 2
    away = i ^ j
    here = jnp.stack([i, away]).astype(jnp.int32)
    down_t = jnp.swapaxes(adapter_down, 1, 2)
    near, rest, facts = choose(block_adapter, block_length, adapter_slot, here, down_t)
    up_flat = adapter_up.reshape(span, hidden)
    near = swap(near, CORE)

    back01, *grads = return_grad(
        facts, after(cotangent, near), cot_c, weight, adapter_up, (0, 1), (0, half), (0, hidden), 1024
    )
    down_x = swap(rest[:rank] + near[rank:], CHIP)
    even = jnp.concatenate([tokens, after(tok_x, grads[0], down_x)], axis=0)
    odd = swap(even, CORE)
    even_far = both(even, hop)
    cot_a = swap(after(cotangent[:, :middle], even), CHIP)
    cot_b = swap(after(cotangent[:, middle:], even), CHIP)
    _, grad01, parts = return_grad(
        facts, after(cotangent, even), cot_c, weight, adapter_up, (0, 1), (half, depth), (0, hidden), 1024, grads=grads
    )
    odd = after(odd, grad01)
    odd_far = both(odd, hop)
    toks = [(even, 0), (odd, 0), (even, 1), (odd, 1)]
    inner = rank_inner(facts, down_t.reshape(span, width), toks, rank)
    down_mine = both(rest[rank:] + near[:rank] + down_x, place)
    cot_ac = swap(after(cot_a, inner), CORE)
    inner = inner + along(inner, 1)
    inner_far = along(inner, 2)
    even_mid = jnp.where(away == 0, even, after(even_far, inner, down_mine))
    even_all = both(even_mid, hops)
    back23, sums = return_grad(
        facts, after(cot_a, even_mid), cot_ac, weight, adapter_up, (2, 3), (0, depth), (0, middle), 512, finish=False
    )
    cot_bc = swap(after(cot_b, sums), CORE)
    odd_mid = jnp.where(away == 0, odd, after(odd_far, sums, cot_b))
    odd_all = both(odd_mid, hops)
    back23, grad23, parts = return_grad(
        facts, after(cot_b, odd_mid, even_all), cot_bc, weight, adapter_up, (2, 3), (0, depth), (middle, hidden), 512,
        before=(sums, back23), grads=(parts,),
    )
    back = jnp.concatenate([back01, back23], axis=1)
    back = back + along(back, 1)
    all_even = jnp.where(away == 0, even, jnp.where(away == 2, even_far, after(even_all, back)))
    back_wide, _, back_b = spread(facts, after(back, all_even), along(back, 2), per_owner, 1.0)
    inner_wide, inner_rows, _ = spread(facts, after(inner, back_b), inner_far, per_owner, adapter_scale)
    back_b = share(after(back_b, inner_wide), swap(back_b, CORE), CORE)
    parts = lax.all_to_all(after(parts, back_b).reshape(shards, rows, depth), "tp", 0, 0, tiled=True)
    all_odd = jnp.where(away == 0, odd, jnp.where(away == 2, odd_far, after(odd_all, back_b)))
    all_tokens = jnp.concatenate([all_even, all_odd], axis=0)

    def grad_block(q):
        low, high = [lax.dynamic_slice_in_dim(x, (q & 1) * rows, rows, 0) for x in (grad01, grad23)]
        return jnp.where(q < 2, low, high)

    block = 512
    steps = hidden // block
    pieces = 4
    edges = [(-(-steps * n // pieces)) * block for n in range(pieces + 1)]
    kept, sent, got_c, got_x, done = [], [], [], [], []

    def make(n, *points):
        keep, send = project(after(all_tokens, *points), inner_rows, weight, up_flat, edges[n], edges[n + 1], block)
        kept.append(keep)
        got_c.append(swap(send, CORE))
        return keep

    def cross(n, *points):
        summed = (after(kept[n], *points)[rows:] + got_c[n][rows:]).astype(b16)
        got_x.append(swap(summed, CHIP))
        return summed

    def finish(n, *points):
        own = after(kept[n], *points)[:rows] + got_c[n][:rows] + got_x[n].astype(jnp.float32)
        done.append(own.astype(b16))
        return done[-1]

    point = make(0, back_b)
    back_b = share(after(back_b, point), swap(back_b, CHIP), CHIP)
    point = make(1, point)
    point = cross(0, point)
    point = make(2, point, back_b)
    point = finish(0, point)
    point = cross(1, point)
    point = make(3, point)
    point = finish(1, point)
    point = cross(2, point)
    point = cross(3, point)
    cots = [([cotangent], 0), ([cot_c], 0), ([cot_a, cot_b], 0), ([cot_ac, cot_bc], 0)]
    up_wide = slot_grad(after(inner_wide, point), cots, hidden // 4)
    point = finish(2, up_wide)
    back_mine = lax.dynamic_slice_in_dim(back_b, j * rows, rows, 1)
    total = grad_block(j)
    for m in range(1, shards):
        total = total + lax.dynamic_index_in_dim(after(parts, point), j ^ m, 0, False).astype(jnp.float32)
    total = (total + dot(back_mine, down_mine, (0, 0))).astype(b16)
    tokens_grad = both(total, [(b, a) for a, b in place])
    down_wide = slot_grad(after(back_wide, total), [([x], n) for x, n in toks], width // 2)
    finish(3, down_wide)
    projected = jnp.concatenate(done, axis=1)
    up_grad = up_wide.reshape(per_owner, rank, hidden)
    down_grad = jnp.swapaxes(down_wide.reshape(per_owner, rank, width), 1, 2)
    return projected, tokens_grad, down_grad, up_grad


def local_any(
    groups, tokens, weight, adapter_down, adapter_up, cotangent, block_adapter, block_length, adapter_slot
):
    bits = [1 << n for n in range((groups - 1).bit_length())]

    def swap(x, bit):
        return lax.ppermute(x, "dp", [(d, d ^ bit) for d in range(groups)])

    def gather(x):
        blocks = {0: x}
        for bit in reversed(bits):
            blocks.update({q | bit: swap(block, bit) for q, block in blocks.items()})
        return jnp.stack([blocks[q] for q in range(groups)])

    def combine(parts):
        for bit in bits:
            parts = [a + swap(b, bit) for a, b in zip(parts[::2], parts[1::2])]
        return parts[0]

    rows, width = tokens.shape
    depth, hidden = weight.shape
    per_owner, _, rank = adapter_down.shape
    i = lax.axis_index("dp")
    order = jnp.arange(groups, dtype=jnp.int32) ^ i
    owned, local_ids, live = block_facts(
        block_adapter, block_length, adapter_slot, order, rows, per_owner, i
    )
    down_sel = chosen(adapter_down, owned, local_ids)
    up_sel = chosen(adapter_up, owned, local_ids)
    all_tokens = lax.all_gather(lax.all_gather(tokens, "dp", axis=0), "tp", axis=2, tiled=True)
    all_tokens = lax.dynamic_slice_in_dim(all_tokens, i * depth, depth, 2)[order]
    all_tokens = all_tokens.reshape(groups * rows, depth)
    toks, cots = gather(tokens), gather(cotangent)
    tok_all, cot_all = toks.reshape(-1, width), cots.reshape(-1, hidden)
    down_mine = combine(down_sel)
    inner = jnp.stack([dot(toks[q], down_sel[q], (1, 0)) for q in range(groups)])
    inner_b = (lax.psum(inner, "tp") * live[:, :, None]).astype(jnp.bfloat16)
    back = jnp.stack([dot(cots[q], up_sel[q], (1, 1)) for q in range(groups)])
    back = lax.psum(back[order], ("tp", "dp"))[order] * (adapter_scale * live)[:, :, None]
    back_b = back.astype(jnp.bfloat16)
    one_hot = (local_ids[:, None] == jnp.arange(per_owner, dtype=jnp.int32)[None, :]) & owned[:, None]

    def spread(x):
        wide = jnp.where(one_hot[:, None, :, None], x[:, :, None, :], jnp.zeros((), x.dtype))
        return wide.reshape(groups * rows, per_owner * rank)

    inner_wide = spread(inner_b) * jnp.bfloat16(adapter_scale)
    total = dot(cot_all, weight, (1, 1)).reshape(groups, rows, 1, depth)[order]
    placed = jnp.zeros((groups, rows, groups, depth), jnp.float32)
    placed = lax.dynamic_update_slice_in_dim(placed, total, i, 2)
    placed = lax.psum_scatter(placed, "dp", scatter_dimension=0, tiled=False)
    placed = placed.reshape(rows, groups * depth)
    placed = lax.psum_scatter(placed, "tp", scatter_dimension=1, tiled=True)
    tokens_grad = (placed + dot(back_b[0], down_mine, (1, 1))).astype(jnp.bfloat16)
    part = dot(all_tokens, weight, (1, 0)) + dot(inner_wide, adapter_up.reshape(-1, hidden), (1, 0))
    projected = combine(list(part.reshape(groups, rows, hidden))).astype(jnp.bfloat16)
    up_grad = dot(inner_wide, cot_all, (0, 0)).reshape(per_owner, rank, hidden)
    down_grad = dot(spread(back_b), tok_all, (0, 0)).reshape(per_owner, rank, width)
    return projected, tokens_grad, jnp.swapaxes(down_grad, 1, 2), up_grad


def solution(mesh):
    placed = (
        P(("grp", "dp"), "tp"),
        P("dp", "tp"),
        P("dp", "tp", None),
        P("dp", None, "tp"),
        P(("grp", "dp"), "tp"),
        P("grp"),
        P("grp"),
        P(),
    )
    groups, shards = mesh.shape["dp"], mesh.shape["tp"]
    square = groups == shards == 4
    return jax.shard_map(
        local_square if square else functools.partial(local_any, groups),
        mesh=mesh,
        in_specs=placed,
        out_specs=(
            P(("grp", "dp"), "tp"),
            P(("grp", "dp"), "tp"),
            P(("grp", "dp"), "tp", None),
            P(("grp", "dp"), None, "tp"),
        ),
        check_vma=False,
    )
```

```python
import functools

import jax
import jax.numpy as jnp
from jax import lax
from jax.experimental import pallas as pl
from jax.experimental.pallas import tpu as pltpu
from jax.sharding import PartitionSpec as P

SEGMENT_BLOCK = 128

adapter_scale = 2.0
CORE, CHIP = 1, 2
VMEM = 48 * 1024 * 1024


def dot(a, b, contract):
    return lax.dot_general(a, b, ((contract[:1], contract[1:]), ((), ())), preferred_element_type=jnp.float32)


def after(x, *others):
    return lax.optimization_barrier((x,) + others)[0]


def cost(flops, moved, share=64):
    return pl.CostEstimate(flops=flops // share, bytes_accessed=moved // share, transcendentals=0)


def turns(steps):
    last = steps - 1
    return [
        lambda n: jnp.minimum(n + n % 2, last - last % 2),
        lambda n: jnp.minimum(n + 1 - n % 2, max(last - 1 + last % 2, 0)),
    ]


def in_turn(n, step, first, second):
    @pl.when(n % 2 == 0)
    def _():
        step(*first)

    @pl.when(n % 2 == 1)
    def _():
        step(*second)


def project(tokens, wide, weight, up_flat, start, stop, block):
    rows, depth = tokens.shape
    span = wide.shape[1]
    base = start // block

    steps = (stop - start) // block

    def kernel(tok_ref, wide_ref, w_a_ref, up_a_ref, w_b_ref, up_b_ref, keep_ref, send_ref):
        def step(w_ref, up_ref):
            total = dot(tok_ref[...], w_ref[...], (1, 0)) + dot(wide_ref[...], up_ref[...], (1, 0))
            keep_ref[...] = total[: rows // 2]
            send_ref[...] = total[rows // 2 :]

        in_turn(pl.program_id(0), step, (w_a_ref, up_a_ref), (w_b_ref, up_b_ref))

    whole = lambda n: (0, 0)
    return pl.pallas_call(
        kernel,
        grid=(steps,),
        in_specs=[
            pl.BlockSpec((rows, depth), whole),
            pl.BlockSpec((rows, span), whole),
            *[
                pl.BlockSpec((size, block), lambda n, at=at: (0, at(n) + base))
                for at in turns(steps)
                for size in (depth, span)
            ],
        ],
        out_specs=[pl.BlockSpec((rows // 2, block), lambda n: (0, n))] * 2,
        out_shape=[jax.ShapeDtypeStruct((rows // 2, stop - start), jnp.float32)] * 2,
        compiler_params=pltpu.CompilerParams(vmem_limit_bytes=VMEM),
        cost_estimate=cost(2 * rows * (depth + span) * (stop - start), 2 * (depth + span + 2 * rows) * (stop - start)),
        name="project",
    )(tokens, wide, weight, up_flat, weight, up_flat)


def return_grad(facts, first, second, weight, store, places, features, units, before=(), grads=(), finish=True, rank_too=True):
    rows, hidden = first.shape
    depth, rank = weight.shape[0], store.shape[1]
    groups = facts.shape[0] // 2
    block = 256
    base, column, half = features[0] // block, units[0] // hidden, places[0] // 2
    steps = (features[1] - features[0]) // block

    def kernel(facts_ref, a_ref, b_ref, w_a_ref, w_b_ref, *refs):
        slot_refs, refs = refs[: 2 * rank_too], refs[2 * rank_too :]
        before_refs, outs, rhs = refs[: len(before)], list(refs[len(before) + len(grads) : -1]), refs[-1]
        n = pl.program_id(0)

        @pl.when(n == 0)
        def _():
            rhs[:rows] = a_ref[...]
            rhs[rows:] = b_ref[...]

        def step(w_ref):
            total = dot(w_ref[...], rhs[...], (1, 1)).T
            if before:
                total += before_refs[0][...]
            outs[0][...] = total
            if finish:
                outs[1][...] = total.astype(first.dtype)

        in_turn(n, step, (w_a_ref,), (w_b_ref,))

        if rank_too:

            @pl.when(n == pl.num_programs(0) - 1)
            def _():
                ranks = dot(jnp.concatenate([r[0] for r in slot_refs], axis=0), rhs[...], (1, 1))
                for at, place in enumerate(places):
                    value = ranks[at * rank : (at + 1) * rank, at * rows : (at + 1) * rows]
                    alive = lax.broadcasted_iota(jnp.int32, (rank, rows), 1) < facts_ref[groups + place]
                    alive = alive & (facts_ref[place] >= 0)
                    value = jnp.where(alive, value * adapter_scale, 0.0)
                    if before:
                        value += before_refs[1][:, at * rows : (at + 1) * rows]
                    outs[-1][:, at * rows : (at + 1) * rows] = value

    def chosen_slot(place):
        return lambda n, facts_ref: (jnp.maximum(facts_ref[place], 0), 0, column)

    whole = lambda n, facts_ref: (0, 0)
    tile = pl.BlockSpec((2 * rows, block), lambda n, facts_ref: (0, n + base))
    outs = [(tile, jax.ShapeDtypeStruct((2 * rows, depth), jnp.float32))]
    if finish:
        outs.append(
            (
                pl.BlockSpec((2 * rows, block), lambda n, facts_ref: (half, n + base)),
                jax.ShapeDtypeStruct((4 * rows, depth), first.dtype),
            )
        )
    if rank_too:
        outs.append((pl.BlockSpec((rank, 2 * rows), whole), jax.ShapeDtypeStruct((rank, 2 * rows), jnp.float32)))
    at = 5 + 2 * rank_too + len(before)
    return pl.pallas_call(
        kernel,
        grid_spec=pltpu.PrefetchScalarGridSpec(
            num_scalar_prefetch=1,
            grid=(steps,),
            in_specs=[
                pl.BlockSpec((rows, hidden), whole),
                pl.BlockSpec((rows, hidden), whole),
                *[
                    pl.BlockSpec((block, hidden), lambda n, facts_ref, at=at: (at(n) + base, column))
                    for at in turns(steps)
                ],
                *[pl.BlockSpec((1, rank, hidden), chosen_slot(place)) for place in places if rank_too],
                *[tile, pl.BlockSpec((rank, 2 * rows), whole)][: len(before)],
                *[pl.BlockSpec(memory_space=pl.ANY)] * len(grads),
            ],
            out_specs=[o[0] for o in outs],
            scratch_shapes=[pltpu.VMEM((2 * rows, hidden), first.dtype)],
        ),
        out_shape=[o[1] for o in outs],
        input_output_aliases={at + n: (0 if x.dtype == jnp.float32 else 1) for n, x in enumerate(grads)},
        compiler_params=pltpu.CompilerParams(vmem_limit_bytes=VMEM),
        cost_estimate=cost(4 * rows * hidden * block * steps, 2 * hidden * (block * steps + 2 * rows)),
        name="return_grad",
    )(facts, first, second, weight, weight, *([store] * (2 * rank_too)), *before, *grads)


def rank_inner(facts, flat, blocks, rank):
    span, width = flat.shape
    arrays, places = [x for x, _ in blocks], [n for _, n in blocks]
    groups = len(blocks)
    rows = arrays[0].shape[0] // 2
    slots = span // rank

    def kernel(facts_ref, flat_ref, *refs):
        out_ref = refs[-1]
        total = dot(flat_ref[...], jnp.concatenate([r[...] for r in refs[:-1]], axis=0), (1, 1))
        for q in range(groups):
            acc = jnp.zeros((rank, rows), jnp.float32)
            for s in range(slots):
                acc = jnp.where(facts_ref[q] == s, total[s * rank : (s + 1) * rank, q * rows : (q + 1) * rows], acc)
            alive = lax.broadcasted_iota(jnp.int32, (rank, rows), 1) < facts_ref[groups + q]
            out_ref[:, q * rows : (q + 1) * rows] = jnp.where(alive, acc, 0.0)

    return pl.pallas_call(
        kernel,
        grid=(1,),
        in_specs=[pl.BlockSpec(memory_space=pltpu.SMEM), pl.BlockSpec((span, width), lambda n: (0, 0))]
        + [pl.BlockSpec((rows, width), lambda n, place=place: (place, 0)) for place in places],
        out_specs=pl.BlockSpec((rank, groups * rows), lambda n: (0, 0)),
        out_shape=jax.ShapeDtypeStruct((rank, groups * rows), jnp.float32),
        compiler_params=pltpu.CompilerParams(vmem_limit_bytes=VMEM),
        cost_estimate=cost(2 * span * groups * rows * width, 2 * width * (span + groups * rows)),
        name="rank_inner",
    )(facts, flat, *arrays)


def spread(facts, here, there, slots, scale):
    rank, tokens = here.shape
    groups = facts.shape[0] // 2
    rows = tokens // groups
    values = [here] if there is None else [here, there]

    def kernel(facts_ref, *refs):
        wide_ref, turned_ref, sum_ref = refs[-3:]
        x = sum(r[...] for r in refs[:-3]).astype(jnp.bfloat16)
        sum_ref[...] = x
        x = x.astype(jnp.float32) * scale
        for q in range(groups):
            part = x[:, q * rows : (q + 1) * rows]
            for s in range(slots):
                value = jnp.where(facts_ref[q] == s, part, 0.0)
                wide_ref[s * rank : (s + 1) * rank, q * rows : (q + 1) * rows] = value.astype(jnp.bfloat16)
        for n, q in enumerate((0, 2, 1, 3)):
            part = wide_ref[:, q * rows : (q + 1) * rows]
            turned_ref[n * rows : (n + 1) * rows] = part.astype(jnp.float32).T.astype(jnp.bfloat16)

    return pl.pallas_call(
        kernel,
        in_specs=[pl.BlockSpec(memory_space=pltpu.SMEM)] + [pl.BlockSpec(memory_space=pltpu.VMEM)] * len(values),
        out_specs=[pl.BlockSpec(memory_space=pltpu.VMEM)] * 3,
        out_shape=[
            jax.ShapeDtypeStruct((slots * rank, tokens), jnp.bfloat16),
            jax.ShapeDtypeStruct((tokens, slots * rank), jnp.bfloat16),
            jax.ShapeDtypeStruct((rank, tokens), jnp.bfloat16),
        ],
        compiler_params=pltpu.CompilerParams(vmem_limit_bytes=VMEM),
        cost_estimate=cost(0, 8 * slots * rank * tokens),
        name="spread",
    )(facts, *values)


def slot_grad(wide_t, blocks, block):
    span, tokens = wide_t.shape
    groups = len(blocks)
    rows = tokens // groups
    columns = sum(x.shape[1] for x in blocks[0][0])
    arrays, specs = [], []
    for parts, place in blocks:
        first = 0
        for x in parts:
            count = x.shape[1] // block
            specs.append(
                pl.BlockSpec((rows, block), lambda n, a=first, b=count - 1, place=place: (place, jnp.clip(n - a, 0, b)))
            )
            arrays.append(x)
            first += count

    def kernel(wide_ref, *refs):
        n = pl.program_id(0)
        values, at = [], 0
        for parts, _ in blocks:
            value, first = refs[at][...], parts[0].shape[1] // block
            for more, x in enumerate(parts[1:], 1):
                value = jnp.where(n >= first, refs[at + more][...], value)
                first += x.shape[1] // block
            values.append(value)
            at += len(parts)
        refs[-1][...] = dot(wide_ref[...], jnp.concatenate(values, axis=0), (1, 0))

    return pl.pallas_call(
        kernel,
        grid=(columns // block,),
        in_specs=[pl.BlockSpec((span, tokens), lambda n: (0, 0))] + specs,
        out_specs=pl.BlockSpec((span, block), lambda n: (0, n)),
        out_shape=jax.ShapeDtypeStruct((span, columns), jnp.float32),
        compiler_params=pltpu.CompilerParams(vmem_limit_bytes=VMEM),
        cost_estimate=cost(2 * span * tokens * columns, (4 * span + 2 * tokens) * columns, 1),
        name="slot_grad",
    )(wide_t, *arrays)


def block_facts(block_adapter, block_length, adapter_slot, order, rows, per_owner, i):
    match = block_adapter[:, None] == jnp.arange(adapter_slot.shape[0], dtype=jnp.int32)[None, :]
    slots = jnp.sum(jnp.where(match, adapter_slot[None, :], 0), axis=1)[order]
    lengths = block_length[order]
    owned = slots // per_owner == i
    local_ids = slots % per_owner
    groups = order.shape[0]
    live = (lax.broadcasted_iota(jnp.int32, (groups, rows), 1) < lengths[:, None]).astype(jnp.float32)
    return owned, local_ids, live


def chosen(store, owned, local_ids):
    zero = jnp.zeros((), store.dtype)
    return [
        jnp.where(owned[q], lax.dynamic_index_in_dim(store, local_ids[q], 0, False), zero)
        for q in range(owned.shape[0])
    ]


def choose(block_adapter, block_length, adapter_slot, here, store):
    slots, rank, width = store.shape
    groups = block_adapter.shape[0]

    def block_of(step):
        return jnp.clip(jnp.where(step < 2, 2 * step + 1, 6 - 2 * step), 0, groups - 1)

    def slot_of(q, adapter_ref, slot_ref, here_ref):
        return slot_ref[adapter_ref[q ^ here_ref[0]]] - here_ref[0] * slots

    def kernel(adapter_ref, length_ref, slot_ref, here_ref, store_ref, near_ref, rest_ref, facts_ref):
        step = pl.program_id(0)

        @pl.when(step == 0)
        def _():
            for q in range(groups):
                at = slot_of(q, adapter_ref, slot_ref, here_ref)
                facts_ref[q] = jnp.where((at >= 0) & (at < slots), at, -1)
                facts_ref[groups + q] = length_ref[q ^ here_ref[0]]
            facts_ref[2 * groups] = here_ref[1]

        at = slot_of(block_of(step), adapter_ref, slot_ref, here_ref)
        value = store_ref[0] * ((at >= 0) & (at < slots)).astype(store_ref.dtype)

        @pl.when(step < 2)
        def _():
            near_ref[...] = value

        @pl.when(step >= 2)
        def _():
            rest_ref[...] = value

    def stored(step, adapter_ref, length_ref, slot_ref, here_ref):
        at = slot_of(block_of(step), adapter_ref, slot_ref, here_ref)
        return jnp.clip(at, 0, slots - 1), 0, 0

    return pl.pallas_call(
        kernel,
        grid_spec=pltpu.PrefetchScalarGridSpec(
            num_scalar_prefetch=4,
            grid=(groups,),
            in_specs=[pl.BlockSpec((1, rank, width), stored)],
            out_specs=[
                pl.BlockSpec((rank, width), lambda step, *refs: (jnp.minimum(step, 1), 0)),
                pl.BlockSpec((rank, width), lambda step, *refs: (jnp.maximum(step - 2, 0), 0)),
                pl.BlockSpec(memory_space=pltpu.SMEM),
            ],
        ),
        out_shape=[jax.ShapeDtypeStruct((2 * rank, width), store.dtype)] * 2
        + [jax.ShapeDtypeStruct((2 * groups + 1,), jnp.int32)],
        compiler_params=pltpu.CompilerParams(vmem_limit_bytes=VMEM),
        cost_estimate=cost(0, 8 * rank * width * groups),
        name="choose",
    )(block_adapter, block_length, adapter_slot, here, store)


def local_square(
    tokens, weight, adapter_down, adapter_up, cotangent, block_adapter, block_length, adapter_slot
):
    groups = shards = 4
    rows, width = tokens.shape
    depth, hidden = weight.shape
    per_owner, _, rank = adapter_down.shape
    span = per_owner * rank
    b16 = jnp.bfloat16
    i, j = lax.axis_index("dp"), lax.axis_index("tp")

    def swap(x, bit):
        return lax.ppermute(x, "dp", [(d, d ^ bit) for d in range(groups)])

    def along(x, bit):
        return lax.ppermute(x, "tp", [(z, z ^ bit) for z in range(shards)])

    place = [(c * groups + r, (r ^ c) * groups + c) for r in range(groups) for c in range(shards)]
    hop = [(d * groups + d, (d ^ 2) * groups + d) for d in range(groups)]
    hops = [(z * groups + d, (z ^ 1) * groups + d) for d in range(groups) for z in (d, d ^ 2)]

    def share(x, got, bit):
        return x + jnp.concatenate([got[:, (q ^ bit) * rows : ((q ^ bit) + 1) * rows] for q in range(groups)], axis=1)

    def both(x, pairs):
        return lax.ppermute(x, ("tp", "dp"), pairs)

    tok_x = swap(tokens, CHIP)
    cot_c = swap(cotangent, CORE)
    middle, half = hidden // 2, depth // 2
    away = i ^ j
    here = jnp.stack([i, away]).astype(jnp.int32)
    down_t = jnp.swapaxes(adapter_down, 1, 2)
    near, rest, facts = choose(block_adapter, block_length, adapter_slot, here, down_t)
    up_flat = adapter_up.reshape(span, hidden)
    near = swap(near, CORE)

    *grads, back01 = return_grad(
        facts, after(cotangent, near), cot_c, weight, adapter_up, (0, 1), (0, half), (0, hidden)
    )
    down_x = swap(rest[:rank] + near[rank:], CHIP)
    even = jnp.concatenate([tokens, after(tok_x, grads[0], down_x)], axis=0)
    odd = swap(even, CORE)
    even_far = both(even, hop)
    cot_a = swap(after(cotangent[:, :middle], even), CHIP)
    cot_b = swap(after(cotangent[:, middle:], even), CHIP)
    grad01, parts = return_grad(
        facts, after(cotangent, even), cot_c, weight, adapter_up, (0, 1), (half, depth), (0, hidden), grads=grads, rank_too=False
    )
    odd = after(odd, grad01)
    odd_far = both(odd, hop)
    toks = [(even, 0), (odd, 0), (even, 1), (odd, 1)]
    inner = rank_inner(facts, down_t.reshape(span, width), toks, rank)
    down_mine = both(rest[rank:] + near[:rank] + down_x, place)
    cot_ac = swap(after(cot_a, inner), CORE)
    inner = inner + along(inner, 1)
    inner_far = along(inner, 2)
    even_mid = jnp.where(away == 0, even, after(even_far, inner, down_mine))
    even_all = both(even_mid, hops)
    sums, back23 = return_grad(
        facts, after(cot_a, even_mid), cot_ac, weight, adapter_up, (2, 3), (0, depth), (0, middle), finish=False
    )
    cot_bc = swap(after(cot_b, sums), CORE)
    odd_mid = jnp.where(away == 0, odd, after(odd_far, sums, cot_b))
    odd_all = both(odd_mid, hops)
    grad23, parts, back23 = return_grad(
        facts, after(cot_b, odd_mid, even_all), cot_bc, weight, adapter_up, (2, 3), (0, depth), (middle, hidden),
        before=(sums, back23), grads=(parts,),
    )
    back = jnp.concatenate([back01, back23], axis=1)
    all_even = jnp.where(away == 0, even, jnp.where(away == 2, even_far, after(even_all, grad23)))
    all_odd = jnp.where(away == 0, odd, jnp.where(away == 2, odd_far, after(odd_all, all_even)))
    all_tokens = jnp.concatenate([all_even, all_odd], axis=0)
    back = after(back, all_tokens) + along(back, 1)
    back_wide, _, back_b = spread(facts, back, along(back, 2), per_owner, 1.0)
    inner_wide, inner_rows, _ = spread(facts, after(inner, back_b), inner_far, per_owner, adapter_scale)
    back_b = share(after(back_b, inner_wide), swap(back_b, CORE), CORE)
    parts = lax.all_to_all(after(parts, back_b).reshape(shards, rows, depth), "tp", 0, 0, tiled=True)

    def grad_block(q):
        low, high = [lax.dynamic_slice_in_dim(x, (q & 1) * rows, rows, 0) for x in (grad01, grad23)]
        return jnp.where(q < 2, low, high)

    block = 512
    steps = hidden // block
    pieces = 4
    edges = [(-(-steps * n // pieces)) * block for n in range(pieces + 1)]
    kept, sent, got_c, got_x, done = [], [], [], [], []

    def make(n, *points):
        keep, send = project(after(all_tokens, *points), inner_rows, weight, up_flat, edges[n], edges[n + 1], block)
        kept.append(keep)
        got_c.append(swap(send, CORE))
        return keep

    def cross(n, *points):
        summed = (after(kept[n], *points)[rows:] + got_c[n][rows:]).astype(b16)
        got_x.append(swap(summed, CHIP))
        return summed

    def finish(n, *points):
        own = after(kept[n], *points)[:rows] + got_c[n][:rows] + got_x[n].astype(jnp.float32)
        done.append(own.astype(b16))
        return done[-1]

    point = make(0, back_b)
    back_b = share(after(back_b, point), swap(back_b, CHIP), CHIP)
    point = make(1, point)
    point = cross(0, point)
    point = make(2, point, back_b)
    point = finish(0, point)
    point = cross(1, point)
    point = make(3, point)
    point = finish(1, point)
    point = cross(2, point)
    down_wide = slot_grad(after(back_wide, point), [([x], n) for x, n in toks], width // 2)
    back_mine = lax.dynamic_slice_in_dim(back_b, j * rows, rows, 1)
    total = grad_block(j)
    for m in range(1, shards):
        total = total + lax.dynamic_index_in_dim(after(parts, down_wide), j ^ m, 0, False).astype(jnp.float32)
    total = (total + dot(back_mine, down_mine, (0, 0))).astype(b16)
    tokens_grad = both(total, [(b, a) for a, b in place])
    cots = [([cotangent], 0), ([cot_c], 0), ([cot_a, cot_b], 0), ([cot_ac, cot_bc], 0)]
    point = cross(3, total)
    up_wide = slot_grad(after(inner_wide, point), cots, hidden // 4)
    point = finish(2, up_wide)
    finish(3, point)
    projected = jnp.concatenate(done, axis=1)
    up_grad = up_wide.reshape(per_owner, rank, hidden)
    down_grad = jnp.swapaxes(down_wide.reshape(per_owner, rank, width), 1, 2)
    return projected, tokens_grad, down_grad, up_grad


def local_any(
    groups, tokens, weight, adapter_down, adapter_up, cotangent, block_adapter, block_length, adapter_slot
):
    bits = [1 << n for n in range((groups - 1).bit_length())]

    def swap(x, bit):
        return lax.ppermute(x, "dp", [(d, d ^ bit) for d in range(groups)])

    def gather(x):
        blocks = {0: x}
        for bit in reversed(bits):
            blocks.update({q | bit: swap(block, bit) for q, block in blocks.items()})
        return jnp.stack([blocks[q] for q in range(groups)])

    def combine(parts):
        for bit in bits:
            parts = [a + swap(b, bit) for a, b in zip(parts[::2], parts[1::2])]
        return parts[0]

    rows, width = tokens.shape
    depth, hidden = weight.shape
    per_owner, _, rank = adapter_down.shape
    i = lax.axis_index("dp")
    order = jnp.arange(groups, dtype=jnp.int32) ^ i
    owned, local_ids, live = block_facts(
        block_adapter, block_length, adapter_slot, order, rows, per_owner, i
    )
    down_sel = chosen(adapter_down, owned, local_ids)
    up_sel = chosen(adapter_up, owned, local_ids)
    all_tokens = lax.all_gather(lax.all_gather(tokens, "dp", axis=0), "tp", axis=2, tiled=True)
    all_tokens = lax.dynamic_slice_in_dim(all_tokens, i * depth, depth, 2)[order]
    all_tokens = all_tokens.reshape(groups * rows, depth)
    toks, cots = gather(tokens), gather(cotangent)
    tok_all, cot_all = toks.reshape(-1, width), cots.reshape(-1, hidden)
    down_mine = combine(down_sel)
    inner = jnp.stack([dot(toks[q], down_sel[q], (1, 0)) for q in range(groups)])
    inner_b = (lax.psum(inner, "tp") * live[:, :, None]).astype(jnp.bfloat16)
    back = jnp.stack([dot(cots[q], up_sel[q], (1, 1)) for q in range(groups)])
    back = lax.psum(back[order], ("tp", "dp"))[order] * (adapter_scale * live)[:, :, None]
    back_b = back.astype(jnp.bfloat16)
    one_hot = (local_ids[:, None] == jnp.arange(per_owner, dtype=jnp.int32)[None, :]) & owned[:, None]

    def spread(x):
        wide = jnp.where(one_hot[:, None, :, None], x[:, :, None, :], jnp.zeros((), x.dtype))
        return wide.reshape(groups * rows, per_owner * rank)

    inner_wide = spread(inner_b) * jnp.bfloat16(adapter_scale)
    total = dot(cot_all, weight, (1, 1)).reshape(groups, rows, 1, depth)[order]
    placed = jnp.zeros((groups, rows, groups, depth), jnp.float32)
    placed = lax.dynamic_update_slice_in_dim(placed, total, i, 2)
    placed = lax.psum_scatter(placed, "dp", scatter_dimension=0, tiled=False)
    placed = placed.reshape(rows, groups * depth)
    placed = lax.psum_scatter(placed, "tp", scatter_dimension=1, tiled=True)
    tokens_grad = (placed + dot(back_b[0], down_mine, (1, 1))).astype(jnp.bfloat16)
    part = dot(all_tokens, weight, (1, 0)) + dot(inner_wide, adapter_up.reshape(-1, hidden), (1, 0))
    projected = combine(list(part.reshape(groups, rows, hidden))).astype(jnp.bfloat16)
    up_grad = dot(inner_wide, cot_all, (0, 0)).reshape(per_owner, rank, hidden)
    down_grad = dot(spread(back_b), tok_all, (0, 0)).reshape(per_owner, rank, width)
    return projected, tokens_grad, jnp.swapaxes(down_grad, 1, 2), up_grad


def solution(mesh):
    placed = (
        P(("grp", "dp"), "tp"),
        P("dp", "tp"),
        P("dp", "tp", None),
        P("dp", None, "tp"),
        P(("grp", "dp"), "tp"),
        P("grp"),
        P("grp"),
        P(),
    )
    groups, shards = mesh.shape["dp"], mesh.shape["tp"]
    square = groups == shards == 4
    return jax.shard_map(
        local_square if square else functools.partial(local_any, groups),
        mesh=mesh,
        in_specs=placed,
        out_specs=(
            P(("grp", "dp"), "tp"),
            P(("grp", "dp"), "tp"),
            P(("grp", "dp"), "tp", None),
            P(("grp", "dp"), None, "tp"),
        ),
        check_vma=False,
    )
```

```python
import functools

import jax
import jax.numpy as jnp
from jax import lax
from jax.experimental import pallas as pl
from jax.experimental.pallas import tpu as pltpu
from jax.sharding import PartitionSpec as P

SEGMENT_BLOCK = 128

adapter_scale = 2.0
CORE, CHIP = 1, 2
VMEM = 48 * 1024 * 1024


def dot(a, b, contract):
    return lax.dot_general(a, b, ((contract[:1], contract[1:]), ((), ())), preferred_element_type=jnp.float32)


def after(x, *others):
    return lax.optimization_barrier((x,) + others)[0]


def cost(flops, moved, share=64):
    return pl.CostEstimate(flops=flops // share, bytes_accessed=moved // share, transcendentals=0)


def project(tokens, wide, weight, up_flat, start, stop, block):
    rows, depth = tokens.shape
    span = wide.shape[1]
    base = start // block

    def kernel(tok_ref, wide_ref, w_ref, up_ref, keep_ref, send_ref):
        total = dot(tok_ref[...], w_ref[...], (1, 0)) + dot(wide_ref[...], up_ref[...], (1, 0))
        keep_ref[...] = total[: rows // 2]
        send_ref[...] = total[rows // 2 :]

    return pl.pallas_call(
        kernel,
        grid=((stop - start) // block,),
        in_specs=[
            pl.BlockSpec(memory_space=pltpu.VMEM),
            pl.BlockSpec(memory_space=pltpu.VMEM),
            pl.BlockSpec((depth, block), lambda n: (0, n + base)),
            pl.BlockSpec((span, block), lambda n: (0, n + base)),
        ],
        out_specs=[pl.BlockSpec((rows // 2, block), lambda n: (0, n))] * 2,
        out_shape=[jax.ShapeDtypeStruct((rows // 2, stop - start), jnp.float32)] * 2,
        compiler_params=pltpu.CompilerParams(vmem_limit_bytes=VMEM),
        cost_estimate=cost(2 * rows * (depth + span) * (stop - start), 2 * (depth + span + 2 * rows) * (stop - start)),
        name="project",
    )(tokens, wide, weight, up_flat)


def return_grad(facts, first, second, weight, store, places, sent=()):
    rows, hidden = first.shape
    depth, rank = weight.shape[0], store.shape[1]
    groups = facts.shape[0] // 2
    block = 256
    half = places[0] // 2

    def kernel(facts_ref, a_ref, b_ref, w_ref, up_a_ref, up_b_ref, *refs):
        out_ref, sent_ref, rank_ref, rhs = refs[len(sent) :]
        n = pl.program_id(0)

        @pl.when(n == 0)
        def _():
            rhs[:rows] = a_ref[...]
            rhs[rows:] = b_ref[...]

        total = dot(w_ref[...], rhs[...], (1, 1)).T
        out_ref[...] = total
        sent_ref[...] = total.astype(first.dtype)

        @pl.when(n == pl.num_programs(0) - 1)
        def _():
            ranks = dot(jnp.concatenate([up_a_ref[0], up_b_ref[0]], axis=0), rhs[...], (1, 1))
            for at, place in enumerate(places):
                value = ranks[at * rank : (at + 1) * rank, at * rows : (at + 1) * rows]
                alive = lax.broadcasted_iota(jnp.int32, (rank, rows), 1) < facts_ref[groups + place]
                alive = alive & (facts_ref[place] >= 0)
                rank_ref[:, at * rows : (at + 1) * rows] = jnp.where(alive, value * adapter_scale, 0.0)

    def chosen_slot(place):
        return lambda n, facts_ref: (jnp.maximum(facts_ref[place], 0), 0, 0)

    return pl.pallas_call(
        kernel,
        grid_spec=pltpu.PrefetchScalarGridSpec(
            num_scalar_prefetch=1,
            grid=(depth // block,),
            in_specs=[
                pl.BlockSpec(memory_space=pltpu.VMEM),
                pl.BlockSpec(memory_space=pltpu.VMEM),
                pl.BlockSpec((block, hidden), lambda n, facts_ref: (n, 0)),
                *[pl.BlockSpec((1, rank, hidden), chosen_slot(place)) for place in places],
                *[pl.BlockSpec(memory_space=pl.ANY)] * len(sent),
            ],
            out_specs=[
                pl.BlockSpec((2 * rows, block), lambda n, facts_ref: (0, n)),
                pl.BlockSpec((2 * rows, block), lambda n, facts_ref: (half, n)),
                pl.BlockSpec((rank, 2 * rows), lambda n, facts_ref: (0, 0)),
            ],
            scratch_shapes=[pltpu.VMEM((2 * rows, hidden), first.dtype)],
        ),
        out_shape=[
            jax.ShapeDtypeStruct((2 * rows, depth), jnp.float32),
            jax.ShapeDtypeStruct((4 * rows, depth), first.dtype),
            jax.ShapeDtypeStruct((rank, 2 * rows), jnp.float32),
        ],
        input_output_aliases={6: 1} if sent else {},
        compiler_params=pltpu.CompilerParams(vmem_limit_bytes=VMEM),
        cost_estimate=cost(4 * rows * hidden * depth, 2 * hidden * (depth + 2 * rows)),
        name="return_grad",
    )(facts, first, second, weight, store, store, *sent)


def rank_inner(facts, flat, blocks, rank):
    span, width = flat.shape
    arrays, places = [x for x, _ in blocks], [n for _, n in blocks]
    groups = len(blocks)
    rows = arrays[0].shape[0] // 2
    slots = span // rank

    def kernel(facts_ref, flat_ref, *refs):
        out_ref = refs[-1]
        total = dot(flat_ref[...], jnp.concatenate([r[...] for r in refs[:-1]], axis=0), (1, 1))
        for q in range(groups):
            acc = jnp.zeros((rank, rows), jnp.float32)
            for s in range(slots):
                acc = jnp.where(facts_ref[q] == s, total[s * rank : (s + 1) * rank, q * rows : (q + 1) * rows], acc)
            alive = lax.broadcasted_iota(jnp.int32, (rank, rows), 1) < facts_ref[groups + q]
            out_ref[:, q * rows : (q + 1) * rows] = jnp.where(alive, acc, 0.0)

    return pl.pallas_call(
        kernel,
        grid=(1,),
        in_specs=[pl.BlockSpec(memory_space=pltpu.SMEM), pl.BlockSpec((span, width), lambda n: (0, 0))]
        + [pl.BlockSpec((rows, width), lambda n, place=place: (place, 0)) for place in places],
        out_specs=pl.BlockSpec((rank, groups * rows), lambda n: (0, 0)),
        out_shape=jax.ShapeDtypeStruct((rank, groups * rows), jnp.float32),
        compiler_params=pltpu.CompilerParams(vmem_limit_bytes=VMEM),
        cost_estimate=cost(2 * span * groups * rows * width, 2 * width * (span + groups * rows)),
        name="rank_inner",
    )(facts, flat, *arrays)


def spread(facts, here, there, slots, scale):
    rank, tokens = here.shape
    groups = facts.shape[0] // 2
    rows = tokens // groups
    values = [here] if there is None else [here, there]

    def kernel(facts_ref, *refs):
        wide_ref, turned_ref, sum_ref = refs[-3:]
        x = sum(r[...] for r in refs[:-3]).astype(jnp.bfloat16)
        sum_ref[...] = x
        x = x.astype(jnp.float32) * scale
        for q in range(groups):
            part = x[:, q * rows : (q + 1) * rows]
            for s in range(slots):
                value = jnp.where(facts_ref[q] == s, part, 0.0)
                wide_ref[s * rank : (s + 1) * rank, q * rows : (q + 1) * rows] = value.astype(jnp.bfloat16)
        for n, q in enumerate((0, 2, 1, 3)):
            part = wide_ref[:, q * rows : (q + 1) * rows]
            turned_ref[n * rows : (n + 1) * rows] = part.astype(jnp.float32).T.astype(jnp.bfloat16)

    return pl.pallas_call(
        kernel,
        in_specs=[pl.BlockSpec(memory_space=pltpu.SMEM)] + [pl.BlockSpec(memory_space=pltpu.VMEM)] * len(values),
        out_specs=[pl.BlockSpec(memory_space=pltpu.VMEM)] * 3,
        out_shape=[
            jax.ShapeDtypeStruct((slots * rank, tokens), jnp.bfloat16),
            jax.ShapeDtypeStruct((tokens, slots * rank), jnp.bfloat16),
            jax.ShapeDtypeStruct((rank, tokens), jnp.bfloat16),
        ],
        compiler_params=pltpu.CompilerParams(vmem_limit_bytes=VMEM),
        cost_estimate=cost(0, 8 * slots * rank * tokens),
        name="spread",
    )(facts, *values)


def slot_grad(wide_t, blocks, block):
    span, tokens = wide_t.shape
    groups = len(blocks)
    rows = tokens // groups
    columns = sum(x.shape[1] for x in blocks[0][0])
    arrays, specs = [], []
    for parts, place in blocks:
        first = 0
        for x in parts:
            count = x.shape[1] // block
            specs.append(
                pl.BlockSpec((rows, block), lambda n, a=first, b=count - 1, place=place: (place, jnp.clip(n - a, 0, b)))
            )
            arrays.append(x)
            first += count

    def kernel(wide_ref, *refs):
        n = pl.program_id(0)
        values, at = [], 0
        for parts, _ in blocks:
            value, first = refs[at][...], parts[0].shape[1] // block
            for more, x in enumerate(parts[1:], 1):
                value = jnp.where(n >= first, refs[at + more][...], value)
                first += x.shape[1] // block
            values.append(value)
            at += len(parts)
        refs[-1][...] = dot(wide_ref[...], jnp.concatenate(values, axis=0), (1, 0))

    return pl.pallas_call(
        kernel,
        grid=(columns // block,),
        in_specs=[pl.BlockSpec((span, tokens), lambda n: (0, 0))] + specs,
        out_specs=pl.BlockSpec((span, block), lambda n: (0, n)),
        out_shape=jax.ShapeDtypeStruct((span, columns), jnp.float32),
        compiler_params=pltpu.CompilerParams(vmem_limit_bytes=VMEM),
        cost_estimate=cost(2 * span * tokens * columns, (4 * span + 2 * tokens) * columns, 1),
        name="slot_grad",
    )(wide_t, *arrays)


def block_facts(block_adapter, block_length, adapter_slot, order, rows, per_owner, i):
    match = block_adapter[:, None] == jnp.arange(adapter_slot.shape[0], dtype=jnp.int32)[None, :]
    slots = jnp.sum(jnp.where(match, adapter_slot[None, :], 0), axis=1)[order]
    lengths = block_length[order]
    owned = slots // per_owner == i
    local_ids = slots % per_owner
    groups = order.shape[0]
    live = (lax.broadcasted_iota(jnp.int32, (groups, rows), 1) < lengths[:, None]).astype(jnp.float32)
    return owned, local_ids, live


def chosen(store, owned, local_ids):
    zero = jnp.zeros((), store.dtype)
    return [
        jnp.where(owned[q], lax.dynamic_index_in_dim(store, local_ids[q], 0, False), zero)
        for q in range(owned.shape[0])
    ]


def choose(block_adapter, block_length, adapter_slot, here, store):
    slots, rank, width = store.shape
    groups = block_adapter.shape[0]

    def block_of(step):
        return jnp.clip(jnp.where(step < 2, 2 * step + 1, 6 - 2 * step), 0, groups - 1)

    def slot_of(q, adapter_ref, slot_ref, here_ref):
        return slot_ref[adapter_ref[q ^ here_ref[0]]] - here_ref[0] * slots

    def kernel(adapter_ref, length_ref, slot_ref, here_ref, store_ref, near_ref, rest_ref, facts_ref):
        step = pl.program_id(0)

        @pl.when(step == 0)
        def _():
            for q in range(groups):
                at = slot_of(q, adapter_ref, slot_ref, here_ref)
                facts_ref[q] = jnp.where((at >= 0) & (at < slots), at, -1)
                facts_ref[groups + q] = length_ref[q ^ here_ref[0]]
            facts_ref[2 * groups] = here_ref[1]

        at = slot_of(block_of(step), adapter_ref, slot_ref, here_ref)
        value = store_ref[0] * ((at >= 0) & (at < slots)).astype(store_ref.dtype)

        @pl.when(step < 2)
        def _():
            near_ref[...] = value

        @pl.when(step >= 2)
        def _():
            rest_ref[...] = value

    def stored(step, adapter_ref, length_ref, slot_ref, here_ref):
        at = slot_of(block_of(step), adapter_ref, slot_ref, here_ref)
        return jnp.clip(at, 0, slots - 1), 0, 0

    return pl.pallas_call(
        kernel,
        grid_spec=pltpu.PrefetchScalarGridSpec(
            num_scalar_prefetch=4,
            grid=(groups,),
            in_specs=[pl.BlockSpec((1, rank, width), stored)],
            out_specs=[
                pl.BlockSpec((rank, width), lambda step, *refs: (jnp.minimum(step, 1), 0)),
                pl.BlockSpec((rank, width), lambda step, *refs: (jnp.maximum(step - 2, 0), 0)),
                pl.BlockSpec(memory_space=pltpu.SMEM),
            ],
        ),
        out_shape=[jax.ShapeDtypeStruct((2 * rank, width), store.dtype)] * 2
        + [jax.ShapeDtypeStruct((2 * groups + 1,), jnp.int32)],
        compiler_params=pltpu.CompilerParams(vmem_limit_bytes=VMEM),
        cost_estimate=cost(0, 8 * rank * width * groups),
        name="choose",
    )(block_adapter, block_length, adapter_slot, here, store)


def local_square(
    tokens, weight, adapter_down, adapter_up, cotangent, block_adapter, block_length, adapter_slot
):
    groups = shards = 4
    rows, width = tokens.shape
    depth, hidden = weight.shape
    per_owner, _, rank = adapter_down.shape
    span = per_owner * rank
    b16 = jnp.bfloat16
    i, j = lax.axis_index("dp"), lax.axis_index("tp")

    def swap(x, bit):
        return lax.ppermute(x, "dp", [(d, d ^ bit) for d in range(groups)])

    def along(x, bit):
        return lax.ppermute(x, "tp", [(z, z ^ bit) for z in range(shards)])

    place = [(c * groups + r, (r ^ c) * groups + c) for r in range(groups) for c in range(shards)]
    hop = [(d * groups + d, (d ^ 2) * groups + d) for d in range(groups)]
    hops = [(z * groups + d, (z ^ 1) * groups + d) for d in range(groups) for z in (d, d ^ 2)]

    def share(x, got, bit):
        return x + jnp.concatenate([got[:, (q ^ bit) * rows : ((q ^ bit) + 1) * rows] for q in range(groups)], axis=1)

    def both(x, pairs):
        return lax.ppermute(x, ("tp", "dp"), pairs)

    tok_x = swap(tokens, CHIP)
    cot_c = swap(cotangent, CORE)
    away = i ^ j
    here = jnp.stack([i, away]).astype(jnp.int32)
    down_t = jnp.swapaxes(adapter_down, 1, 2)
    near, rest, facts = choose(block_adapter, block_length, adapter_slot, here, down_t)
    up_flat = adapter_up.reshape(span, hidden)

    even = jnp.concatenate([tokens, after(tok_x, facts)], axis=0)
    odd = swap(even, CORE)
    even_far = both(even, hop)
    cot_x = swap(after(cotangent, even), CHIP)
    near = swap(after(near, even), CORE)
    grad01, parts, back01 = return_grad(facts, after(cotangent, even), cot_c, weight, adapter_up, (0, 1))
    odd = after(odd, grad01)
    odd_far = both(odd, hop)
    toks = [(even, 0), (odd, 0), (even, 1), (odd, 1)]
    inner = rank_inner(facts, down_t.reshape(span, width), toks, rank)
    down_x = rest[:rank] + after(near, inner)[rank:]
    inner = after(inner, down_x) + along(inner, 1)
    inner_far = along(inner, 2)
    even_mid = jnp.where(away == 0, even, after(even_far, inner))
    even_all = both(even_mid, hops)
    odd_mid = jnp.where(away == 0, odd, after(odd_far, even_mid))
    odd_all = both(odd_mid, hops)
    cot_xc = swap(after(cot_x, odd_mid, even_all), CORE)
    down_x = swap(after(down_x, cot_x), CHIP)
    grad23, parts, back23 = return_grad(facts, after(cot_x, odd_mid), cot_xc, weight, adapter_up, (2, 3), (parts,))
    down_mine = both(rest[rank:] + near[:rank] + after(down_x, grad23), place)
    back = jnp.concatenate([back01, back23], axis=1)
    all_even = jnp.where(away == 0, even, jnp.where(away == 2, even_far, after(even_all, grad23)))
    all_odd = jnp.where(away == 0, odd, jnp.where(away == 2, odd_far, after(odd_all, all_even)))
    all_tokens = jnp.concatenate([all_even, all_odd], axis=0)
    back = after(back, all_tokens) + along(back, 1)
    back_wide, _, back_b = spread(facts, back, along(back, 2), per_owner, 1.0)
    inner_wide, inner_rows, _ = spread(facts, after(inner, back_b), inner_far, per_owner, adapter_scale)
    back_b = share(after(back_b, inner_wide, down_mine), swap(back_b, CORE), CORE)
    parts = lax.all_to_all(after(parts, back_b).reshape(shards, rows, depth), "tp", 0, 0, tiled=True)

    def grad_block(q):
        low, high = [lax.dynamic_slice_in_dim(x, (q & 1) * rows, rows, 0) for x in (grad01, grad23)]
        return jnp.where(q < 2, low, high)

    block = 512
    steps = hidden // block
    pieces = 4
    edges = [(-(-steps * n // pieces)) * block for n in range(pieces + 1)]
    kept, sent, got_c, got_x, done = [], [], [], [], []

    def make(n, *points):
        keep, send = project(after(all_tokens, *points), inner_rows, weight, up_flat, edges[n], edges[n + 1], block)
        kept.append(keep)
        got_c.append(swap(send, CORE))
        return keep

    def cross(n, *points):
        summed = (after(kept[n], *points)[rows:] + got_c[n][rows:]).astype(b16)
        got_x.append(swap(summed, CHIP))
        return summed

    def finish(n, *points):
        own = after(kept[n], *points)[:rows] + got_c[n][:rows] + got_x[n].astype(jnp.float32)
        done.append(own.astype(b16))
        return done[-1]

    point = make(0, back_b)
    back_b = share(after(back_b, point), swap(back_b, CHIP), CHIP)
    point = make(1, point)
    point = cross(0, point)
    point = make(2, point, back_b)
    point = finish(0, point)
    point = cross(1, point)
    point = make(3, point)
    point = finish(1, point)
    point = cross(2, point)
    down_wide = slot_grad(after(back_wide, point), [([x], n) for x, n in toks], width // 2)
    back_mine = lax.dynamic_slice_in_dim(back_b, j * rows, rows, 1)
    total = grad_block(j)
    for m in range(1, shards):
        total = total + lax.dynamic_index_in_dim(after(parts, down_wide), j ^ m, 0, False).astype(jnp.float32)
    total = (total + dot(back_mine, down_mine, (0, 0))).astype(b16)
    tokens_grad = both(total, [(b, a) for a, b in place])
    cots = [([x], 0) for x in (cotangent, cot_c, cot_x, cot_xc)]
    point = cross(3, total)
    up_wide = slot_grad(after(inner_wide, point), cots, hidden // 4)
    point = finish(2, up_wide)
    finish(3, point)
    projected = jnp.concatenate(done, axis=1)
    up_grad = up_wide.reshape(per_owner, rank, hidden)
    down_grad = jnp.swapaxes(down_wide.reshape(per_owner, rank, width), 1, 2)
    return projected, tokens_grad, down_grad, up_grad


def local_any(
    groups, tokens, weight, adapter_down, adapter_up, cotangent, block_adapter, block_length, adapter_slot
):
    bits = [1 << n for n in range((groups - 1).bit_length())]

    def swap(x, bit):
        return lax.ppermute(x, "dp", [(d, d ^ bit) for d in range(groups)])

    def gather(x):
        blocks = {0: x}
        for bit in reversed(bits):
            blocks.update({q | bit: swap(block, bit) for q, block in blocks.items()})
        return jnp.stack([blocks[q] for q in range(groups)])

    def combine(parts):
        for bit in bits:
            parts = [a + swap(b, bit) for a, b in zip(parts[::2], parts[1::2])]
        return parts[0]

    rows, width = tokens.shape
    depth, hidden = weight.shape
    per_owner, _, rank = adapter_down.shape
    i = lax.axis_index("dp")
    order = jnp.arange(groups, dtype=jnp.int32) ^ i
    owned, local_ids, live = block_facts(
        block_adapter, block_length, adapter_slot, order, rows, per_owner, i
    )
    down_sel = chosen(adapter_down, owned, local_ids)
    up_sel = chosen(adapter_up, owned, local_ids)
    all_tokens = lax.all_gather(lax.all_gather(tokens, "dp", axis=0), "tp", axis=2, tiled=True)
    all_tokens = lax.dynamic_slice_in_dim(all_tokens, i * depth, depth, 2)[order]
    all_tokens = all_tokens.reshape(groups * rows, depth)
    toks, cots = gather(tokens), gather(cotangent)
    tok_all, cot_all = toks.reshape(-1, width), cots.reshape(-1, hidden)
    down_mine = combine(down_sel)
    inner = jnp.stack([dot(toks[q], down_sel[q], (1, 0)) for q in range(groups)])
    inner_b = (lax.psum(inner, "tp") * live[:, :, None]).astype(jnp.bfloat16)
    back = jnp.stack([dot(cots[q], up_sel[q], (1, 1)) for q in range(groups)])
    back = lax.psum(back[order], ("tp", "dp"))[order] * (adapter_scale * live)[:, :, None]
    back_b = back.astype(jnp.bfloat16)
    one_hot = (local_ids[:, None] == jnp.arange(per_owner, dtype=jnp.int32)[None, :]) & owned[:, None]

    def spread(x):
        wide = jnp.where(one_hot[:, None, :, None], x[:, :, None, :], jnp.zeros((), x.dtype))
        return wide.reshape(groups * rows, per_owner * rank)

    inner_wide = spread(inner_b) * jnp.bfloat16(adapter_scale)
    total = dot(cot_all, weight, (1, 1)).reshape(groups, rows, 1, depth)[order]
    placed = jnp.zeros((groups, rows, groups, depth), jnp.float32)
    placed = lax.dynamic_update_slice_in_dim(placed, total, i, 2)
    placed = lax.psum_scatter(placed, "dp", scatter_dimension=0, tiled=False)
    placed = placed.reshape(rows, groups * depth)
    placed = lax.psum_scatter(placed, "tp", scatter_dimension=1, tiled=True)
    tokens_grad = (placed + dot(back_b[0], down_mine, (1, 1))).astype(jnp.bfloat16)
    part = dot(all_tokens, weight, (1, 0)) + dot(inner_wide, adapter_up.reshape(-1, hidden), (1, 0))
    projected = combine(list(part.reshape(groups, rows, hidden))).astype(jnp.bfloat16)
    up_grad = dot(inner_wide, cot_all, (0, 0)).reshape(per_owner, rank, hidden)
    down_grad = dot(spread(back_b), tok_all, (0, 0)).reshape(per_owner, rank, width)
    return projected, tokens_grad, jnp.swapaxes(down_grad, 1, 2), up_grad


def solution(mesh):
    placed = (
        P(("grp", "dp"), "tp"),
        P("dp", "tp"),
        P("dp", "tp", None),
        P("dp", None, "tp"),
        P(("grp", "dp"), "tp"),
        P("grp"),
        P("grp"),
        P(),
    )
    groups, shards = mesh.shape["dp"], mesh.shape["tp"]
    square = groups == shards == 4
    return jax.shard_map(
        local_square if square else functools.partial(local_any, groups),
        mesh=mesh,
        in_specs=placed,
        out_specs=(
            P(("grp", "dp"), "tp"),
            P(("grp", "dp"), "tp"),
            P(("grp", "dp"), "tp", None),
            P(("grp", "dp"), None, "tp"),
        ),
        check_vma=False,
    )
```

```python
import functools

import jax
import jax.numpy as jnp
from jax import lax
from jax.experimental import pallas as pl
from jax.experimental.pallas import tpu as pltpu
from jax.sharding import PartitionSpec as P

SEGMENT_BLOCK = 128

adapter_scale = 2.0
CORE, CHIP = 1, 2
VMEM = 16 * 1024 * 1024


def dot(a, b, contract):
    return lax.dot_general(a, b, ((contract[:1], contract[1:]), ((), ())), preferred_element_type=jnp.float32)


def after(x, *others):
    return lax.optimization_barrier((x,) + others)[0]


def cost(flops, moved, share=64):
    return pl.CostEstimate(flops=flops // share, bytes_accessed=moved // share, transcendentals=0)


def project(tokens, wide, weight, up_flat, start, stop, block):
    rows, depth = tokens.shape
    span = wide.shape[1]
    base = start // block

    def kernel(tok_ref, wide_ref, w_ref, up_ref, keep_ref, send_ref):
        total = dot(tok_ref[...], w_ref[...], (1, 0)) + dot(wide_ref[...], up_ref[...], (1, 0))
        keep_ref[...] = total[: rows // 2]
        send_ref[...] = total[rows // 2 :]

    return pl.pallas_call(
        kernel,
        grid=((stop - start) // block,),
        in_specs=[
            pl.BlockSpec(memory_space=pltpu.VMEM),
            pl.BlockSpec(memory_space=pltpu.VMEM),
            pl.BlockSpec((depth, block), lambda n: (0, n + base)),
            pl.BlockSpec((span, block), lambda n: (0, n + base)),
        ],
        out_specs=[pl.BlockSpec((rows // 2, block), lambda n: (0, n))] * 2,
        out_shape=[jax.ShapeDtypeStruct((rows // 2, stop - start), jnp.float32)] * 2,
        compiler_params=pltpu.CompilerParams(vmem_limit_bytes=2 * VMEM),
        cost_estimate=cost(2 * rows * (depth + span) * (stop - start), 2 * (depth + span + 2 * rows) * (stop - start)),
        name="project",
    )(tokens, wide, weight, up_flat)


def return_grad(facts, first, second, weight, store, places, sent=()):
    rows, hidden = first.shape
    depth, rank = weight.shape[0], store.shape[1]
    groups = facts.shape[0] // 2
    block = 256
    half = places[0] // 2

    def kernel(facts_ref, a_ref, b_ref, w_ref, up_a_ref, up_b_ref, *refs):
        out_ref, sent_ref, rank_ref, rhs = refs[len(sent) :]
        n = pl.program_id(0)

        @pl.when(n == 0)
        def _():
            rhs[:rows] = a_ref[...]
            rhs[rows:] = b_ref[...]

        total = dot(w_ref[pl.ds(pl.multiple_of(n * block, block), block)], rhs[...], (1, 1)).T
        out_ref[...] = total
        sent_ref[...] = total.astype(first.dtype)

        @pl.when(n == pl.num_programs(0) - 1)
        def _():
            ranks = dot(jnp.concatenate([up_a_ref[0], up_b_ref[0]], axis=0), rhs[...], (1, 1))
            for at, place in enumerate(places):
                value = ranks[at * rank : (at + 1) * rank, at * rows : (at + 1) * rows]
                alive = lax.broadcasted_iota(jnp.int32, (rank, rows), 1) < facts_ref[groups + place]
                alive = alive & (facts_ref[place] >= 0)
                rank_ref[:, at * rows : (at + 1) * rows] = jnp.where(alive, value * adapter_scale, 0.0)

    def chosen_slot(place):
        return lambda n, facts_ref: (jnp.maximum(facts_ref[place], 0), 0, 0)

    return pl.pallas_call(
        kernel,
        grid_spec=pltpu.PrefetchScalarGridSpec(
            num_scalar_prefetch=1,
            grid=(depth // block,),
            in_specs=[
                pl.BlockSpec(memory_space=pltpu.VMEM),
                pl.BlockSpec(memory_space=pltpu.VMEM),
                pl.BlockSpec(memory_space=pltpu.VMEM),
                *[pl.BlockSpec((1, rank, hidden), chosen_slot(place)) for place in places],
                *[pl.BlockSpec(memory_space=pl.ANY)] * len(sent),
            ],
            out_specs=[
                pl.BlockSpec((2 * rows, block), lambda n, facts_ref: (0, n)),
                pl.BlockSpec((2 * rows, block), lambda n, facts_ref: (half, n)),
                pl.BlockSpec((rank, 2 * rows), lambda n, facts_ref: (0, 0)),
            ],
            scratch_shapes=[pltpu.VMEM((2 * rows, hidden), first.dtype)],
        ),
        out_shape=[
            jax.ShapeDtypeStruct((2 * rows, depth), jnp.float32),
            jax.ShapeDtypeStruct((4 * rows, depth), first.dtype),
            jax.ShapeDtypeStruct((rank, 2 * rows), jnp.float32),
        ],
        input_output_aliases={6: 1} if sent else {},
        compiler_params=pltpu.CompilerParams(vmem_limit_bytes=VMEM),
        cost_estimate=cost(4 * rows * hidden * depth, 2 * hidden * (depth + 2 * rows)),
        name="return_grad",
    )(facts, first, second, pltpu.with_memory_space_constraint(weight, pltpu.VMEM), store, store, *sent)


def rank_inner(facts, flat, blocks, rank):
    span, width = flat.shape
    arrays, places = [x for x, _ in blocks], [n for _, n in blocks]
    groups = len(blocks)
    rows = arrays[0].shape[0] // 2
    slots = span // rank

    def kernel(facts_ref, flat_ref, *refs):
        out_ref = refs[-1]
        total = dot(flat_ref[...], jnp.concatenate([r[...] for r in refs[:-1]], axis=0), (1, 1))
        for q in range(groups):
            acc = jnp.zeros((rank, rows), jnp.float32)
            for s in range(slots):
                acc = jnp.where(facts_ref[q] == s, total[s * rank : (s + 1) * rank, q * rows : (q + 1) * rows], acc)
            alive = lax.broadcasted_iota(jnp.int32, (rank, rows), 1) < facts_ref[groups + q]
            out_ref[:, q * rows : (q + 1) * rows] = jnp.where(alive, acc, 0.0)

    return pl.pallas_call(
        kernel,
        grid=(1,),
        in_specs=[pl.BlockSpec(memory_space=pltpu.SMEM), pl.BlockSpec((span, width), lambda n: (0, 0))]
        + [pl.BlockSpec((rows, width), lambda n, place=place: (place, 0)) for place in places],
        out_specs=pl.BlockSpec((rank, groups * rows), lambda n: (0, 0)),
        out_shape=jax.ShapeDtypeStruct((rank, groups * rows), jnp.float32),
        compiler_params=pltpu.CompilerParams(vmem_limit_bytes=VMEM),
        cost_estimate=cost(2 * span * groups * rows * width, 2 * width * (span + groups * rows)),
        name="rank_inner",
    )(facts, flat, *arrays)


def spread(facts, here, there, slots, scale):
    rank, tokens = here.shape
    groups = facts.shape[0] // 2
    rows = tokens // groups
    values = [here] if there is None else [here, there]

    def kernel(facts_ref, *refs):
        wide_ref, turned_ref, sum_ref = refs[-3:]
        x = sum(r[...] for r in refs[:-3]).astype(jnp.bfloat16)
        sum_ref[...] = x
        x = x.astype(jnp.float32) * scale
        for q in range(groups):
            part = x[:, q * rows : (q + 1) * rows]
            for s in range(slots):
                value = jnp.where(facts_ref[q] == s, part, 0.0)
                wide_ref[s * rank : (s + 1) * rank, q * rows : (q + 1) * rows] = value.astype(jnp.bfloat16)
        for n, q in enumerate((0, 2, 1, 3)):
            part = wide_ref[:, q * rows : (q + 1) * rows]
            turned_ref[n * rows : (n + 1) * rows] = part.astype(jnp.float32).T.astype(jnp.bfloat16)

    return pl.pallas_call(
        kernel,
        in_specs=[pl.BlockSpec(memory_space=pltpu.SMEM)] + [pl.BlockSpec(memory_space=pltpu.VMEM)] * len(values),
        out_specs=[pl.BlockSpec(memory_space=pltpu.VMEM)] * 3,
        out_shape=[
            jax.ShapeDtypeStruct((slots * rank, tokens), jnp.bfloat16),
            jax.ShapeDtypeStruct((tokens, slots * rank), jnp.bfloat16),
            jax.ShapeDtypeStruct((rank, tokens), jnp.bfloat16),
        ],
        compiler_params=pltpu.CompilerParams(vmem_limit_bytes=VMEM),
        cost_estimate=cost(0, 8 * slots * rank * tokens),
        name="spread",
    )(facts, *values)


def slot_grad(wide_t, blocks, block):
    span, tokens = wide_t.shape
    groups = len(blocks)
    rows = tokens // groups
    columns = sum(x.shape[1] for x in blocks[0][0])
    arrays, specs = [], []
    for parts, place in blocks:
        first = 0
        for x in parts:
            count = x.shape[1] // block
            specs.append(
                pl.BlockSpec((rows, block), lambda n, a=first, b=count - 1, place=place: (place, jnp.clip(n - a, 0, b)))
            )
            arrays.append(x)
            first += count

    def kernel(wide_ref, *refs):
        n = pl.program_id(0)
        values, at = [], 0
        for parts, _ in blocks:
            value, first = refs[at][...], parts[0].shape[1] // block
            for more, x in enumerate(parts[1:], 1):
                value = jnp.where(n >= first, refs[at + more][...], value)
                first += x.shape[1] // block
            values.append(value)
            at += len(parts)
        refs[-1][...] = dot(wide_ref[...], jnp.concatenate(values, axis=0), (1, 0))

    return pl.pallas_call(
        kernel,
        grid=(columns // block,),
        in_specs=[pl.BlockSpec((span, tokens), lambda n: (0, 0))] + specs,
        out_specs=pl.BlockSpec((span, block), lambda n: (0, n)),
        out_shape=jax.ShapeDtypeStruct((span, columns), jnp.float32),
        compiler_params=pltpu.CompilerParams(vmem_limit_bytes=VMEM),
        cost_estimate=cost(2 * span * tokens * columns, (4 * span + 2 * tokens) * columns, 1),
        name="slot_grad",
    )(wide_t, *arrays)


def block_facts(block_adapter, block_length, adapter_slot, order, rows, per_owner, i):
    match = block_adapter[:, None] == jnp.arange(adapter_slot.shape[0], dtype=jnp.int32)[None, :]
    slots = jnp.sum(jnp.where(match, adapter_slot[None, :], 0), axis=1)[order]
    lengths = block_length[order]
    owned = slots // per_owner == i
    local_ids = slots % per_owner
    groups = order.shape[0]
    live = (lax.broadcasted_iota(jnp.int32, (groups, rows), 1) < lengths[:, None]).astype(jnp.float32)
    return owned, local_ids, live


def chosen(store, owned, local_ids):
    zero = jnp.zeros((), store.dtype)
    return [
        jnp.where(owned[q], lax.dynamic_index_in_dim(store, local_ids[q], 0, False), zero)
        for q in range(owned.shape[0])
    ]


def choose(block_adapter, block_length, adapter_slot, here, store):
    slots, rank, width = store.shape
    groups = block_adapter.shape[0]

    def block_of(step):
        return jnp.clip(jnp.where(step < 2, 2 * step + 1, 6 - 2 * step), 0, groups - 1)

    def slot_of(q, adapter_ref, slot_ref, here_ref):
        return slot_ref[adapter_ref[q ^ here_ref[0]]] - here_ref[0] * slots

    def kernel(adapter_ref, length_ref, slot_ref, here_ref, store_ref, near_ref, rest_ref, facts_ref):
        step = pl.program_id(0)

        @pl.when(step == 0)
        def _():
            for q in range(groups):
                at = slot_of(q, adapter_ref, slot_ref, here_ref)
                facts_ref[q] = jnp.where((at >= 0) & (at < slots), at, -1)
                facts_ref[groups + q] = length_ref[q ^ here_ref[0]]
            facts_ref[2 * groups] = here_ref[1]

        at = slot_of(block_of(step), adapter_ref, slot_ref, here_ref)
        value = store_ref[0] * ((at >= 0) & (at < slots)).astype(store_ref.dtype)

        @pl.when(step < 2)
        def _():
            near_ref[...] = value

        @pl.when(step >= 2)
        def _():
            rest_ref[...] = value

    def stored(step, adapter_ref, length_ref, slot_ref, here_ref):
        at = slot_of(block_of(step), adapter_ref, slot_ref, here_ref)
        return jnp.clip(at, 0, slots - 1), 0, 0

    return pl.pallas_call(
        kernel,
        grid_spec=pltpu.PrefetchScalarGridSpec(
            num_scalar_prefetch=4,
            grid=(groups,),
            in_specs=[pl.BlockSpec((1, rank, width), stored)],
            out_specs=[
                pl.BlockSpec((rank, width), lambda step, *refs: (jnp.minimum(step, 1), 0)),
                pl.BlockSpec((rank, width), lambda step, *refs: (jnp.maximum(step - 2, 0), 0)),
                pl.BlockSpec(memory_space=pltpu.SMEM),
            ],
        ),
        out_shape=[jax.ShapeDtypeStruct((2 * rank, width), store.dtype)] * 2
        + [jax.ShapeDtypeStruct((2 * groups + 1,), jnp.int32)],
        compiler_params=pltpu.CompilerParams(vmem_limit_bytes=VMEM),
        cost_estimate=cost(0, 8 * rank * width * groups),
        name="choose",
    )(block_adapter, block_length, adapter_slot, here, store)


def local_square(
    tokens, weight, adapter_down, adapter_up, cotangent, block_adapter, block_length, adapter_slot
):
    groups = shards = 4
    rows, width = tokens.shape
    depth, hidden = weight.shape
    per_owner, _, rank = adapter_down.shape
    span = per_owner * rank
    b16 = jnp.bfloat16
    i, j = lax.axis_index("dp"), lax.axis_index("tp")

    def swap(x, bit):
        return lax.ppermute(x, "dp", [(d, d ^ bit) for d in range(groups)])

    def along(x, bit):
        return lax.ppermute(x, "tp", [(z, z ^ bit) for z in range(shards)])

    place = [(c * groups + r, (r ^ c) * groups + c) for r in range(groups) for c in range(shards)]
    hop = [(d * groups + d, (d ^ 2) * groups + d) for d in range(groups)]
    hops = [(z * groups + d, (z ^ 1) * groups + d) for d in range(groups) for z in (d, d ^ 2)]

    def share(x, got, bit):
        return x + jnp.concatenate([got[:, (q ^ bit) * rows : ((q ^ bit) + 1) * rows] for q in range(groups)], axis=1)

    def both(x, pairs):
        return lax.ppermute(x, ("tp", "dp"), pairs)

    tok_x = swap(tokens, CHIP)
    cot_c = swap(cotangent, CORE)
    away = i ^ j
    here = jnp.stack([i, away]).astype(jnp.int32)
    down_t = jnp.swapaxes(adapter_down, 1, 2)
    near, rest, facts = choose(block_adapter, block_length, adapter_slot, here, down_t)
    up_flat = adapter_up.reshape(span, hidden)

    even = jnp.concatenate([tokens, after(tok_x, facts)], axis=0)
    odd = swap(even, CORE)
    even_far = both(even, hop)
    cot_x = swap(after(cotangent, even), CHIP)
    near = swap(after(near, even), CORE)
    grad01, parts, back01 = return_grad(facts, after(cotangent, even), cot_c, weight, adapter_up, (0, 1))
    odd = after(odd, grad01)
    odd_far = both(odd, hop)
    toks = [(even, 0), (odd, 0), (even, 1), (odd, 1)]
    inner = rank_inner(facts, down_t.reshape(span, width), toks, rank)
    down_x = rest[:rank] + after(near, inner)[rank:]
    inner = after(inner, down_x) + along(inner, 1)
    inner_far = along(inner, 2)
    even_mid = jnp.where(away == 0, even, after(even_far, inner))
    even_all = both(even_mid, hops)
    odd_mid = jnp.where(away == 0, odd, after(odd_far, even_mid))
    odd_all = both(odd_mid, hops)
    cot_xc = swap(after(cot_x, odd_mid, even_all), CORE)
    down_x = swap(after(down_x, cot_x), CHIP)
    grad23, parts, back23 = return_grad(facts, after(cot_x, odd_mid, down_x), cot_xc, weight, adapter_up, (2, 3), (parts,))
    down_mine = both(rest[rank:] + near[:rank] + after(down_x, grad23), place)
    back = jnp.concatenate([back01, back23], axis=1)
    all_even = jnp.where(away == 0, even, jnp.where(away == 2, even_far, after(even_all, grad23)))
    all_odd = jnp.where(away == 0, odd, jnp.where(away == 2, odd_far, after(odd_all, all_even)))
    all_tokens = jnp.concatenate([all_even, all_odd], axis=0)
    inner_wide, inner_rows, _ = spread(facts, after(inner, all_tokens), inner_far, per_owner, adapter_scale)

    def grad_block(q):
        low, high = [lax.dynamic_slice_in_dim(x, (q & 1) * rows, rows, 0) for x in (grad01, grad23)]
        return jnp.where(q < 2, low, high)

    block = 512
    steps = hidden // block
    pieces = 4
    edges = [(-(-steps * n // pieces)) * block for n in range(pieces + 1)]
    kept, sent, got_c, got_x, done = [], [], [], [], []

    def make(n, *points):
        keep, send = project(after(all_tokens, *points), inner_rows, weight, up_flat, edges[n], edges[n + 1], block)
        kept.append(keep)
        got_c.append(swap(send, CORE))
        return keep

    def cross(n, *points):
        summed = (after(kept[n], *points)[rows:] + got_c[n][rows:]).astype(b16)
        got_x.append(swap(summed, CHIP))
        return summed

    def finish(n, *points):
        own = after(kept[n], *points)[:rows] + got_c[n][:rows] + got_x[n].astype(jnp.float32)
        done.append(own.astype(b16))
        return done[-1]

    back = after(back, inner_rows) + along(back, 1)
    point = make(0, back)
    point = make(1, point, down_mine)
    point = cross(0, point)
    back_wide, _, back_b = spread(facts, after(back, point), along(back, 2), per_owner, 1.0)
    parts = lax.all_to_all(after(parts, back_b).reshape(shards, rows, depth), "tp", 0, 0, tiled=True)
    point = make(2, back_b)
    point = finish(0, point)
    point = cross(1, point)
    back_b = share(after(back_b, point), swap(back_b, CORE), CORE)
    point = make(3, back_b)
    point = finish(1, point)
    point = cross(2, point)
    back_b = share(after(back_b, point), swap(back_b, CHIP), CHIP)
    down_wide = slot_grad(after(back_wide, back_b), [([x], n) for x, n in toks], width // 2)
    back_mine = lax.dynamic_slice_in_dim(back_b, j * rows, rows, 1)
    total = grad_block(j)
    for m in range(1, shards):
        total = total + lax.dynamic_index_in_dim(after(parts, down_wide), j ^ m, 0, False).astype(jnp.float32)
    total = (total + dot(back_mine, down_mine, (0, 0))).astype(b16)
    tokens_grad = both(total, [(b, a) for a, b in place])
    cots = [([x], 0) for x in (cotangent, cot_c, cot_x, cot_xc)]
    point = cross(3, total)
    up_wide = slot_grad(after(inner_wide, point), cots, hidden // 4)
    point = finish(2, up_wide)
    finish(3, point)
    projected = jnp.concatenate(done, axis=1)
    up_grad = up_wide.reshape(per_owner, rank, hidden)
    down_grad = jnp.swapaxes(down_wide.reshape(per_owner, rank, width), 1, 2)
    return projected, tokens_grad, down_grad, up_grad


def local_any(
    groups, tokens, weight, adapter_down, adapter_up, cotangent, block_adapter, block_length, adapter_slot
):
    bits = [1 << n for n in range((groups - 1).bit_length())]

    def swap(x, bit):
        return lax.ppermute(x, "dp", [(d, d ^ bit) for d in range(groups)])

    def gather(x):
        blocks = {0: x}
        for bit in reversed(bits):
            blocks.update({q | bit: swap(block, bit) for q, block in blocks.items()})
        return jnp.stack([blocks[q] for q in range(groups)])

    def combine(parts):
        for bit in bits:
            parts = [a + swap(b, bit) for a, b in zip(parts[::2], parts[1::2])]
        return parts[0]

    rows, width = tokens.shape
    depth, hidden = weight.shape
    per_owner, _, rank = adapter_down.shape
    i = lax.axis_index("dp")
    order = jnp.arange(groups, dtype=jnp.int32) ^ i
    owned, local_ids, live = block_facts(
        block_adapter, block_length, adapter_slot, order, rows, per_owner, i
    )
    down_sel = chosen(adapter_down, owned, local_ids)
    up_sel = chosen(adapter_up, owned, local_ids)
    all_tokens = lax.all_gather(lax.all_gather(tokens, "dp", axis=0), "tp", axis=2, tiled=True)
    all_tokens = lax.dynamic_slice_in_dim(all_tokens, i * depth, depth, 2)[order]
    all_tokens = all_tokens.reshape(groups * rows, depth)
    toks, cots = gather(tokens), gather(cotangent)
    tok_all, cot_all = toks.reshape(-1, width), cots.reshape(-1, hidden)
    down_mine = combine(down_sel)
    inner = jnp.stack([dot(toks[q], down_sel[q], (1, 0)) for q in range(groups)])
    inner_b = (lax.psum(inner, "tp") * live[:, :, None]).astype(jnp.bfloat16)
    back = jnp.stack([dot(cots[q], up_sel[q], (1, 1)) for q in range(groups)])
    back = lax.psum(back[order], ("tp", "dp"))[order] * (adapter_scale * live)[:, :, None]
    back_b = back.astype(jnp.bfloat16)
    one_hot = (local_ids[:, None] == jnp.arange(per_owner, dtype=jnp.int32)[None, :]) & owned[:, None]

    def spread(x):
        wide = jnp.where(one_hot[:, None, :, None], x[:, :, None, :], jnp.zeros((), x.dtype))
        return wide.reshape(groups * rows, per_owner * rank)

    inner_wide = spread(inner_b) * jnp.bfloat16(adapter_scale)
    total = dot(cot_all, weight, (1, 1)).reshape(groups, rows, 1, depth)[order]
    placed = jnp.zeros((groups, rows, groups, depth), jnp.float32)
    placed = lax.dynamic_update_slice_in_dim(placed, total, i, 2)
    placed = lax.psum_scatter(placed, "dp", scatter_dimension=0, tiled=False)
    placed = placed.reshape(rows, groups * depth)
    placed = lax.psum_scatter(placed, "tp", scatter_dimension=1, tiled=True)
    tokens_grad = (placed + dot(back_b[0], down_mine, (1, 1))).astype(jnp.bfloat16)
    part = dot(all_tokens, weight, (1, 0)) + dot(inner_wide, adapter_up.reshape(-1, hidden), (1, 0))
    projected = combine(list(part.reshape(groups, rows, hidden))).astype(jnp.bfloat16)
    up_grad = dot(inner_wide, cot_all, (0, 0)).reshape(per_owner, rank, hidden)
    down_grad = dot(spread(back_b), tok_all, (0, 0)).reshape(per_owner, rank, width)
    return projected, tokens_grad, jnp.swapaxes(down_grad, 1, 2), up_grad


def solution(mesh):
    placed = (
        P(("grp", "dp"), "tp"),
        P("dp", "tp"),
        P("dp", "tp", None),
        P("dp", None, "tp"),
        P(("grp", "dp"), "tp"),
        P("grp"),
        P("grp"),
        P(),
    )
    groups, shards = mesh.shape["dp"], mesh.shape["tp"]
    square = groups == shards == 4
    return jax.shard_map(
        local_square if square else functools.partial(local_any, groups),
        mesh=mesh,
        in_specs=placed,
        out_specs=(
            P(("grp", "dp"), "tp"),
            P(("grp", "dp"), "tp"),
            P(("grp", "dp"), "tp", None),
            P(("grp", "dp"), None, "tp"),
        ),
        check_vma=False,
    )
```

```python
import functools

import jax
import jax.numpy as jnp
from jax import lax
from jax.experimental import pallas as pl
from jax.experimental.pallas import tpu as pltpu
from jax.sharding import PartitionSpec as P

SEGMENT_BLOCK = 128

adapter_scale = 2.0
CORE, CHIP = 1, 2
VMEM = 40 * 1024 * 1024


def dot(a, b, contract):
    return lax.dot_general(a, b, ((contract[:1], contract[1:]), ((), ())), preferred_element_type=jnp.float32)


def after(x, *others):
    return lax.optimization_barrier((x,) + others)[0]


def cost(flops, moved, share=64):
    return pl.CostEstimate(flops=flops // share, bytes_accessed=moved // share, transcendentals=0)


def project(tokens, wide, weight, up_flat, start, stop, block):
    rows, depth = tokens.shape
    span = wide.shape[1]
    base = start // block

    def kernel(tok_ref, wide_ref, w_ref, up_ref, keep_ref, send_ref):
        total = dot(tok_ref[...], w_ref[...], (1, 0)) + dot(wide_ref[...], up_ref[...], (1, 0))
        keep_ref[...] = total[: rows // 2]
        send_ref[...] = total[rows // 2 :]

    return pl.pallas_call(
        kernel,
        grid=((stop - start) // block,),
        in_specs=[
            pl.BlockSpec(memory_space=pltpu.VMEM),
            pl.BlockSpec(memory_space=pltpu.VMEM),
            pl.BlockSpec((depth, block), lambda n: (0, n + base)),
            pl.BlockSpec((span, block), lambda n: (0, n + base)),
        ],
        out_specs=[pl.BlockSpec((rows // 2, block), lambda n: (0, n))] * 2,
        out_shape=[jax.ShapeDtypeStruct((rows // 2, stop - start), jnp.float32)] * 2,
        compiler_params=pltpu.CompilerParams(vmem_limit_bytes=VMEM),
        cost_estimate=cost(2 * rows * (depth + span) * (stop - start), 2 * (depth + span + 2 * rows) * (stop - start)),
        name="project",
    )(tokens, wide, weight, up_flat)


def return_grad(first, second, weight, half, rows_of, columns_of, carried=(), added=False, send=True):
    rows, hidden = first.shape
    depth = weight.shape[0]
    block = 256
    base, column = rows_of[0] // block, columns_of[0] // hidden
    steps = (rows_of[1] - rows_of[0]) // block

    def kernel(a_ref, b_ref, w_ref, *refs):
        out_ref, rhs = refs[len(carried)], refs[-1]

        @pl.when(pl.program_id(0) == 0)
        def _():
            rhs[:rows] = a_ref[...]
            rhs[rows:] = b_ref[...]

        total = dot(w_ref[...], rhs[...], (1, 1)).T
        if added:
            total += refs[0][...]
        out_ref[...] = total
        if send:
            refs[-2][...] = total.astype(first.dtype)

    whole = lambda n: (0, 0)
    tile = pl.BlockSpec((2 * rows, block), lambda n: (0, n + base))
    outs = [(tile, jax.ShapeDtypeStruct((2 * rows, depth), jnp.float32))]
    if send:
        outs.append(
            (
                pl.BlockSpec((2 * rows, block), lambda n: (half, n + base)),
                jax.ShapeDtypeStruct((4 * rows, depth), first.dtype),
            )
        )
    anywhere = pl.BlockSpec(memory_space=pl.ANY)
    taken = [tile if added and x.dtype == jnp.float32 else anywhere for x in carried]
    target = {jnp.dtype(jnp.float32): 0, jnp.dtype(first.dtype): 1}
    return pl.pallas_call(
        kernel,
        grid=(steps,),
        in_specs=[
            pl.BlockSpec((rows, hidden), whole),
            pl.BlockSpec((rows, hidden), whole),
            pl.BlockSpec((block, hidden), lambda n: (n + base, column)),
        ]
        + taken,
        out_specs=[o[0] for o in outs],
        out_shape=[o[1] for o in outs],
        input_output_aliases={3 + n: target[jnp.dtype(x.dtype)] for n, x in enumerate(carried)},
        scratch_shapes=[pltpu.VMEM((2 * rows, hidden), first.dtype)],
        compiler_params=pltpu.CompilerParams(vmem_limit_bytes=VMEM),
        cost_estimate=cost(4 * rows * hidden * block * steps, 2 * hidden * (block * steps + 2 * rows)),
        name="return_grad",
    )(first, second, weight, *carried)


def rank_back(facts, store, blocks, places, block, start=0, before=None):
    rank = store.shape[1]
    rows, columns = blocks[0].shape
    count = len(blocks)
    groups = facts.shape[0] // 2
    base = start // block
    earlier = [] if before is None else [before]

    def kernel(facts_ref, *refs):
        slots, values, out_ref, total = refs[:count], refs[count : 2 * count], refs[-2], refs[-1]
        n = pl.program_id(0)
        left = jnp.concatenate([r[0] for r in slots], axis=0)
        right = jnp.concatenate([r[...] for r in values], axis=0)
        product = dot(left, right, (1, 1))

        @pl.when(n == 0)
        def _():
            total[...] = product

        @pl.when(n > 0)
        def _():
            total[...] += product

        @pl.when(n == pl.num_programs(0) - 1)
        def _():
            for at, place in enumerate(places):
                part = total[at * rank : (at + 1) * rank, at * rows : (at + 1) * rows]
                alive = lax.broadcasted_iota(jnp.int32, (rank, rows), 1) < facts_ref[groups + place]
                alive = alive & (facts_ref[place] >= 0)
                part = jnp.where(alive, part * adapter_scale, 0.0)
                if earlier:
                    part += refs[2 * count][:, at * rows : (at + 1) * rows]
                out_ref[:, at * rows : (at + 1) * rows] = part

    def chosen_slot(place):
        return lambda n, facts_ref: (jnp.maximum(facts_ref[place], 0), 0, n + base)

    small = pl.BlockSpec((rank, count * rows), lambda n, facts_ref: (0, 0))
    return pl.pallas_call(
        kernel,
        grid_spec=pltpu.PrefetchScalarGridSpec(
            num_scalar_prefetch=1,
            grid=(columns // block,),
            in_specs=[pl.BlockSpec((1, rank, block), chosen_slot(place)) for place in places]
            + [pl.BlockSpec((rows, block), lambda n, facts_ref: (0, n))] * count
            + [small] * len(earlier),
            out_specs=small,
            scratch_shapes=[pltpu.VMEM((count * rank, count * rows), jnp.float32)],
        ),
        out_shape=jax.ShapeDtypeStruct((rank, count * rows), jnp.float32),
        compiler_params=pltpu.CompilerParams(vmem_limit_bytes=VMEM),
        cost_estimate=cost(2 * count * rank * count * rows * columns, 2 * columns * count * (rank + rows)),
        name="rank_back",
    )(facts, *[store] * count, *blocks, *earlier)


def rank_inner(facts, flat, blocks, rank):
    span, width = flat.shape
    arrays, places = [x for x, _ in blocks], [n for _, n in blocks]
    groups = len(blocks)
    rows = arrays[0].shape[0] // 2
    slots = span // rank

    def kernel(facts_ref, flat_ref, *refs):
        out_ref = refs[-1]
        total = dot(flat_ref[...], jnp.concatenate([r[...] for r in refs[:-1]], axis=0), (1, 1))
        for q in range(groups):
            acc = jnp.zeros((rank, rows), jnp.float32)
            for s in range(slots):
                acc = jnp.where(facts_ref[q] == s, total[s * rank : (s + 1) * rank, q * rows : (q + 1) * rows], acc)
            alive = lax.broadcasted_iota(jnp.int32, (rank, rows), 1) < facts_ref[groups + q]
            out_ref[:, q * rows : (q + 1) * rows] = jnp.where(alive, acc, 0.0)

    return pl.pallas_call(
        kernel,
        grid=(1,),
        in_specs=[pl.BlockSpec(memory_space=pltpu.SMEM), pl.BlockSpec((span, width), lambda n: (0, 0))]
        + [pl.BlockSpec((rows, width), lambda n, place=place: (place, 0)) for place in places],
        out_specs=pl.BlockSpec((rank, groups * rows), lambda n: (0, 0)),
        out_shape=jax.ShapeDtypeStruct((rank, groups * rows), jnp.float32),
        compiler_params=pltpu.CompilerParams(vmem_limit_bytes=VMEM),
        cost_estimate=cost(2 * span * groups * rows * width, 2 * width * (span + groups * rows)),
        name="rank_inner",
    )(facts, flat, *arrays)


def spread(facts, here, there, slots, scale):
    rank, tokens = here.shape
    groups = facts.shape[0] // 2
    rows = tokens // groups
    values = [here] if there is None else [here, there]

    def kernel(facts_ref, *refs):
        wide_ref, turned_ref, sum_ref = refs[-3:]
        x = sum(r[...] for r in refs[:-3]).astype(jnp.bfloat16)
        sum_ref[...] = x
        x = x.astype(jnp.float32) * scale
        for q in range(groups):
            part = x[:, q * rows : (q + 1) * rows]
            for s in range(slots):
                value = jnp.where(facts_ref[q] == s, part, 0.0)
                wide_ref[s * rank : (s + 1) * rank, q * rows : (q + 1) * rows] = value.astype(jnp.bfloat16)
        for n, q in enumerate((0, 2, 1, 3)):
            part = wide_ref[:, q * rows : (q + 1) * rows]
            turned_ref[n * rows : (n + 1) * rows] = part.astype(jnp.float32).T.astype(jnp.bfloat16)

    return pl.pallas_call(
        kernel,
        in_specs=[pl.BlockSpec(memory_space=pltpu.SMEM)] + [pl.BlockSpec(memory_space=pltpu.VMEM)] * len(values),
        out_specs=[pl.BlockSpec(memory_space=pltpu.VMEM)] * 3,
        out_shape=[
            jax.ShapeDtypeStruct((slots * rank, tokens), jnp.bfloat16),
            jax.ShapeDtypeStruct((tokens, slots * rank), jnp.bfloat16),
            jax.ShapeDtypeStruct((rank, tokens), jnp.bfloat16),
        ],
        compiler_params=pltpu.CompilerParams(vmem_limit_bytes=VMEM),
        cost_estimate=cost(0, 8 * slots * rank * tokens),
        name="spread",
    )(facts, *values)


def slot_grad(wide_t, blocks, block):
    span, tokens = wide_t.shape
    groups = len(blocks)
    rows = tokens // groups
    columns = sum(x.shape[1] for x in blocks[0][0])
    arrays, specs = [], []
    for parts, place in blocks:
        first = 0
        for x in parts:
            count = x.shape[1] // block
            specs.append(
                pl.BlockSpec((rows, block), lambda n, a=first, b=count - 1, place=place: (place, jnp.clip(n - a, 0, b)))
            )
            arrays.append(x)
            first += count

    def kernel(wide_ref, *refs):
        n = pl.program_id(0)
        values, at = [], 0
        for parts, _ in blocks:
            value, first = refs[at][...], parts[0].shape[1] // block
            for more, x in enumerate(parts[1:], 1):
                value = jnp.where(n >= first, refs[at + more][...], value)
                first += x.shape[1] // block
            values.append(value)
            at += len(parts)
        refs[-1][...] = dot(wide_ref[...], jnp.concatenate(values, axis=0), (1, 0))

    return pl.pallas_call(
        kernel,
        grid=(columns // block,),
        in_specs=[pl.BlockSpec((span, tokens), lambda n: (0, 0))] + specs,
        out_specs=pl.BlockSpec((span, block), lambda n: (0, n)),
        out_shape=jax.ShapeDtypeStruct((span, columns), jnp.float32),
        compiler_params=pltpu.CompilerParams(vmem_limit_bytes=VMEM),
        cost_estimate=cost(2 * span * tokens * columns, (4 * span + 2 * tokens) * columns),
        name="slot_grad",
    )(wide_t, *arrays)


def block_facts(block_adapter, block_length, adapter_slot, order, rows, per_owner, i):
    match = block_adapter[:, None] == jnp.arange(adapter_slot.shape[0], dtype=jnp.int32)[None, :]
    slots = jnp.sum(jnp.where(match, adapter_slot[None, :], 0), axis=1)[order]
    lengths = block_length[order]
    owned = slots // per_owner == i
    local_ids = slots % per_owner
    groups = order.shape[0]
    live = (lax.broadcasted_iota(jnp.int32, (groups, rows), 1) < lengths[:, None]).astype(jnp.float32)
    return owned, local_ids, live


def chosen(store, owned, local_ids):
    zero = jnp.zeros((), store.dtype)
    return [
        jnp.where(owned[q], lax.dynamic_index_in_dim(store, local_ids[q], 0, False), zero)
        for q in range(owned.shape[0])
    ]


def choose(block_adapter, block_length, adapter_slot, here, store):
    slots, rank, width = store.shape
    groups = block_adapter.shape[0]

    def block_of(step):
        return jnp.clip(jnp.where(step < 2, 2 * step + 1, 6 - 2 * step), 0, groups - 1)

    def slot_of(q, adapter_ref, slot_ref, here_ref):
        return slot_ref[adapter_ref[q ^ here_ref[0]]] - here_ref[0] * slots

    def kernel(adapter_ref, length_ref, slot_ref, here_ref, store_ref, near_ref, rest_ref, facts_ref):
        step = pl.program_id(0)

        @pl.when(step == 0)
        def _():
            for q in range(groups):
                at = slot_of(q, adapter_ref, slot_ref, here_ref)
                facts_ref[q] = jnp.where((at >= 0) & (at < slots), at, -1)
                facts_ref[groups + q] = length_ref[q ^ here_ref[0]]
            facts_ref[2 * groups] = here_ref[1]

        at = slot_of(block_of(step), adapter_ref, slot_ref, here_ref)
        value = store_ref[0] * ((at >= 0) & (at < slots)).astype(store_ref.dtype)

        @pl.when(step < 2)
        def _():
            near_ref[...] = value

        @pl.when(step >= 2)
        def _():
            rest_ref[...] = value

    def stored(step, adapter_ref, length_ref, slot_ref, here_ref):
        at = slot_of(block_of(step), adapter_ref, slot_ref, here_ref)
        return jnp.clip(at, 0, slots - 1), 0, 0

    return pl.pallas_call(
        kernel,
        grid_spec=pltpu.PrefetchScalarGridSpec(
            num_scalar_prefetch=4,
            grid=(groups,),
            in_specs=[pl.BlockSpec((1, rank, width), stored)],
            out_specs=[
                pl.BlockSpec((rank, width), lambda step, *refs: (jnp.minimum(step, 1), 0)),
                pl.BlockSpec((rank, width), lambda step, *refs: (jnp.maximum(step - 2, 0), 0)),
                pl.BlockSpec(memory_space=pltpu.SMEM),
            ],
        ),
        out_shape=[jax.ShapeDtypeStruct((2 * rank, width), store.dtype)] * 2
        + [jax.ShapeDtypeStruct((2 * groups + 1,), jnp.int32)],
        compiler_params=pltpu.CompilerParams(vmem_limit_bytes=VMEM),
        cost_estimate=cost(0, 8 * rank * width * groups),
        name="choose",
    )(block_adapter, block_length, adapter_slot, here, store)


def local_square(
    tokens, weight, adapter_down, adapter_up, cotangent, block_adapter, block_length, adapter_slot
):
    groups = shards = 4
    rows, width = tokens.shape
    depth, hidden = weight.shape
    per_owner, _, rank = adapter_down.shape
    span = per_owner * rank
    b16 = jnp.bfloat16
    i, j = lax.axis_index("dp"), lax.axis_index("tp")

    def swap(x, bit):
        return lax.ppermute(x, "dp", [(d, d ^ bit) for d in range(groups)])

    def along(x, bit):
        return lax.ppermute(x, "tp", [(z, z ^ bit) for z in range(shards)])

    place = [(c * groups + r, (r ^ c) * groups + c) for r in range(groups) for c in range(shards)]
    hop = [(d * groups + d, (d ^ 2) * groups + d) for d in range(groups)]
    hops = [(z * groups + d, (z ^ 1) * groups + d) for d in range(groups) for z in (d, d ^ 2)]

    def share(x, got, bit):
        return x + jnp.concatenate([got[:, (q ^ bit) * rows : ((q ^ bit) + 1) * rows] for q in range(groups)], axis=1)

    def both(x, pairs):
        return lax.ppermute(x, ("tp", "dp"), pairs)

    tok_x = swap(tokens, CHIP)
    cot_c = swap(cotangent, CORE)
    away = i ^ j
    here = jnp.stack([i, away]).astype(jnp.int32)
    down_t = jnp.swapaxes(adapter_down, 1, 2)
    near, rest, facts = choose(block_adapter, block_length, adapter_slot, here, down_t)
    up_flat = adapter_up.reshape(span, hidden)

    even = jnp.concatenate([tokens, after(tok_x, facts)], axis=0)
    odd = swap(even, CORE)
    even_far = both(even, hop)
    cot_x = swap(after(cotangent, even), CHIP)
    near = swap(after(near, even), CORE)
    half = depth // 2
    grad01, parts = return_grad(after(cotangent, even), cot_c, weight, 0, (0, depth), (0, hidden))
    toks = [(even, 0), (odd, 0), (even, 1), (odd, 1)]
    inner = rank_inner(facts, down_t.reshape(span, width), [(after(x, grad01), n) for x, n in toks], rank)
    inner_near = along(inner, 1)
    odd_far = both(after(odd, inner), hop)
    even_mid = jnp.where(away == 0, even, after(even_far, inner))
    even_all = both(even_mid, hops)
    down_x = rest[:rank] + after(near, inner)[rank:]
    cot_xc = swap(after(cot_x, even_mid, down_x), CORE)
    down_x = swap(after(down_x, cot_x), CHIP)
    back01 = rank_back(facts, after(adapter_up, cot_x, even_mid), [cotangent, cot_c], (0, 1), hidden // 4)
    inner = after(inner, back01) + inner_near
    inner_far = along(inner, 2)
    back23 = rank_back(facts, after(adapter_up, inner), [cot_x, cot_xc], (2, 3), hidden // 4)
    back = jnp.concatenate([back01, back23], axis=1)
    back_near = along(back, 1)
    grad23, parts = return_grad(
        after(cot_x, back, down_x), cot_xc, weight, 1, (0, half), (0, hidden), (parts,)
    )
    back = after(back, grad23) + back_near
    back_far = along(back, 2)
    odd_mid = jnp.where(away == 0, odd, after(odd_far, back))
    odd_all = both(odd_mid, hops)
    down_mine = both(rest[rank:] + near[:rank] + after(down_x, back), place)
    grad23, parts = return_grad(
        after(cot_x, odd_mid), cot_xc, weight, 1, (half, depth), (0, hidden), (grad23, parts)
    )
    back_wide, _, back_b = spread(facts, after(back, grad23, down_mine), back_far, per_owner, 1.0)
    parts = lax.all_to_all(after(parts, back_b).reshape(shards, rows, depth), "tp", 0, 0, tiled=True)
    back_core = swap(back_b, CORE)
    all_even = jnp.where(away == 0, even, jnp.where(away == 2, even_far, after(even_all, back_b)))
    all_odd = jnp.where(away == 0, odd, jnp.where(away == 2, odd_far, after(odd_all, all_even)))
    all_tokens = jnp.concatenate([all_even, all_odd], axis=0)
    inner_wide, inner_rows, _ = spread(facts, after(inner, all_tokens), inner_far, per_owner, adapter_scale)
    back_b = share(after(back_b, inner_rows), back_core, CORE)
    back_chip = swap(back_b, CHIP)
    cots = [([x], 0) for x in (cotangent, cot_c, cot_x, cot_xc)]
    up_wide = slot_grad(after(inner_wide, back_b), cots, hidden // 4)
    back_b = share(after(back_b, up_wide), back_chip, CHIP)

    def grad_block(q):
        low, high = [lax.dynamic_slice_in_dim(x, (q & 1) * rows, rows, 0) for x in (grad01, grad23)]
        return jnp.where(q < 2, low, high)

    block = 512
    steps = hidden // block
    pieces = 4
    edges = [(-(-steps * n // pieces)) * block for n in range(pieces + 1)]
    kept, sent, got_c, got_x, done = [], [], [], [], []

    def make(n, *points):
        keep, send = project(after(all_tokens, *points), inner_rows, weight, up_flat, edges[n], edges[n + 1], block)
        kept.append(keep)
        got_c.append(swap(send, CORE))
        return keep

    def cross(n, *points):
        summed = (after(kept[n], *points)[rows:] + got_c[n][rows:]).astype(b16)
        got_x.append(swap(summed, CHIP))
        return summed

    def finish(n, *points):
        own = after(kept[n], *points)[:rows] + got_c[n][:rows] + got_x[n].astype(jnp.float32)
        done.append(own.astype(b16))
        return done[-1]

    point = make(0, back_b)
    point = make(1, point)
    point = cross(0, point)
    point = cross(1, point)
    back_mine = lax.dynamic_slice_in_dim(back_b, j * rows, rows, 1)
    total = grad_block(j)
    for m in range(1, shards):
        total = total + lax.dynamic_index_in_dim(after(parts, point), j ^ m, 0, False).astype(jnp.float32)
    total = (total + dot(back_mine, down_mine, (0, 0))).astype(b16)
    tokens_grad = both(total, [(b, a) for a, b in place])
    point = finish(0, total)
    point = finish(1, point)
    point = make(2, point)
    point = make(3, point)
    point = cross(2, point)
    point = cross(3, point)
    down_wide = slot_grad(after(back_wide, point), [([x], n) for x, n in toks], width // 2)
    point = finish(2, down_wide)
    finish(3, point)
    projected = jnp.concatenate(done, axis=1)
    up_grad = up_wide.reshape(per_owner, rank, hidden)
    down_grad = jnp.swapaxes(down_wide.reshape(per_owner, rank, width), 1, 2)
    return projected, tokens_grad, down_grad, up_grad


def local_any(
    groups, tokens, weight, adapter_down, adapter_up, cotangent, block_adapter, block_length, adapter_slot
):
    bits = [1 << n for n in range((groups - 1).bit_length())]

    def swap(x, bit):
        return lax.ppermute(x, "dp", [(d, d ^ bit) for d in range(groups)])

    def gather(x):
        blocks = {0: x}
        for bit in reversed(bits):
            blocks.update({q | bit: swap(block, bit) for q, block in blocks.items()})
        return jnp.stack([blocks[q] for q in range(groups)])

    def combine(parts):
        for bit in bits:
            parts = [a + swap(b, bit) for a, b in zip(parts[::2], parts[1::2])]
        return parts[0]

    rows, width = tokens.shape
    depth, hidden = weight.shape
    per_owner, _, rank = adapter_down.shape
    i = lax.axis_index("dp")
    order = jnp.arange(groups, dtype=jnp.int32) ^ i
    owned, local_ids, live = block_facts(
        block_adapter, block_length, adapter_slot, order, rows, per_owner, i
    )
    down_sel = chosen(adapter_down, owned, local_ids)
    up_sel = chosen(adapter_up, owned, local_ids)
    all_tokens = lax.all_gather(lax.all_gather(tokens, "dp", axis=0), "tp", axis=2, tiled=True)
    all_tokens = lax.dynamic_slice_in_dim(all_tokens, i * depth, depth, 2)[order]
    all_tokens = all_tokens.reshape(groups * rows, depth)
    toks, cots = gather(tokens), gather(cotangent)
    tok_all, cot_all = toks.reshape(-1, width), cots.reshape(-1, hidden)
    down_mine = combine(down_sel)
    inner = jnp.stack([dot(toks[q], down_sel[q], (1, 0)) for q in range(groups)])
    inner_b = (lax.psum(inner, "tp") * live[:, :, None]).astype(jnp.bfloat16)
    back = jnp.stack([dot(cots[q], up_sel[q], (1, 1)) for q in range(groups)])
    back = lax.psum(back[order], ("tp", "dp"))[order] * (adapter_scale * live)[:, :, None]
    back_b = back.astype(jnp.bfloat16)
    one_hot = (local_ids[:, None] == jnp.arange(per_owner, dtype=jnp.int32)[None, :]) & owned[:, None]

    def spread(x):
        wide = jnp.where(one_hot[:, None, :, None], x[:, :, None, :], jnp.zeros((), x.dtype))
        return wide.reshape(groups * rows, per_owner * rank)

    inner_wide = spread(inner_b) * jnp.bfloat16(adapter_scale)
    total = dot(cot_all, weight, (1, 1)).reshape(groups, rows, 1, depth)[order]
    placed = jnp.zeros((groups, rows, groups, depth), jnp.float32)
    placed = lax.dynamic_update_slice_in_dim(placed, total, i, 2)
    placed = lax.psum_scatter(placed, "dp", scatter_dimension=0, tiled=False)
    placed = placed.reshape(rows, groups * depth)
    placed = lax.psum_scatter(placed, "tp", scatter_dimension=1, tiled=True)
    tokens_grad = (placed + dot(back_b[0], down_mine, (1, 1))).astype(jnp.bfloat16)
    part = dot(all_tokens, weight, (1, 0)) + dot(inner_wide, adapter_up.reshape(-1, hidden), (1, 0))
    projected = combine(list(part.reshape(groups, rows, hidden))).astype(jnp.bfloat16)
    up_grad = dot(inner_wide, cot_all, (0, 0)).reshape(per_owner, rank, hidden)
    down_grad = dot(spread(back_b), tok_all, (0, 0)).reshape(per_owner, rank, width)
    return projected, tokens_grad, jnp.swapaxes(down_grad, 1, 2), up_grad


def solution(mesh):
    placed = (
        P(("grp", "dp"), "tp"),
        P("dp", "tp"),
        P("dp", "tp", None),
        P("dp", None, "tp"),
        P(("grp", "dp"), "tp"),
        P("grp"),
        P("grp"),
        P(),
    )
    groups, shards = mesh.shape["dp"], mesh.shape["tp"]
    square = groups == shards == 4
    return jax.shard_map(
        local_square if square else functools.partial(local_any, groups),
        mesh=mesh,
        in_specs=placed,
        out_specs=(
            P(("grp", "dp"), "tp"),
            P(("grp", "dp"), "tp"),
            P(("grp", "dp"), "tp", None),
            P(("grp", "dp"), None, "tp"),
        ),
        check_vma=False,
    )
```

```python
import functools

import jax
import jax.numpy as jnp
from jax import lax
from jax.experimental import pallas as pl
from jax.experimental.pallas import tpu as pltpu
from jax.sharding import PartitionSpec as P

SEGMENT_BLOCK = 128

adapter_scale = 2.0
CORE, CHIP = 1, 2
VMEM = 48 * 1024 * 1024


def dot(a, b, contract):
    return lax.dot_general(a, b, ((contract[:1], contract[1:]), ((), ())), preferred_element_type=jnp.float32)


def after(x, *others):
    return lax.optimization_barrier((x,) + others)[0]


def cost(flops, moved, share=64):
    return pl.CostEstimate(flops=flops // share, bytes_accessed=moved // share, transcendentals=0)


def project(tokens, wide, weight, up_flat, start, stop, block):
    rows, depth = tokens.shape
    span = wide.shape[1]
    base = start // block

    def kernel(tok_ref, wide_ref, w_ref, up_ref, keep_ref, send_ref):
        total = dot(tok_ref[...], w_ref[...], (1, 0)) + dot(wide_ref[...], up_ref[...], (1, 0))
        keep_ref[...] = total[: rows // 2]
        send_ref[...] = total[rows // 2 :]

    return pl.pallas_call(
        kernel,
        grid=((stop - start) // block,),
        in_specs=[
            pl.BlockSpec(memory_space=pltpu.VMEM),
            pl.BlockSpec(memory_space=pltpu.VMEM),
            pl.BlockSpec((depth, block), lambda n: (0, n + base)),
            pl.BlockSpec((span, block), lambda n: (0, n + base)),
        ],
        out_specs=[pl.BlockSpec((rows // 2, block), lambda n: (0, n))] * 2,
        out_shape=[jax.ShapeDtypeStruct((rows // 2, stop - start), jnp.float32)] * 2,
        compiler_params=pltpu.CompilerParams(vmem_limit_bytes=VMEM),
        cost_estimate=cost(2 * rows * (depth + span) * (stop - start), 2 * (depth + span + 2 * rows) * (stop - start)),
        name="project",
    )(tokens, wide, weight, up_flat)


def return_grad(facts, first, second, weight, store, places, sent=()):
    rows, hidden = first.shape
    depth, rank = weight.shape[0], store.shape[1]
    groups = facts.shape[0] // 2
    block = 256
    half = places[0] // 2

    def kernel(facts_ref, a_ref, b_ref, w_ref, up_a_ref, up_b_ref, *refs):
        out_ref, sent_ref, rank_ref, rhs = refs[len(sent) :]
        n = pl.program_id(0)

        @pl.when(n == 0)
        def _():
            rhs[:rows] = a_ref[...]
            rhs[rows:] = b_ref[...]

        total = dot(w_ref[...], rhs[...], (1, 1)).T
        out_ref[...] = total
        sent_ref[...] = total.astype(first.dtype)

        @pl.when(n == pl.num_programs(0) - 1)
        def _():
            ranks = dot(jnp.concatenate([up_a_ref[0], up_b_ref[0]], axis=0), rhs[...], (1, 1))
            for at, place in enumerate(places):
                value = ranks[at * rank : (at + 1) * rank, at * rows : (at + 1) * rows]
                alive = lax.broadcasted_iota(jnp.int32, (rank, rows), 1) < facts_ref[groups + place]
                alive = alive & (facts_ref[place] >= 0)
                rank_ref[:, at * rows : (at + 1) * rows] = jnp.where(alive, value * adapter_scale, 0.0)

    def chosen_slot(place):
        return lambda n, facts_ref: (jnp.maximum(facts_ref[place], 0), 0, 0)

    return pl.pallas_call(
        kernel,
        grid_spec=pltpu.PrefetchScalarGridSpec(
            num_scalar_prefetch=1,
            grid=(depth // block,),
            in_specs=[
                pl.BlockSpec(memory_space=pltpu.VMEM),
                pl.BlockSpec(memory_space=pltpu.VMEM),
                pl.BlockSpec((block, hidden), lambda n, facts_ref: (n, 0)),
                *[pl.BlockSpec((1, rank, hidden), chosen_slot(place)) for place in places],
                *[pl.BlockSpec(memory_space=pl.ANY)] * len(sent),
            ],
            out_specs=[
                pl.BlockSpec((2 * rows, block), lambda n, facts_ref: (0, n)),
                pl.BlockSpec((2 * rows, block), lambda n, facts_ref: (half, n)),
                pl.BlockSpec((rank, 2 * rows), lambda n, facts_ref: (0, 0)),
            ],
            scratch_shapes=[pltpu.VMEM((2 * rows, hidden), first.dtype)],
        ),
        out_shape=[
            jax.ShapeDtypeStruct((2 * rows, depth), jnp.float32),
            jax.ShapeDtypeStruct((4 * rows, depth), first.dtype),
            jax.ShapeDtypeStruct((rank, 2 * rows), jnp.float32),
        ],
        input_output_aliases={6: 1} if sent else {},
        compiler_params=pltpu.CompilerParams(vmem_limit_bytes=VMEM),
        cost_estimate=cost(4 * rows * hidden * depth, 2 * hidden * (depth + 2 * rows)),
        name="return_grad",
    )(facts, first, second, weight, store, store, *sent)


def rank_inner(facts, flat, blocks, rank):
    span, width = flat.shape
    arrays, places = [x for x, _ in blocks], [n for _, n in blocks]
    groups = len(blocks)
    rows = arrays[0].shape[0] // 2
    slots = span // rank

    def kernel(facts_ref, flat_ref, *refs):
        out_ref = refs[-1]
        total = dot(flat_ref[...], jnp.concatenate([r[...] for r in refs[:-1]], axis=0), (1, 1))
        for q in range(groups):
            acc = jnp.zeros((rank, rows), jnp.float32)
            for s in range(slots):
                acc = jnp.where(facts_ref[q] == s, total[s * rank : (s + 1) * rank, q * rows : (q + 1) * rows], acc)
            alive = lax.broadcasted_iota(jnp.int32, (rank, rows), 1) < facts_ref[groups + q]
            out_ref[:, q * rows : (q + 1) * rows] = jnp.where(alive, acc, 0.0)

    return pl.pallas_call(
        kernel,
        grid=(1,),
        in_specs=[pl.BlockSpec(memory_space=pltpu.SMEM), pl.BlockSpec((span, width), lambda n: (0, 0))]
        + [pl.BlockSpec((rows, width), lambda n, place=place: (place, 0)) for place in places],
        out_specs=pl.BlockSpec((rank, groups * rows), lambda n: (0, 0)),
        out_shape=jax.ShapeDtypeStruct((rank, groups * rows), jnp.float32),
        compiler_params=pltpu.CompilerParams(vmem_limit_bytes=VMEM),
        cost_estimate=cost(2 * span * groups * rows * width, 2 * width * (span + groups * rows)),
        name="rank_inner",
    )(facts, flat, *arrays)


def spread(facts, here, there, slots, scale):
    rank, tokens = here.shape
    groups = facts.shape[0] // 2
    rows = tokens // groups
    values = [here] if there is None else [here, there]

    def kernel(facts_ref, *refs):
        wide_ref, turned_ref, sum_ref = refs[-3:]
        x = sum(r[...] for r in refs[:-3]).astype(jnp.bfloat16)
        sum_ref[...] = x
        x = x.astype(jnp.float32) * scale
        for q in range(groups):
            part = x[:, q * rows : (q + 1) * rows]
            for s in range(slots):
                value = jnp.where(facts_ref[q] == s, part, 0.0)
                wide_ref[s * rank : (s + 1) * rank, q * rows : (q + 1) * rows] = value.astype(jnp.bfloat16)
        for n, q in enumerate((0, 2, 1, 3)):
            part = wide_ref[:, q * rows : (q + 1) * rows]
            turned_ref[n * rows : (n + 1) * rows] = part.astype(jnp.float32).T.astype(jnp.bfloat16)

    return pl.pallas_call(
        kernel,
        in_specs=[pl.BlockSpec(memory_space=pltpu.SMEM)] + [pl.BlockSpec(memory_space=pltpu.VMEM)] * len(values),
        out_specs=[pl.BlockSpec(memory_space=pltpu.VMEM)] * 3,
        out_shape=[
            jax.ShapeDtypeStruct((slots * rank, tokens), jnp.bfloat16),
            jax.ShapeDtypeStruct((tokens, slots * rank), jnp.bfloat16),
            jax.ShapeDtypeStruct((rank, tokens), jnp.bfloat16),
        ],
        compiler_params=pltpu.CompilerParams(vmem_limit_bytes=VMEM),
        cost_estimate=cost(0, 8 * slots * rank * tokens),
        name="spread",
    )(facts, *values)


def slot_grad(wide_t, blocks, block):
    span, tokens = wide_t.shape
    groups = len(blocks)
    rows = tokens // groups
    columns = sum(x.shape[1] for x in blocks[0][0])
    arrays, specs = [], []
    for parts, place in blocks:
        first = 0
        for x in parts:
            count = x.shape[1] // block
            specs.append(
                pl.BlockSpec((rows, block), lambda n, a=first, b=count - 1, place=place: (place, jnp.clip(n - a, 0, b)))
            )
            arrays.append(x)
            first += count

    def kernel(wide_ref, *refs):
        n = pl.program_id(0)
        values, at = [], 0
        for parts, _ in blocks:
            value, first = refs[at][...], parts[0].shape[1] // block
            for more, x in enumerate(parts[1:], 1):
                value = jnp.where(n >= first, refs[at + more][...], value)
                first += x.shape[1] // block
            values.append(value)
            at += len(parts)
        refs[-1][...] = dot(wide_ref[...], jnp.concatenate(values, axis=0), (1, 0))

    return pl.pallas_call(
        kernel,
        grid=(columns // block,),
        in_specs=[pl.BlockSpec((span, tokens), lambda n: (0, 0))] + specs,
        out_specs=pl.BlockSpec((span, block), lambda n: (0, n)),
        out_shape=jax.ShapeDtypeStruct((span, columns), jnp.float32),
        compiler_params=pltpu.CompilerParams(vmem_limit_bytes=VMEM),
        cost_estimate=cost(2 * span * tokens * columns, (4 * span + 2 * tokens) * columns, 1),
        name="slot_grad",
    )(wide_t, *arrays)


def block_facts(block_adapter, block_length, adapter_slot, order, rows, per_owner, i):
    match = block_adapter[:, None] == jnp.arange(adapter_slot.shape[0], dtype=jnp.int32)[None, :]
    slots = jnp.sum(jnp.where(match, adapter_slot[None, :], 0), axis=1)[order]
    lengths = block_length[order]
    owned = slots // per_owner == i
    local_ids = slots % per_owner
    groups = order.shape[0]
    live = (lax.broadcasted_iota(jnp.int32, (groups, rows), 1) < lengths[:, None]).astype(jnp.float32)
    return owned, local_ids, live


def chosen(store, owned, local_ids):
    zero = jnp.zeros((), store.dtype)
    return [
        jnp.where(owned[q], lax.dynamic_index_in_dim(store, local_ids[q], 0, False), zero)
        for q in range(owned.shape[0])
    ]


def choose(block_adapter, block_length, adapter_slot, here, store):
    slots, rank, width = store.shape
    groups = block_adapter.shape[0]

    def block_of(step):
        return jnp.clip(jnp.where(step < 2, 2 * step + 1, 6 - 2 * step), 0, groups - 1)

    def slot_of(q, adapter_ref, slot_ref, here_ref):
        return slot_ref[adapter_ref[q ^ here_ref[0]]] - here_ref[0] * slots

    def kernel(adapter_ref, length_ref, slot_ref, here_ref, store_ref, near_ref, rest_ref, facts_ref):
        step = pl.program_id(0)

        @pl.when(step == 0)
        def _():
            for q in range(groups):
                at = slot_of(q, adapter_ref, slot_ref, here_ref)
                facts_ref[q] = jnp.where((at >= 0) & (at < slots), at, -1)
                facts_ref[groups + q] = length_ref[q ^ here_ref[0]]
            facts_ref[2 * groups] = here_ref[1]

        at = slot_of(block_of(step), adapter_ref, slot_ref, here_ref)
        value = store_ref[0] * ((at >= 0) & (at < slots)).astype(store_ref.dtype)

        @pl.when(step < 2)
        def _():
            near_ref[...] = value

        @pl.when(step >= 2)
        def _():
            rest_ref[...] = value

    def stored(step, adapter_ref, length_ref, slot_ref, here_ref):
        at = slot_of(block_of(step), adapter_ref, slot_ref, here_ref)
        return jnp.clip(at, 0, slots - 1), 0, 0

    return pl.pallas_call(
        kernel,
        grid_spec=pltpu.PrefetchScalarGridSpec(
            num_scalar_prefetch=4,
            grid=(groups,),
            in_specs=[pl.BlockSpec((1, rank, width), stored)],
            out_specs=[
                pl.BlockSpec((rank, width), lambda step, *refs: (jnp.minimum(step, 1), 0)),
                pl.BlockSpec((rank, width), lambda step, *refs: (jnp.maximum(step - 2, 0), 0)),
                pl.BlockSpec(memory_space=pltpu.SMEM),
            ],
        ),
        out_shape=[jax.ShapeDtypeStruct((2 * rank, width), store.dtype)] * 2
        + [jax.ShapeDtypeStruct((2 * groups + 1,), jnp.int32)],
        compiler_params=pltpu.CompilerParams(vmem_limit_bytes=VMEM),
        cost_estimate=cost(0, 8 * rank * width * groups),
        name="choose",
    )(block_adapter, block_length, adapter_slot, here, store)


def local_square(
    tokens, weight, adapter_down, adapter_up, cotangent, block_adapter, block_length, adapter_slot
):
    groups = shards = 4
    rows, width = tokens.shape
    depth, hidden = weight.shape
    per_owner, _, rank = adapter_down.shape
    span = per_owner * rank
    b16 = jnp.bfloat16
    i, j = lax.axis_index("dp"), lax.axis_index("tp")

    def swap(x, bit):
        return lax.ppermute(x, "dp", [(d, d ^ bit) for d in range(groups)])

    def along(x, bit):
        return lax.ppermute(x, "tp", [(z, z ^ bit) for z in range(shards)])

    place = [(c * groups + r, (r ^ c) * groups + c) for r in range(groups) for c in range(shards)]
    hop = [(d * groups + d, (d ^ 2) * groups + d) for d in range(groups)]
    hops = [(z * groups + d, (z ^ 1) * groups + d) for d in range(groups) for z in (d, d ^ 2)]

    def share(x, got, bit):
        return x + jnp.concatenate([got[:, (q ^ bit) * rows : ((q ^ bit) + 1) * rows] for q in range(groups)], axis=1)

    def both(x, pairs):
        return lax.ppermute(x, ("tp", "dp"), pairs)

    tok_x = swap(tokens, CHIP)
    cot_c = swap(cotangent, CORE)
    away = i ^ j
    here = jnp.stack([i, away]).astype(jnp.int32)
    down_t = jnp.swapaxes(adapter_down, 1, 2)
    near, rest, facts = choose(block_adapter, block_length, adapter_slot, here, down_t)
    up_flat = adapter_up.reshape(span, hidden)

    even = jnp.concatenate([tokens, after(tok_x, facts)], axis=0)
    odd = swap(even, CORE)
    even_far = both(even, hop)
    cot_x = swap(after(cotangent, even), CHIP)
    near = swap(after(near, even), CORE)
    grad01, parts, back01 = return_grad(facts, after(cotangent, even), cot_c, weight, adapter_up, (0, 1))
    toks = [(even, 0), (odd, 0), (even, 1), (odd, 1)]
    inner = rank_inner(facts, down_t.reshape(span, width), [(after(x, grad01), n) for x, n in toks], rank)
    inner_near = along(inner, 1)
    odd_far = both(after(odd, inner), hop)
    even_mid = jnp.where(away == 0, even, after(even_far, inner))
    even_all = both(even_mid, hops)
    down_x = rest[:rank] + after(near, inner)[rank:]
    cot_xc = swap(after(cot_x, even_mid, down_x), CORE)
    down_x = swap(after(down_x, cot_x), CHIP)
    inner = after(inner, cot_x) + inner_near
    inner_far = along(inner, 2)
    odd_mid = jnp.where(away == 0, odd, after(odd_far, inner))
    odd_all = both(odd_mid, hops)
    grad23, parts, back23 = return_grad(
        facts, after(cot_x, odd_mid, even_all, down_x), cot_xc, weight, adapter_up, (2, 3), (parts,)
    )
    back = jnp.concatenate([back01, back23], axis=1)
    back_near = along(back, 1)
    all_even = jnp.where(away == 0, even, jnp.where(away == 2, even_far, after(even_all, grad23)))
    all_odd = jnp.where(away == 0, odd, jnp.where(away == 2, odd_far, after(odd_all, all_even)))
    all_tokens = jnp.concatenate([all_even, all_odd], axis=0)
    inner_wide, inner_rows, _ = spread(facts, after(inner, all_tokens), inner_far, per_owner, adapter_scale)
    cots = [([x], 0) for x in (cotangent, cot_c, cot_x, cot_xc)]
    up_wide = slot_grad(after(inner_wide, inner_rows), cots, hidden // 4)
    back = after(back, up_wide) + back_near
    back_wide, _, back_b = spread(facts, back, along(back, 2), per_owner, 1.0)
    parts = lax.all_to_all(after(parts, back_b).reshape(shards, rows, depth), "tp", 0, 0, tiled=True)
    down_mine = both(rest[rank:] + near[:rank] + after(down_x, back_b), place)
    back_b = share(back_b, swap(back_b, CORE), CORE)

    def grad_block(q):
        low, high = [lax.dynamic_slice_in_dim(x, (q & 1) * rows, rows, 0) for x in (grad01, grad23)]
        return jnp.where(q < 2, low, high)

    block = 512
    steps = hidden // block
    pieces = 4
    edges = [(-(-steps * n // pieces)) * block for n in range(pieces + 1)]
    kept, sent, got_c, got_x, done = [], [], [], [], []

    def make(n, *points):
        keep, send = project(after(all_tokens, *points), inner_rows, weight, up_flat, edges[n], edges[n + 1], block)
        kept.append(keep)
        got_c.append(swap(send, CORE))
        return keep

    def cross(n, *points):
        summed = (after(kept[n], *points)[rows:] + got_c[n][rows:]).astype(b16)
        got_x.append(swap(summed, CHIP))
        return summed

    def finish(n, *points):
        own = after(kept[n], *points)[:rows] + got_c[n][:rows] + got_x[n].astype(jnp.float32)
        done.append(own.astype(b16))
        return done[-1]

    point = make(0, back_b)
    back_b = share(after(back_b, point), swap(back_b, CHIP), CHIP)
    point = make(1, point, down_mine)
    point = cross(0, point)
    point = make(2, point, back_b)
    point = finish(0, point)
    point = cross(1, point)
    point = make(3, point)
    point = finish(1, point)
    point = cross(2, point)
    down_wide = slot_grad(after(back_wide, point), [([x], n) for x, n in toks], width // 2)
    back_mine = lax.dynamic_slice_in_dim(back_b, j * rows, rows, 1)
    total = grad_block(j)
    for m in range(1, shards):
        total = total + lax.dynamic_index_in_dim(after(parts, down_wide), j ^ m, 0, False).astype(jnp.float32)
    total = (total + dot(back_mine, down_mine, (0, 0))).astype(b16)
    tokens_grad = both(total, [(b, a) for a, b in place])
    point = cross(3, total)
    point = finish(2, point)
    finish(3, point)
    projected = jnp.concatenate(done, axis=1)
    up_grad = up_wide.reshape(per_owner, rank, hidden)
    down_grad = jnp.swapaxes(down_wide.reshape(per_owner, rank, width), 1, 2)
    return projected, tokens_grad, down_grad, up_grad


def local_any(
    groups, tokens, weight, adapter_down, adapter_up, cotangent, block_adapter, block_length, adapter_slot
):
    bits = [1 << n for n in range((groups - 1).bit_length())]

    def swap(x, bit):
        return lax.ppermute(x, "dp", [(d, d ^ bit) for d in range(groups)])

    def gather(x):
        blocks = {0: x}
        for bit in reversed(bits):
            blocks.update({q | bit: swap(block, bit) for q, block in blocks.items()})
        return jnp.stack([blocks[q] for q in range(groups)])

    def combine(parts):
        for bit in bits:
            parts = [a + swap(b, bit) for a, b in zip(parts[::2], parts[1::2])]
        return parts[0]

    rows, width = tokens.shape
    depth, hidden = weight.shape
    per_owner, _, rank = adapter_down.shape
    i = lax.axis_index("dp")
    order = jnp.arange(groups, dtype=jnp.int32) ^ i
    owned, local_ids, live = block_facts(
        block_adapter, block_length, adapter_slot, order, rows, per_owner, i
    )
    down_sel = chosen(adapter_down, owned, local_ids)
    up_sel = chosen(adapter_up, owned, local_ids)
    all_tokens = lax.all_gather(lax.all_gather(tokens, "dp", axis=0), "tp", axis=2, tiled=True)
    all_tokens = lax.dynamic_slice_in_dim(all_tokens, i * depth, depth, 2)[order]
    all_tokens = all_tokens.reshape(groups * rows, depth)
    toks, cots = gather(tokens), gather(cotangent)
    tok_all, cot_all = toks.reshape(-1, width), cots.reshape(-1, hidden)
    down_mine = combine(down_sel)
    inner = jnp.stack([dot(toks[q], down_sel[q], (1, 0)) for q in range(groups)])
    inner_b = (lax.psum(inner, "tp") * live[:, :, None]).astype(jnp.bfloat16)
    back = jnp.stack([dot(cots[q], up_sel[q], (1, 1)) for q in range(groups)])
    back = lax.psum(back[order], ("tp", "dp"))[order] * (adapter_scale * live)[:, :, None]
    back_b = back.astype(jnp.bfloat16)
    one_hot = (local_ids[:, None] == jnp.arange(per_owner, dtype=jnp.int32)[None, :]) & owned[:, None]

    def spread(x):
        wide = jnp.where(one_hot[:, None, :, None], x[:, :, None, :], jnp.zeros((), x.dtype))
        return wide.reshape(groups * rows, per_owner * rank)

    inner_wide = spread(inner_b) * jnp.bfloat16(adapter_scale)
    total = dot(cot_all, weight, (1, 1)).reshape(groups, rows, 1, depth)[order]
    placed = jnp.zeros((groups, rows, groups, depth), jnp.float32)
    placed = lax.dynamic_update_slice_in_dim(placed, total, i, 2)
    placed = lax.psum_scatter(placed, "dp", scatter_dimension=0, tiled=False)
    placed = placed.reshape(rows, groups * depth)
    placed = lax.psum_scatter(placed, "tp", scatter_dimension=1, tiled=True)
    tokens_grad = (placed + dot(back_b[0], down_mine, (1, 1))).astype(jnp.bfloat16)
    part = dot(all_tokens, weight, (1, 0)) + dot(inner_wide, adapter_up.reshape(-1, hidden), (1, 0))
    projected = combine(list(part.reshape(groups, rows, hidden))).astype(jnp.bfloat16)
    up_grad = dot(inner_wide, cot_all, (0, 0)).reshape(per_owner, rank, hidden)
    down_grad = dot(spread(back_b), tok_all, (0, 0)).reshape(per_owner, rank, width)
    return projected, tokens_grad, jnp.swapaxes(down_grad, 1, 2), up_grad


def solution(mesh):
    placed = (
        P(("grp", "dp"), "tp"),
        P("dp", "tp"),
        P("dp", "tp", None),
        P("dp", None, "tp"),
        P(("grp", "dp"), "tp"),
        P("grp"),
        P("grp"),
        P(),
    )
    groups, shards = mesh.shape["dp"], mesh.shape["tp"]
    square = groups == shards == 4
    return jax.shard_map(
        local_square if square else functools.partial(local_any, groups),
        mesh=mesh,
        in_specs=placed,
        out_specs=(
            P(("grp", "dp"), "tp"),
            P(("grp", "dp"), "tp"),
            P(("grp", "dp"), "tp", None),
            P(("grp", "dp"), None, "tp"),
        ),
        check_vma=False,
    )
```

```python
import functools

import jax
import jax.numpy as jnp
from jax import lax
from jax.experimental import pallas as pl
from jax.experimental.pallas import tpu as pltpu
from jax.sharding import PartitionSpec as P

SEGMENT_BLOCK = 128

adapter_scale = 2.0
CORE, CHIP = 1, 2
VMEM = 48 * 1024 * 1024


def dot(a, b, contract):
    return lax.dot_general(a, b, ((contract[:1], contract[1:]), ((), ())), preferred_element_type=jnp.float32)


def after(x, *others):
    return lax.optimization_barrier((x,) + others)[0]


def cost(flops, moved, share=64):
    return pl.CostEstimate(flops=flops // share, bytes_accessed=moved // share, transcendentals=0)


def project(tokens, wide, weight, up_flat, start, stop, block):
    rows, depth = tokens.shape
    span = wide.shape[1]
    base = start // block

    def kernel(tok_ref, wide_ref, w_ref, up_ref, keep_ref, send_ref):
        total = dot(tok_ref[...], w_ref[...], (1, 0)) + dot(wide_ref[...], up_ref[...], (1, 0))
        keep_ref[...] = total[: rows // 2]
        send_ref[...] = total[rows // 2 :]

    return pl.pallas_call(
        kernel,
        grid=((stop - start) // block,),
        in_specs=[
            pl.BlockSpec(memory_space=pltpu.VMEM),
            pl.BlockSpec(memory_space=pltpu.VMEM),
            pl.BlockSpec((depth, block), lambda n: (0, n + base)),
            pl.BlockSpec((span, block), lambda n: (0, n + base)),
        ],
        out_specs=[pl.BlockSpec((rows // 2, block), lambda n: (0, n))] * 2,
        out_shape=[jax.ShapeDtypeStruct((rows // 2, stop - start), jnp.float32)] * 2,
        compiler_params=pltpu.CompilerParams(vmem_limit_bytes=VMEM),
        cost_estimate=cost(2 * rows * (depth + span) * (stop - start), 2 * (depth + span + 2 * rows) * (stop - start)),
        name="project",
    )(tokens, wide, weight, up_flat)


def return_grad(facts, first, second, weight, store, places, sent=()):
    rows, hidden = first.shape
    depth, rank = weight.shape[0], store.shape[1]
    groups = facts.shape[0] // 2
    block = 256
    half = places[0] // 2

    def kernel(facts_ref, a_ref, b_ref, w_ref, up_a_ref, up_b_ref, *refs):
        out_ref, sent_ref, rank_ref, rhs = refs[len(sent) :]
        n = pl.program_id(0)

        @pl.when(n == 0)
        def _():
            rhs[:rows] = a_ref[...]
            rhs[rows:] = b_ref[...]

        total = dot(w_ref[...], rhs[...], (1, 1)).T
        out_ref[...] = total
        sent_ref[...] = total.astype(first.dtype)

        @pl.when(n == pl.num_programs(0) - 1)
        def _():
            ranks = dot(jnp.concatenate([up_a_ref[0], up_b_ref[0]], axis=0), rhs[...], (1, 1))
            for at, place in enumerate(places):
                value = ranks[at * rank : (at + 1) * rank, at * rows : (at + 1) * rows]
                alive = lax.broadcasted_iota(jnp.int32, (rank, rows), 1) < facts_ref[groups + place]
                alive = alive & (facts_ref[place] >= 0)
                rank_ref[:, at * rows : (at + 1) * rows] = jnp.where(alive, value * adapter_scale, 0.0)

    def chosen_slot(place):
        return lambda n, facts_ref: (jnp.maximum(facts_ref[place], 0), 0, 0)

    return pl.pallas_call(
        kernel,
        grid_spec=pltpu.PrefetchScalarGridSpec(
            num_scalar_prefetch=1,
            grid=(depth // block,),
            in_specs=[
                pl.BlockSpec(memory_space=pltpu.VMEM),
                pl.BlockSpec(memory_space=pltpu.VMEM),
                pl.BlockSpec((block, hidden), lambda n, facts_ref: (n, 0)),
                *[pl.BlockSpec((1, rank, hidden), chosen_slot(place)) for place in places],
                *[pl.BlockSpec(memory_space=pl.ANY)] * len(sent),
            ],
            out_specs=[
                pl.BlockSpec((2 * rows, block), lambda n, facts_ref: (0, n)),
                pl.BlockSpec((2 * rows, block), lambda n, facts_ref: (half, n)),
                pl.BlockSpec((rank, 2 * rows), lambda n, facts_ref: (0, 0)),
            ],
            scratch_shapes=[pltpu.VMEM((2 * rows, hidden), first.dtype)],
        ),
        out_shape=[
            jax.ShapeDtypeStruct((2 * rows, depth), jnp.float32),
            jax.ShapeDtypeStruct((4 * rows, depth), first.dtype),
            jax.ShapeDtypeStruct((rank, 2 * rows), jnp.float32),
        ],
        input_output_aliases={6: 1} if sent else {},
        compiler_params=pltpu.CompilerParams(vmem_limit_bytes=VMEM),
        cost_estimate=cost(4 * rows * hidden * depth, 2 * hidden * (depth + 2 * rows)),
        name="return_grad",
    )(facts, first, second, weight, store, store, *sent)


def rank_inner(facts, flat, blocks, rank):
    span, width = flat.shape
    arrays, places = [x for x, _ in blocks], [n for _, n in blocks]
    groups = len(blocks)
    rows = arrays[0].shape[0] // 2
    slots = span // rank

    def kernel(facts_ref, flat_ref, *refs):
        out_ref = refs[-1]
        total = dot(flat_ref[...], jnp.concatenate([r[...] for r in refs[:-1]], axis=0), (1, 1))
        for q in range(groups):
            acc = jnp.zeros((rank, rows), jnp.float32)
            for s in range(slots):
                acc = jnp.where(facts_ref[q] == s, total[s * rank : (s + 1) * rank, q * rows : (q + 1) * rows], acc)
            alive = lax.broadcasted_iota(jnp.int32, (rank, rows), 1) < facts_ref[groups + q]
            out_ref[:, q * rows : (q + 1) * rows] = jnp.where(alive, acc, 0.0)

    return pl.pallas_call(
        kernel,
        grid=(1,),
        in_specs=[pl.BlockSpec(memory_space=pltpu.SMEM), pl.BlockSpec((span, width), lambda n: (0, 0))]
        + [pl.BlockSpec((rows, width), lambda n, place=place: (place, 0)) for place in places],
        out_specs=pl.BlockSpec((rank, groups * rows), lambda n: (0, 0)),
        out_shape=jax.ShapeDtypeStruct((rank, groups * rows), jnp.float32),
        compiler_params=pltpu.CompilerParams(vmem_limit_bytes=VMEM),
        cost_estimate=cost(2 * span * groups * rows * width, 2 * width * (span + groups * rows)),
        name="rank_inner",
    )(facts, flat, *arrays)


def spread(facts, here, there, slots, scale):
    rank, tokens = here.shape
    groups = facts.shape[0] // 2
    rows = tokens // groups
    values = [here] if there is None else [here, there]

    def kernel(facts_ref, *refs):
        wide_ref, turned_ref, sum_ref = refs[-3:]
        x = sum(r[...] for r in refs[:-3]).astype(jnp.bfloat16)
        sum_ref[...] = x
        x = x.astype(jnp.float32) * scale
        for q in range(groups):
            part = x[:, q * rows : (q + 1) * rows]
            for s in range(slots):
                value = jnp.where(facts_ref[q] == s, part, 0.0)
                wide_ref[s * rank : (s + 1) * rank, q * rows : (q + 1) * rows] = value.astype(jnp.bfloat16)
        for n, q in enumerate((0, 2, 1, 3)):
            part = wide_ref[:, q * rows : (q + 1) * rows]
            turned_ref[n * rows : (n + 1) * rows] = part.astype(jnp.float32).T.astype(jnp.bfloat16)

    return pl.pallas_call(
        kernel,
        in_specs=[pl.BlockSpec(memory_space=pltpu.SMEM)] + [pl.BlockSpec(memory_space=pltpu.VMEM)] * len(values),
        out_specs=[pl.BlockSpec(memory_space=pltpu.VMEM)] * 3,
        out_shape=[
            jax.ShapeDtypeStruct((slots * rank, tokens), jnp.bfloat16),
            jax.ShapeDtypeStruct((tokens, slots * rank), jnp.bfloat16),
            jax.ShapeDtypeStruct((rank, tokens), jnp.bfloat16),
        ],
        compiler_params=pltpu.CompilerParams(vmem_limit_bytes=VMEM),
        cost_estimate=cost(0, 8 * slots * rank * tokens),
        name="spread",
    )(facts, *values)


def slot_grad(wide_t, blocks, block):
    span, tokens = wide_t.shape
    groups = len(blocks)
    rows = tokens // groups
    columns = sum(x.shape[1] for x in blocks[0][0])
    arrays, specs = [], []
    for parts, place in blocks:
        first = 0
        for x in parts:
            count = x.shape[1] // block
            specs.append(
                pl.BlockSpec((rows, block), lambda n, a=first, b=count - 1, place=place: (place, jnp.clip(n - a, 0, b)))
            )
            arrays.append(x)
            first += count

    def kernel(wide_ref, *refs):
        n = pl.program_id(0)
        values, at = [], 0
        for parts, _ in blocks:
            value, first = refs[at][...], parts[0].shape[1] // block
            for more, x in enumerate(parts[1:], 1):
                value = jnp.where(n >= first, refs[at + more][...], value)
                first += x.shape[1] // block
            values.append(value)
            at += len(parts)
        refs[-1][...] = dot(wide_ref[...], jnp.concatenate(values, axis=0), (1, 0))

    return pl.pallas_call(
        kernel,
        grid=(columns // block,),
        in_specs=[pl.BlockSpec((span, tokens), lambda n: (0, 0))] + specs,
        out_specs=pl.BlockSpec((span, block), lambda n: (0, n)),
        out_shape=jax.ShapeDtypeStruct((span, columns), jnp.float32),
        compiler_params=pltpu.CompilerParams(vmem_limit_bytes=VMEM),
        cost_estimate=cost(2 * span * tokens * columns, (4 * span + 2 * tokens) * columns, 1),
        name="slot_grad",
    )(wide_t, *arrays)


def block_facts(block_adapter, block_length, adapter_slot, order, rows, per_owner, i):
    match = block_adapter[:, None] == jnp.arange(adapter_slot.shape[0], dtype=jnp.int32)[None, :]
    slots = jnp.sum(jnp.where(match, adapter_slot[None, :], 0), axis=1)[order]
    lengths = block_length[order]
    owned = slots // per_owner == i
    local_ids = slots % per_owner
    groups = order.shape[0]
    live = (lax.broadcasted_iota(jnp.int32, (groups, rows), 1) < lengths[:, None]).astype(jnp.float32)
    return owned, local_ids, live


def chosen(store, owned, local_ids):
    zero = jnp.zeros((), store.dtype)
    return [
        jnp.where(owned[q], lax.dynamic_index_in_dim(store, local_ids[q], 0, False), zero)
        for q in range(owned.shape[0])
    ]


def choose(block_adapter, block_length, adapter_slot, here, store):
    slots, rank, width = store.shape
    groups = block_adapter.shape[0]

    def block_of(step):
        return jnp.clip(jnp.where(step < 2, 2 * step + 1, 6 - 2 * step), 0, groups - 1)

    def slot_of(q, adapter_ref, slot_ref, here_ref):
        return slot_ref[adapter_ref[q ^ here_ref[0]]] - here_ref[0] * slots

    def kernel(adapter_ref, length_ref, slot_ref, here_ref, store_ref, near_ref, rest_ref, facts_ref):
        step = pl.program_id(0)

        @pl.when(step == 0)
        def _():
            for q in range(groups):
                at = slot_of(q, adapter_ref, slot_ref, here_ref)
                facts_ref[q] = jnp.where((at >= 0) & (at < slots), at, -1)
                facts_ref[groups + q] = length_ref[q ^ here_ref[0]]
            facts_ref[2 * groups] = here_ref[1]

        at = slot_of(block_of(step), adapter_ref, slot_ref, here_ref)
        value = store_ref[0] * ((at >= 0) & (at < slots)).astype(store_ref.dtype)

        @pl.when(step < 2)
        def _():
            near_ref[...] = value

        @pl.when(step >= 2)
        def _():
            rest_ref[...] = value

    def stored(step, adapter_ref, length_ref, slot_ref, here_ref):
        at = slot_of(block_of(step), adapter_ref, slot_ref, here_ref)
        return jnp.clip(at, 0, slots - 1), 0, 0

    return pl.pallas_call(
        kernel,
        grid_spec=pltpu.PrefetchScalarGridSpec(
            num_scalar_prefetch=4,
            grid=(groups,),
            in_specs=[pl.BlockSpec((1, rank, width), stored)],
            out_specs=[
                pl.BlockSpec((rank, width), lambda step, *refs: (jnp.minimum(step, 1), 0)),
                pl.BlockSpec((rank, width), lambda step, *refs: (jnp.maximum(step - 2, 0), 0)),
                pl.BlockSpec(memory_space=pltpu.SMEM),
            ],
        ),
        out_shape=[jax.ShapeDtypeStruct((2 * rank, width), store.dtype)] * 2
        + [jax.ShapeDtypeStruct((2 * groups + 1,), jnp.int32)],
        compiler_params=pltpu.CompilerParams(vmem_limit_bytes=VMEM),
        cost_estimate=cost(0, 8 * rank * width * groups),
        name="choose",
    )(block_adapter, block_length, adapter_slot, here, store)


def local_square(
    tokens, weight, adapter_down, adapter_up, cotangent, block_adapter, block_length, adapter_slot
):
    groups = shards = 4
    rows, width = tokens.shape
    depth, hidden = weight.shape
    per_owner, _, rank = adapter_down.shape
    span = per_owner * rank
    b16 = jnp.bfloat16
    i, j = lax.axis_index("dp"), lax.axis_index("tp")

    def swap(x, bit):
        return lax.ppermute(x, "dp", [(d, d ^ bit) for d in range(groups)])

    def along(x, bit):
        return lax.ppermute(x, "tp", [(z, z ^ bit) for z in range(shards)])

    place = [(c * groups + r, (r ^ c) * groups + c) for r in range(groups) for c in range(shards)]
    hop = [(d * groups + d, (d ^ 2) * groups + d) for d in range(groups)]
    hops = [(z * groups + d, (z ^ 1) * groups + d) for d in range(groups) for z in (d, d ^ 2)]

    def share(x, got, bit):
        return x + jnp.concatenate([got[:, (q ^ bit) * rows : ((q ^ bit) + 1) * rows] for q in range(groups)], axis=1)

    def both(x, pairs):
        return lax.ppermute(x, ("tp", "dp"), pairs)

    tok_x = swap(tokens, CHIP)
    cot_c = swap(cotangent, CORE)
    away = i ^ j
    here = jnp.stack([i, away]).astype(jnp.int32)
    down_t = jnp.swapaxes(adapter_down, 1, 2)
    near, rest, facts = choose(block_adapter, block_length, adapter_slot, here, down_t)
    up_flat = adapter_up.reshape(span, hidden)

    near = swap(near, CORE)
    down_x = swap(rest[:rank] + near[rank:], CHIP)
    even = jnp.concatenate([tokens, after(tok_x, facts, down_x)], axis=0)
    odd = swap(even, CORE)
    even_far = both(even, hop)
    cot_x = swap(after(cotangent, even), CHIP)
    grad01, parts, back01 = return_grad(facts, after(cotangent, even), cot_c, weight, adapter_up, (0, 1))
    toks = [(even, 0), (odd, 0), (even, 1), (odd, 1)]
    inner = rank_inner(facts, down_t.reshape(span, width), [(after(x, grad01), n) for x, n in toks], rank)
    inner_near = along(inner, 1)
    odd_far = both(after(odd, inner), hop)
    even_mid = jnp.where(away == 0, even, after(even_far, inner))
    even_all = both(even_mid, hops)
    cot_xc = swap(after(cot_x, even_mid), CORE)
    down_mine = both(rest[rank:] + near[:rank] + after(down_x, inner), place)
    inner = after(inner, cot_x) + inner_near
    inner_far = along(inner, 2)
    odd_mid = jnp.where(away == 0, odd, after(odd_far, inner))
    odd_all = both(odd_mid, hops)
    grad23, parts, back23 = return_grad(
        facts, after(cot_x, odd_mid, even_all), cot_xc, weight, adapter_up, (2, 3), (parts,)
    )
    back = jnp.concatenate([back01, back23], axis=1)
    back_near = along(back, 1)
    all_even = jnp.where(away == 0, even, jnp.where(away == 2, even_far, after(even_all, grad23, down_mine)))
    all_odd = jnp.where(away == 0, odd, jnp.where(away == 2, odd_far, after(odd_all, all_even)))
    all_tokens = jnp.concatenate([all_even, all_odd], axis=0)
    inner_wide, inner_rows, _ = spread(facts, after(inner, all_tokens), inner_far, per_owner, adapter_scale)
    cots = [([x], 0) for x in (cotangent, cot_c, cot_x, cot_xc)]
    up_wide = slot_grad(after(inner_wide, inner_rows), cots, hidden // 4)
    back = after(back, up_wide) + back_near
    back_wide, _, back_b = spread(facts, back, along(back, 2), per_owner, 1.0)
    parts = lax.all_to_all(after(parts, back_b).reshape(shards, rows, depth), "tp", 0, 0, tiled=True)
    back_b = share(back_b, swap(back_b, CORE), CORE)

    def grad_block(q):
        low, high = [lax.dynamic_slice_in_dim(x, (q & 1) * rows, rows, 0) for x in (grad01, grad23)]
        return jnp.where(q < 2, low, high)

    block = 512
    steps = hidden // block
    pieces = 4
    edges = [(-(-steps * n // pieces)) * block for n in range(pieces + 1)]
    kept, sent, got_c, got_x, done = [], [], [], [], []

    def make(n, *points):
        keep, send = project(after(all_tokens, *points), inner_rows, weight, up_flat, edges[n], edges[n + 1], block)
        kept.append(keep)
        got_c.append(swap(send, CORE))
        return keep

    def cross(n, *points):
        summed = (after(kept[n], *points)[rows:] + got_c[n][rows:]).astype(b16)
        got_x.append(swap(summed, CHIP))
        return summed

    def finish(n, *points):
        own = after(kept[n], *points)[:rows] + got_c[n][:rows] + got_x[n].astype(jnp.float32)
        done.append(own.astype(b16))
        return done[-1]

    point = make(0, back_b)
    back_b = share(after(back_b, point), swap(back_b, CHIP), CHIP)
    point = make(1, point)
    point = cross(0, point)
    point = make(2, point, back_b)
    point = finish(0, point)
    point = cross(1, point)
    point = make(3, point)
    point = finish(1, point)
    point = cross(2, point)
    down_wide = slot_grad(after(back_wide, point), [([x], n) for x, n in toks], width // 2)
    back_mine = lax.dynamic_slice_in_dim(back_b, j * rows, rows, 1)
    total = grad_block(j)
    for m in range(1, shards):
        total = total + lax.dynamic_index_in_dim(after(parts, down_wide), j ^ m, 0, False).astype(jnp.float32)
    total = (total + dot(back_mine, down_mine, (0, 0))).astype(b16)
    tokens_grad = both(total, [(b, a) for a, b in place])
    point = cross(3, total)
    point = finish(2, point)
    finish(3, point)
    projected = jnp.concatenate(done, axis=1)
    up_grad = up_wide.reshape(per_owner, rank, hidden)
    down_grad = jnp.swapaxes(down_wide.reshape(per_owner, rank, width), 1, 2)
    return projected, tokens_grad, down_grad, up_grad


def local_any(
    groups, tokens, weight, adapter_down, adapter_up, cotangent, block_adapter, block_length, adapter_slot
):
    bits = [1 << n for n in range((groups - 1).bit_length())]

    def swap(x, bit):
        return lax.ppermute(x, "dp", [(d, d ^ bit) for d in range(groups)])

    def gather(x):
        blocks = {0: x}
        for bit in reversed(bits):
            blocks.update({q | bit: swap(block, bit) for q, block in blocks.items()})
        return jnp.stack([blocks[q] for q in range(groups)])

    def combine(parts):
        for bit in bits:
            parts = [a + swap(b, bit) for a, b in zip(parts[::2], parts[1::2])]
        return parts[0]

    rows, width = tokens.shape
    depth, hidden = weight.shape
    per_owner, _, rank = adapter_down.shape
    i = lax.axis_index("dp")
    order = jnp.arange(groups, dtype=jnp.int32) ^ i
    owned, local_ids, live = block_facts(
        block_adapter, block_length, adapter_slot, order, rows, per_owner, i
    )
    down_sel = chosen(adapter_down, owned, local_ids)
    up_sel = chosen(adapter_up, owned, local_ids)
    all_tokens = lax.all_gather(lax.all_gather(tokens, "dp", axis=0), "tp", axis=2, tiled=True)
    all_tokens = lax.dynamic_slice_in_dim(all_tokens, i * depth, depth, 2)[order]
    all_tokens = all_tokens.reshape(groups * rows, depth)
    toks, cots = gather(tokens), gather(cotangent)
    tok_all, cot_all = toks.reshape(-1, width), cots.reshape(-1, hidden)
    down_mine = combine(down_sel)
    inner = jnp.stack([dot(toks[q], down_sel[q], (1, 0)) for q in range(groups)])
    inner_b = (lax.psum(inner, "tp") * live[:, :, None]).astype(jnp.bfloat16)
    back = jnp.stack([dot(cots[q], up_sel[q], (1, 1)) for q in range(groups)])
    back = lax.psum(back[order], ("tp", "dp"))[order] * (adapter_scale * live)[:, :, None]
    back_b = back.astype(jnp.bfloat16)
    one_hot = (local_ids[:, None] == jnp.arange(per_owner, dtype=jnp.int32)[None, :]) & owned[:, None]

    def spread(x):
        wide = jnp.where(one_hot[:, None, :, None], x[:, :, None, :], jnp.zeros((), x.dtype))
        return wide.reshape(groups * rows, per_owner * rank)

    inner_wide = spread(inner_b) * jnp.bfloat16(adapter_scale)
    total = dot(cot_all, weight, (1, 1)).reshape(groups, rows, 1, depth)[order]
    placed = jnp.zeros((groups, rows, groups, depth), jnp.float32)
    placed = lax.dynamic_update_slice_in_dim(placed, total, i, 2)
    placed = lax.psum_scatter(placed, "dp", scatter_dimension=0, tiled=False)
    placed = placed.reshape(rows, groups * depth)
    placed = lax.psum_scatter(placed, "tp", scatter_dimension=1, tiled=True)
    tokens_grad = (placed + dot(back_b[0], down_mine, (1, 1))).astype(jnp.bfloat16)
    part = dot(all_tokens, weight, (1, 0)) + dot(inner_wide, adapter_up.reshape(-1, hidden), (1, 0))
    projected = combine(list(part.reshape(groups, rows, hidden))).astype(jnp.bfloat16)
    up_grad = dot(inner_wide, cot_all, (0, 0)).reshape(per_owner, rank, hidden)
    down_grad = dot(spread(back_b), tok_all, (0, 0)).reshape(per_owner, rank, width)
    return projected, tokens_grad, jnp.swapaxes(down_grad, 1, 2), up_grad


def solution(mesh):
    placed = (
        P(("grp", "dp"), "tp"),
        P("dp", "tp"),
        P("dp", "tp", None),
        P("dp", None, "tp"),
        P(("grp", "dp"), "tp"),
        P("grp"),
        P("grp"),
        P(),
    )
    groups, shards = mesh.shape["dp"], mesh.shape["tp"]
    square = groups == shards == 4
    return jax.shard_map(
        local_square if square else functools.partial(local_any, groups),
        mesh=mesh,
        in_specs=placed,
        out_specs=(
            P(("grp", "dp"), "tp"),
            P(("grp", "dp"), "tp"),
            P(("grp", "dp"), "tp", None),
            P(("grp", "dp"), None, "tp"),
        ),
        check_vma=False,
    )
```

```python
import functools

import jax
import jax.numpy as jnp
from jax import lax
from jax.experimental import pallas as pl
from jax.experimental.pallas import tpu as pltpu
from jax.sharding import PartitionSpec as P

SEGMENT_BLOCK = 128

adapter_scale = 2.0
CORE, CHIP = 1, 2
VMEM = 48 * 1024 * 1024


def dot(a, b, contract):
    return lax.dot_general(a, b, ((contract[:1], contract[1:]), ((), ())), preferred_element_type=jnp.float32)


def after(x, *others):
    return lax.optimization_barrier((x,) + others)[0]


def cost(flops, moved, share=64):
    return pl.CostEstimate(flops=flops // share, bytes_accessed=moved // share, transcendentals=0)


def project(tokens, wide, weight, up_flat, start, stop, block):
    rows, depth = tokens.shape
    span = wide.shape[1]
    base = start // block

    def kernel(tok_ref, wide_ref, w_ref, up_ref, keep_ref, send_ref):
        total = dot(tok_ref[...], w_ref[...], (1, 0)) + dot(wide_ref[...], up_ref[...], (1, 0))
        keep_ref[...] = total[: rows // 2]
        send_ref[...] = total[rows // 2 :]

    return pl.pallas_call(
        kernel,
        grid=((stop - start) // block,),
        in_specs=[
            pl.BlockSpec(memory_space=pltpu.VMEM),
            pl.BlockSpec(memory_space=pltpu.VMEM),
            pl.BlockSpec((depth, block), lambda n: (0, n + base)),
            pl.BlockSpec((span, block), lambda n: (0, n + base)),
        ],
        out_specs=[pl.BlockSpec((rows // 2, block), lambda n: (0, n))] * 2,
        out_shape=[jax.ShapeDtypeStruct((rows // 2, stop - start), jnp.float32)] * 2,
        compiler_params=pltpu.CompilerParams(vmem_limit_bytes=VMEM),
        cost_estimate=cost(2 * rows * (depth + span) * (stop - start), 2 * (depth + span + 2 * rows) * (stop - start)),
        name="project",
    )(tokens, wide, weight, up_flat)


def return_grad(facts, first, second, weight, store, places, sent=()):
    rows, hidden = first.shape
    depth, rank = weight.shape[0], store.shape[1]
    groups = facts.shape[0] // 2
    block = 256
    half = places[0] // 2

    def kernel(facts_ref, a_ref, b_ref, w_ref, up_a_ref, up_b_ref, *refs):
        out_ref, sent_ref, rank_ref, rhs = refs[len(sent) :]
        n = pl.program_id(0)

        @pl.when(n == 0)
        def _():
            rhs[:rows] = a_ref[...]
            rhs[rows:] = b_ref[...]

        total = dot(w_ref[...], rhs[...], (1, 1)).T
        out_ref[...] = total
        sent_ref[...] = total.astype(first.dtype)

        @pl.when(n == pl.num_programs(0) - 1)
        def _():
            ranks = dot(jnp.concatenate([up_a_ref[0], up_b_ref[0]], axis=0), rhs[...], (1, 1))
            for at, place in enumerate(places):
                value = ranks[at * rank : (at + 1) * rank, at * rows : (at + 1) * rows]
                alive = lax.broadcasted_iota(jnp.int32, (rank, rows), 1) < facts_ref[groups + place]
                alive = alive & (facts_ref[place] >= 0)
                rank_ref[:, at * rows : (at + 1) * rows] = jnp.where(alive, value * adapter_scale, 0.0)

    def chosen_slot(place):
        return lambda n, facts_ref: (jnp.maximum(facts_ref[place], 0), 0, 0)

    return pl.pallas_call(
        kernel,
        grid_spec=pltpu.PrefetchScalarGridSpec(
            num_scalar_prefetch=1,
            grid=(depth // block,),
            in_specs=[
                pl.BlockSpec(memory_space=pltpu.VMEM),
                pl.BlockSpec(memory_space=pltpu.VMEM),
                pl.BlockSpec((block, hidden), lambda n, facts_ref: (n, 0)),
                *[pl.BlockSpec((1, rank, hidden), chosen_slot(place)) for place in places],
                *[pl.BlockSpec(memory_space=pl.ANY)] * len(sent),
            ],
            out_specs=[
                pl.BlockSpec((2 * rows, block), lambda n, facts_ref: (0, n)),
                pl.BlockSpec((2 * rows, block), lambda n, facts_ref: (half, n)),
                pl.BlockSpec((rank, 2 * rows), lambda n, facts_ref: (0, 0)),
            ],
            scratch_shapes=[pltpu.VMEM((2 * rows, hidden), first.dtype)],
        ),
        out_shape=[
            jax.ShapeDtypeStruct((2 * rows, depth), jnp.float32),
            jax.ShapeDtypeStruct((4 * rows, depth), first.dtype),
            jax.ShapeDtypeStruct((rank, 2 * rows), jnp.float32),
        ],
        input_output_aliases={6: 1} if sent else {},
        compiler_params=pltpu.CompilerParams(vmem_limit_bytes=VMEM),
        cost_estimate=cost(4 * rows * hidden * depth, 2 * hidden * (depth + 2 * rows)),
        name="return_grad",
    )(facts, first, second, weight, store, store, *sent)


def rank_inner(facts, flat, blocks, rank):
    span, width = flat.shape
    arrays, places = [x for x, _ in blocks], [n for _, n in blocks]
    groups = len(blocks)
    rows = arrays[0].shape[0] // 2
    slots = span // rank

    def kernel(facts_ref, flat_ref, *refs):
        out_ref = refs[-1]
        total = dot(flat_ref[...], jnp.concatenate([r[...] for r in refs[:-1]], axis=0), (1, 1))
        for q in range(groups):
            acc = jnp.zeros((rank, rows), jnp.float32)
            for s in range(slots):
                acc = jnp.where(facts_ref[q] == s, total[s * rank : (s + 1) * rank, q * rows : (q + 1) * rows], acc)
            alive = lax.broadcasted_iota(jnp.int32, (rank, rows), 1) < facts_ref[groups + q]
            out_ref[:, q * rows : (q + 1) * rows] = jnp.where(alive, acc, 0.0)

    return pl.pallas_call(
        kernel,
        grid=(1,),
        in_specs=[pl.BlockSpec(memory_space=pltpu.SMEM), pl.BlockSpec((span, width), lambda n: (0, 0))]
        + [pl.BlockSpec((rows, width), lambda n, place=place: (place, 0)) for place in places],
        out_specs=pl.BlockSpec((rank, groups * rows), lambda n: (0, 0)),
        out_shape=jax.ShapeDtypeStruct((rank, groups * rows), jnp.float32),
        compiler_params=pltpu.CompilerParams(vmem_limit_bytes=VMEM),
        cost_estimate=cost(2 * span * groups * rows * width, 2 * width * (span + groups * rows)),
        name="rank_inner",
    )(facts, flat, *arrays)


def spread(facts, here, there, slots, scale):
    rank, tokens = here.shape
    groups = facts.shape[0] // 2
    rows = tokens // groups
    values = [here] if there is None else [here, there]

    def kernel(facts_ref, *refs):
        wide_ref, turned_ref, sum_ref = refs[-3:]
        x = sum(r[...] for r in refs[:-3]).astype(jnp.bfloat16)
        sum_ref[...] = x
        x = x.astype(jnp.float32) * scale
        for q in range(groups):
            part = x[:, q * rows : (q + 1) * rows]
            for s in range(slots):
                value = jnp.where(facts_ref[q] == s, part, 0.0)
                wide_ref[s * rank : (s + 1) * rank, q * rows : (q + 1) * rows] = value.astype(jnp.bfloat16)
        for n, q in enumerate((0, 2, 1, 3)):
            part = wide_ref[:, q * rows : (q + 1) * rows]
            turned_ref[n * rows : (n + 1) * rows] = part.astype(jnp.float32).T.astype(jnp.bfloat16)

    return pl.pallas_call(
        kernel,
        in_specs=[pl.BlockSpec(memory_space=pltpu.SMEM)] + [pl.BlockSpec(memory_space=pltpu.VMEM)] * len(values),
        out_specs=[pl.BlockSpec(memory_space=pltpu.VMEM)] * 3,
        out_shape=[
            jax.ShapeDtypeStruct((slots * rank, tokens), jnp.bfloat16),
            jax.ShapeDtypeStruct((tokens, slots * rank), jnp.bfloat16),
            jax.ShapeDtypeStruct((rank, tokens), jnp.bfloat16),
        ],
        compiler_params=pltpu.CompilerParams(vmem_limit_bytes=VMEM),
        cost_estimate=cost(0, 8 * slots * rank * tokens),
        name="spread",
    )(facts, *values)


def slot_grad(wide_t, blocks, block):
    span, tokens = wide_t.shape
    groups = len(blocks)
    rows = tokens // groups
    columns = sum(x.shape[1] for x in blocks[0][0])
    arrays, specs = [], []
    for parts, place in blocks:
        first = 0
        for x in parts:
            count = x.shape[1] // block
            specs.append(
                pl.BlockSpec((rows, block), lambda n, a=first, b=count - 1, place=place: (place, jnp.clip(n - a, 0, b)))
            )
            arrays.append(x)
            first += count

    def kernel(wide_ref, *refs):
        n = pl.program_id(0)
        values, at = [], 0
        for parts, _ in blocks:
            value, first = refs[at][...], parts[0].shape[1] // block
            for more, x in enumerate(parts[1:], 1):
                value = jnp.where(n >= first, refs[at + more][...], value)
                first += x.shape[1] // block
            values.append(value)
            at += len(parts)
        refs[-1][...] = dot(wide_ref[...], jnp.concatenate(values, axis=0), (1, 0))

    return pl.pallas_call(
        kernel,
        grid=(columns // block,),
        in_specs=[pl.BlockSpec((span, tokens), lambda n: (0, 0))] + specs,
        out_specs=pl.BlockSpec((span, block), lambda n: (0, n)),
        out_shape=jax.ShapeDtypeStruct((span, columns), jnp.float32),
        compiler_params=pltpu.CompilerParams(vmem_limit_bytes=VMEM),
        cost_estimate=cost(2 * span * tokens * columns, (4 * span + 2 * tokens) * columns, 1),
        name="slot_grad",
    )(wide_t, *arrays)


def block_facts(block_adapter, block_length, adapter_slot, order, rows, per_owner, i):
    match = block_adapter[:, None] == jnp.arange(adapter_slot.shape[0], dtype=jnp.int32)[None, :]
    slots = jnp.sum(jnp.where(match, adapter_slot[None, :], 0), axis=1)[order]
    lengths = block_length[order]
    owned = slots // per_owner == i
    local_ids = slots % per_owner
    groups = order.shape[0]
    live = (lax.broadcasted_iota(jnp.int32, (groups, rows), 1) < lengths[:, None]).astype(jnp.float32)
    return owned, local_ids, live


def chosen(store, owned, local_ids):
    zero = jnp.zeros((), store.dtype)
    return [
        jnp.where(owned[q], lax.dynamic_index_in_dim(store, local_ids[q], 0, False), zero)
        for q in range(owned.shape[0])
    ]


def choose(block_adapter, block_length, adapter_slot, here, store):
    slots, rank, width = store.shape
    groups = block_adapter.shape[0]

    def block_of(step):
        return jnp.clip(jnp.where(step < 2, 2 * step + 1, 6 - 2 * step), 0, groups - 1)

    def slot_of(q, adapter_ref, slot_ref, here_ref):
        return slot_ref[adapter_ref[q ^ here_ref[0]]] - here_ref[0] * slots

    def kernel(adapter_ref, length_ref, slot_ref, here_ref, store_ref, near_ref, rest_ref, facts_ref):
        step = pl.program_id(0)

        @pl.when(step == 0)
        def _():
            for q in range(groups):
                at = slot_of(q, adapter_ref, slot_ref, here_ref)
                facts_ref[q] = jnp.where((at >= 0) & (at < slots), at, -1)
                facts_ref[groups + q] = length_ref[q ^ here_ref[0]]
            facts_ref[2 * groups] = here_ref[1]

        at = slot_of(block_of(step), adapter_ref, slot_ref, here_ref)
        value = store_ref[0] * ((at >= 0) & (at < slots)).astype(store_ref.dtype)

        @pl.when(step < 2)
        def _():
            near_ref[...] = value

        @pl.when(step >= 2)
        def _():
            rest_ref[...] = value

    def stored(step, adapter_ref, length_ref, slot_ref, here_ref):
        at = slot_of(block_of(step), adapter_ref, slot_ref, here_ref)
        return jnp.clip(at, 0, slots - 1), 0, 0

    return pl.pallas_call(
        kernel,
        grid_spec=pltpu.PrefetchScalarGridSpec(
            num_scalar_prefetch=4,
            grid=(groups,),
            in_specs=[pl.BlockSpec((1, rank, width), stored)],
            out_specs=[
                pl.BlockSpec((rank, width), lambda step, *refs: (jnp.minimum(step, 1), 0)),
                pl.BlockSpec((rank, width), lambda step, *refs: (jnp.maximum(step - 2, 0), 0)),
                pl.BlockSpec(memory_space=pltpu.SMEM),
            ],
        ),
        out_shape=[jax.ShapeDtypeStruct((2 * rank, width), store.dtype)] * 2
        + [jax.ShapeDtypeStruct((2 * groups + 1,), jnp.int32)],
        compiler_params=pltpu.CompilerParams(vmem_limit_bytes=VMEM),
        cost_estimate=cost(0, 8 * rank * width * groups),
        name="choose",
    )(block_adapter, block_length, adapter_slot, here, store)


def local_square(
    tokens, weight, adapter_down, adapter_up, cotangent, block_adapter, block_length, adapter_slot
):
    groups = shards = 4
    rows, width = tokens.shape
    depth, hidden = weight.shape
    per_owner, _, rank = adapter_down.shape
    span = per_owner * rank
    b16 = jnp.bfloat16
    i, j = lax.axis_index("dp"), lax.axis_index("tp")

    def swap(x, bit):
        return lax.ppermute(x, "dp", [(d, d ^ bit) for d in range(groups)])

    def along(x, bit):
        return lax.ppermute(x, "tp", [(z, z ^ bit) for z in range(shards)])

    place = [(c * groups + r, (r ^ c) * groups + c) for r in range(groups) for c in range(shards)]
    hop = [(d * groups + d, (d ^ 2) * groups + d) for d in range(groups)]
    hops = [(z * groups + d, (z ^ 1) * groups + d) for d in range(groups) for z in (d, d ^ 2)]

    def share(x, got, bit):
        return x + jnp.concatenate([got[:, (q ^ bit) * rows : ((q ^ bit) + 1) * rows] for q in range(groups)], axis=1)

    def both(x, pairs):
        return lax.ppermute(x, ("tp", "dp"), pairs)

    tok_x = swap(tokens, CHIP)
    cot_c = swap(cotangent, CORE)
    away = i ^ j
    here = jnp.stack([i, away]).astype(jnp.int32)
    down_t = jnp.swapaxes(adapter_down, 1, 2)
    near, rest, facts = choose(block_adapter, block_length, adapter_slot, here, down_t)
    up_flat = adapter_up.reshape(span, hidden)

    near = swap(near, CORE)
    down_x = swap(rest[:rank] + near[rank:], CHIP)
    even = jnp.concatenate([tokens, after(tok_x, facts)], axis=0)
    odd = swap(even, CORE)
    even_far = both(even, hop)
    cot_x = swap(after(cotangent, even), CHIP)
    grad01, parts, back01 = return_grad(facts, after(cotangent, odd), cot_c, weight, adapter_up, (0, 1))
    toks = [(even, 0), (odd, 0), (even, 1), (odd, 1)]
    inner = rank_inner(facts, down_t.reshape(span, width), [(after(x, grad01), n) for x, n in toks], rank)
    inner_near = along(inner, 1)
    odd_far = both(odd, hop)
    even_mid = jnp.where(away == 0, even, after(even_far, inner))
    even_all = both(even_mid, hops)
    odd_mid = jnp.where(away == 0, odd, after(odd_far, even_mid))
    odd_all = both(odd_mid, hops)
    inner = after(inner, even_mid) + inner_near
    cot_xc = swap(after(cot_x, odd_mid, inner), CORE)
    down_mine = both(rest[rank:] + near[:rank] + after(down_x, inner), place)
    inner_far = along(inner, 2)
    grad23, parts, back23 = return_grad(
        facts, after(cot_x, inner, even_all), cot_xc, weight, adapter_up, (2, 3), (parts,)
    )
    back = jnp.concatenate([back01, back23], axis=1)
    back_near = along(back, 1)
    all_even = jnp.where(away == 0, even, jnp.where(away == 2, even_far, after(even_all, grad23, down_mine)))
    all_odd = jnp.where(away == 0, odd, jnp.where(away == 2, odd_far, after(odd_all, all_even)))
    all_tokens = jnp.concatenate([all_even, all_odd], axis=0)
    inner_wide, inner_rows, _ = spread(facts, after(inner, all_tokens), inner_far, per_owner, adapter_scale)
    cots = [([x], 0) for x in (cotangent, cot_c, cot_x, cot_xc)]
    up_wide = slot_grad(after(inner_wide, inner_rows), cots, hidden // 4)
    back = after(back, up_wide) + back_near
    back_wide, _, back_b = spread(facts, back, along(back, 2), per_owner, 1.0)
    parts = lax.all_to_all(after(parts, back_b).reshape(shards, rows, depth), "tp", 0, 0, tiled=True)
    back_b = share(back_b, swap(back_b, CORE), CORE)

    def grad_block(q):
        low, high = [lax.dynamic_slice_in_dim(x, (q & 1) * rows, rows, 0) for x in (grad01, grad23)]
        return jnp.where(q < 2, low, high)

    block = 512
    steps = hidden // block
    pieces = 4
    edges = [(-(-steps * n // pieces)) * block for n in range(pieces + 1)]
    kept, sent, got_c, got_x, done = [], [], [], [], []

    def make(n, *points):
        keep, send = project(after(all_tokens, *points), inner_rows, weight, up_flat, edges[n], edges[n + 1], block)
        kept.append(keep)
        got_c.append(swap(send, CORE))
        return keep

    def cross(n, *points):
        summed = (after(kept[n], *points)[rows:] + got_c[n][rows:]).astype(b16)
        got_x.append(swap(summed, CHIP))
        return summed

    def finish(n, *points):
        own = after(kept[n], *points)[:rows] + got_c[n][:rows] + got_x[n].astype(jnp.float32)
        done.append(own.astype(b16))
        return done[-1]

    point = make(0, back_b)
    back_b = share(after(back_b, point), swap(back_b, CHIP), CHIP)
    point = make(1, point)
    point = cross(0, point)
    point = make(2, point, back_b)
    point = finish(0, point)
    point = cross(1, point)
    point = make(3, point)
    point = finish(1, point)
    point = cross(2, point)
    down_wide = slot_grad(after(back_wide, point), [([x], n) for x, n in toks], width // 2)
    back_mine = lax.dynamic_slice_in_dim(back_b, j * rows, rows, 1)
    total = grad_block(j)
    for m in range(1, shards):
        total = total + lax.dynamic_index_in_dim(after(parts, down_wide), j ^ m, 0, False).astype(jnp.float32)
    total = (total + dot(back_mine, down_mine, (0, 0))).astype(b16)
    tokens_grad = both(total, [(b, a) for a, b in place])
    point = cross(3, total)
    point = finish(2, point)
    finish(3, point)
    projected = jnp.concatenate(done, axis=1)
    up_grad = up_wide.reshape(per_owner, rank, hidden)
    down_grad = jnp.swapaxes(down_wide.reshape(per_owner, rank, width), 1, 2)
    return projected, tokens_grad, down_grad, up_grad


def local_any(
    groups, tokens, weight, adapter_down, adapter_up, cotangent, block_adapter, block_length, adapter_slot
):
    bits = [1 << n for n in range((groups - 1).bit_length())]

    def swap(x, bit):
        return lax.ppermute(x, "dp", [(d, d ^ bit) for d in range(groups)])

    def gather(x):
        blocks = {0: x}
        for bit in reversed(bits):
            blocks.update({q | bit: swap(block, bit) for q, block in blocks.items()})
        return jnp.stack([blocks[q] for q in range(groups)])

    def combine(parts):
        for bit in bits:
            parts = [a + swap(b, bit) for a, b in zip(parts[::2], parts[1::2])]
        return parts[0]

    rows, width = tokens.shape
    depth, hidden = weight.shape
    per_owner, _, rank = adapter_down.shape
    i = lax.axis_index("dp")
    order = jnp.arange(groups, dtype=jnp.int32) ^ i
    owned, local_ids, live = block_facts(
        block_adapter, block_length, adapter_slot, order, rows, per_owner, i
    )
    down_sel = chosen(adapter_down, owned, local_ids)
    up_sel = chosen(adapter_up, owned, local_ids)
    all_tokens = lax.all_gather(lax.all_gather(tokens, "dp", axis=0), "tp", axis=2, tiled=True)
    all_tokens = lax.dynamic_slice_in_dim(all_tokens, i * depth, depth, 2)[order]
    all_tokens = all_tokens.reshape(groups * rows, depth)
    toks, cots = gather(tokens), gather(cotangent)
    tok_all, cot_all = toks.reshape(-1, width), cots.reshape(-1, hidden)
    down_mine = combine(down_sel)
    inner = jnp.stack([dot(toks[q], down_sel[q], (1, 0)) for q in range(groups)])
    inner_b = (lax.psum(inner, "tp") * live[:, :, None]).astype(jnp.bfloat16)
    back = jnp.stack([dot(cots[q], up_sel[q], (1, 1)) for q in range(groups)])
    back = lax.psum(back[order], ("tp", "dp"))[order] * (adapter_scale * live)[:, :, None]
    back_b = back.astype(jnp.bfloat16)
    one_hot = (local_ids[:, None] == jnp.arange(per_owner, dtype=jnp.int32)[None, :]) & owned[:, None]

    def spread(x):
        wide = jnp.where(one_hot[:, None, :, None], x[:, :, None, :], jnp.zeros((), x.dtype))
        return wide.reshape(groups * rows, per_owner * rank)

    inner_wide = spread(inner_b) * jnp.bfloat16(adapter_scale)
    total = dot(cot_all, weight, (1, 1)).reshape(groups, rows, 1, depth)[order]
    placed = jnp.zeros((groups, rows, groups, depth), jnp.float32)
    placed = lax.dynamic_update_slice_in_dim(placed, total, i, 2)
    placed = lax.psum_scatter(placed, "dp", scatter_dimension=0, tiled=False)
    placed = placed.reshape(rows, groups * depth)
    placed = lax.psum_scatter(placed, "tp", scatter_dimension=1, tiled=True)
    tokens_grad = (placed + dot(back_b[0], down_mine, (1, 1))).astype(jnp.bfloat16)
    part = dot(all_tokens, weight, (1, 0)) + dot(inner_wide, adapter_up.reshape(-1, hidden), (1, 0))
    projected = combine(list(part.reshape(groups, rows, hidden))).astype(jnp.bfloat16)
    up_grad = dot(inner_wide, cot_all, (0, 0)).reshape(per_owner, rank, hidden)
    down_grad = dot(spread(back_b), tok_all, (0, 0)).reshape(per_owner, rank, width)
    return projected, tokens_grad, jnp.swapaxes(down_grad, 1, 2), up_grad


def solution(mesh):
    placed = (
        P(("grp", "dp"), "tp"),
        P("dp", "tp"),
        P("dp", "tp", None),
        P("dp", None, "tp"),
        P(("grp", "dp"), "tp"),
        P("grp"),
        P("grp"),
        P(),
    )
    groups, shards = mesh.shape["dp"], mesh.shape["tp"]
    square = groups == shards == 4
    return jax.shard_map(
        local_square if square else functools.partial(local_any, groups),
        mesh=mesh,
        in_specs=placed,
        out_specs=(
            P(("grp", "dp"), "tp"),
            P(("grp", "dp"), "tp"),
            P(("grp", "dp"), "tp", None),
            P(("grp", "dp"), None, "tp"),
        ),
        check_vma=False,
    )
```

```python
import functools

import jax
import jax.numpy as jnp
from jax import lax
from jax.experimental import pallas as pl
from jax.experimental.pallas import tpu as pltpu
from jax.sharding import PartitionSpec as P

SEGMENT_BLOCK = 128

adapter_scale = 2.0
CORE, CHIP = 1, 2
VMEM = 48 * 1024 * 1024


def dot(a, b, contract):
    return lax.dot_general(a, b, ((contract[:1], contract[1:]), ((), ())), preferred_element_type=jnp.float32)


def after(x, *others):
    return lax.optimization_barrier((x,) + others)[0]


def cost(flops, moved, share=64):
    return pl.CostEstimate(flops=flops // share, bytes_accessed=moved // share, transcendentals=0)


def project(tokens, wide, weight, up_flat, start, stop, block):
    rows, depth = tokens.shape
    span = wide.shape[1]
    base = start // block

    def kernel(tok_ref, wide_ref, w_ref, up_ref, keep_ref, send_ref):
        total = dot(tok_ref[...], w_ref[...], (1, 0)) + dot(wide_ref[...], up_ref[...], (1, 0))
        keep_ref[...] = total[: rows // 2]
        send_ref[...] = total[rows // 2 :]

    return pl.pallas_call(
        kernel,
        grid=((stop - start) // block,),
        in_specs=[
            pl.BlockSpec(memory_space=pltpu.VMEM),
            pl.BlockSpec(memory_space=pltpu.VMEM),
            pl.BlockSpec((depth, block), lambda n: (0, n + base)),
            pl.BlockSpec((span, block), lambda n: (0, n + base)),
        ],
        out_specs=[pl.BlockSpec((rows // 2, block), lambda n: (0, n))] * 2,
        out_shape=[jax.ShapeDtypeStruct((rows // 2, stop - start), jnp.float32)] * 2,
        compiler_params=pltpu.CompilerParams(vmem_limit_bytes=VMEM),
        cost_estimate=cost(2 * rows * (depth + span) * (stop - start), 2 * (depth + span + 2 * rows) * (stop - start)),
        name="project",
    )(tokens, wide, weight, up_flat)


def return_grad(facts, first, second, weight, store, places, sent=()):
    rows, hidden = first.shape
    depth, rank = weight.shape[0], store.shape[1]
    groups = facts.shape[0] // 2
    block = 256
    half = places[0] // 2

    def kernel(facts_ref, a_ref, b_ref, w_ref, up_a_ref, up_b_ref, *refs):
        out_ref, sent_ref, rank_ref, rhs = refs[len(sent) :]
        n = pl.program_id(0)

        @pl.when(n == 0)
        def _():
            rhs[:rows] = a_ref[...]
            rhs[rows:] = b_ref[...]

        total = dot(w_ref[...], rhs[...], (1, 1)).T
        out_ref[...] = total
        sent_ref[...] = total.astype(first.dtype)

        @pl.when(n == pl.num_programs(0) - 1)
        def _():
            ranks = dot(jnp.concatenate([up_a_ref[0], up_b_ref[0]], axis=0), rhs[...], (1, 1))
            for at, place in enumerate(places):
                value = ranks[at * rank : (at + 1) * rank, at * rows : (at + 1) * rows]
                alive = lax.broadcasted_iota(jnp.int32, (rank, rows), 1) < facts_ref[groups + place]
                alive = alive & (facts_ref[place] >= 0)
                rank_ref[:, at * rows : (at + 1) * rows] = jnp.where(alive, value * adapter_scale, 0.0)

    def chosen_slot(place):
        return lambda n, facts_ref: (jnp.maximum(facts_ref[place], 0), 0, 0)

    return pl.pallas_call(
        kernel,
        grid_spec=pltpu.PrefetchScalarGridSpec(
            num_scalar_prefetch=1,
            grid=(depth // block,),
            in_specs=[
                pl.BlockSpec(memory_space=pltpu.VMEM),
                pl.BlockSpec(memory_space=pltpu.VMEM),
                pl.BlockSpec((block, hidden), lambda n, facts_ref: (n, 0)),
                *[pl.BlockSpec((1, rank, hidden), chosen_slot(place)) for place in places],
                *[pl.BlockSpec(memory_space=pl.ANY)] * len(sent),
            ],
            out_specs=[
                pl.BlockSpec((2 * rows, block), lambda n, facts_ref: (0, n)),
                pl.BlockSpec((2 * rows, block), lambda n, facts_ref: (half, n)),
                pl.BlockSpec((rank, 2 * rows), lambda n, facts_ref: (0, 0)),
            ],
            scratch_shapes=[pltpu.VMEM((2 * rows, hidden), first.dtype)],
        ),
        out_shape=[
            jax.ShapeDtypeStruct((2 * rows, depth), jnp.float32),
            jax.ShapeDtypeStruct((4 * rows, depth), first.dtype),
            jax.ShapeDtypeStruct((rank, 2 * rows), jnp.float32),
        ],
        input_output_aliases={6: 1} if sent else {},
        compiler_params=pltpu.CompilerParams(vmem_limit_bytes=VMEM),
        cost_estimate=cost(4 * rows * hidden * depth, 2 * hidden * (depth + 2 * rows)),
        name="return_grad",
    )(facts, first, second, weight, store, store, *sent)


def rank_inner(facts, flat, blocks, rank):
    span, width = flat.shape
    arrays, places = [x for x, _ in blocks], [n for _, n in blocks]
    groups = len(blocks)
    rows = arrays[0].shape[0] // 2
    slots = span // rank

    def kernel(facts_ref, flat_ref, *refs):
        out_ref = refs[-1]
        total = dot(flat_ref[...], jnp.concatenate([r[...] for r in refs[:-1]], axis=0), (1, 1))
        for q in range(groups):
            acc = jnp.zeros((rank, rows), jnp.float32)
            for s in range(slots):
                acc = jnp.where(facts_ref[q] == s, total[s * rank : (s + 1) * rank, q * rows : (q + 1) * rows], acc)
            alive = lax.broadcasted_iota(jnp.int32, (rank, rows), 1) < facts_ref[groups + q]
            out_ref[:, q * rows : (q + 1) * rows] = jnp.where(alive, acc, 0.0)

    return pl.pallas_call(
        kernel,
        grid=(1,),
        in_specs=[pl.BlockSpec(memory_space=pltpu.SMEM), pl.BlockSpec((span, width), lambda n: (0, 0))]
        + [pl.BlockSpec((rows, width), lambda n, place=place: (place, 0)) for place in places],
        out_specs=pl.BlockSpec((rank, groups * rows), lambda n: (0, 0)),
        out_shape=jax.ShapeDtypeStruct((rank, groups * rows), jnp.float32),
        compiler_params=pltpu.CompilerParams(vmem_limit_bytes=VMEM),
        cost_estimate=cost(2 * span * groups * rows * width, 2 * width * (span + groups * rows)),
        name="rank_inner",
    )(facts, flat, *arrays)


def spread(facts, here, there, slots, scale):
    rank, tokens = here.shape
    groups = facts.shape[0] // 2
    rows = tokens // groups
    values = [here] if there is None else [here, there]

    def kernel(facts_ref, *refs):
        wide_ref, turned_ref, sum_ref = refs[-3:]
        x = sum(r[...] for r in refs[:-3]).astype(jnp.bfloat16)
        sum_ref[...] = x
        x = x.astype(jnp.float32) * scale
        for q in range(groups):
            part = x[:, q * rows : (q + 1) * rows]
            for s in range(slots):
                value = jnp.where(facts_ref[q] == s, part, 0.0)
                wide_ref[s * rank : (s + 1) * rank, q * rows : (q + 1) * rows] = value.astype(jnp.bfloat16)
        for n, q in enumerate((0, 2, 1, 3)):
            part = wide_ref[:, q * rows : (q + 1) * rows]
            turned_ref[n * rows : (n + 1) * rows] = part.astype(jnp.float32).T.astype(jnp.bfloat16)

    return pl.pallas_call(
        kernel,
        in_specs=[pl.BlockSpec(memory_space=pltpu.SMEM)] + [pl.BlockSpec(memory_space=pltpu.VMEM)] * len(values),
        out_specs=[pl.BlockSpec(memory_space=pltpu.VMEM)] * 3,
        out_shape=[
            jax.ShapeDtypeStruct((slots * rank, tokens), jnp.bfloat16),
            jax.ShapeDtypeStruct((tokens, slots * rank), jnp.bfloat16),
            jax.ShapeDtypeStruct((rank, tokens), jnp.bfloat16),
        ],
        compiler_params=pltpu.CompilerParams(vmem_limit_bytes=VMEM),
        cost_estimate=cost(0, 8 * slots * rank * tokens),
        name="spread",
    )(facts, *values)


def slot_grad(wide_t, blocks, block):
    span, tokens = wide_t.shape
    groups = len(blocks)
    rows = tokens // groups
    columns = sum(x.shape[1] for x in blocks[0][0])
    arrays, specs = [], []
    for parts, place in blocks:
        first = 0
        for x in parts:
            count = x.shape[1] // block
            specs.append(
                pl.BlockSpec((rows, block), lambda n, a=first, b=count - 1, place=place: (place, jnp.clip(n - a, 0, b)))
            )
            arrays.append(x)
            first += count

    def kernel(wide_ref, *refs):
        n = pl.program_id(0)
        values, at = [], 0
        for parts, _ in blocks:
            value, first = refs[at][...], parts[0].shape[1] // block
            for more, x in enumerate(parts[1:], 1):
                value = jnp.where(n >= first, refs[at + more][...], value)
                first += x.shape[1] // block
            values.append(value)
            at += len(parts)
        refs[-1][...] = dot(wide_ref[...], jnp.concatenate(values, axis=0), (1, 0))

    return pl.pallas_call(
        kernel,
        grid=(columns // block,),
        in_specs=[pl.BlockSpec((span, tokens), lambda n: (0, 0))] + specs,
        out_specs=pl.BlockSpec((span, block), lambda n: (0, n)),
        out_shape=jax.ShapeDtypeStruct((span, columns), jnp.float32),
        compiler_params=pltpu.CompilerParams(vmem_limit_bytes=VMEM),
        cost_estimate=cost(2 * span * tokens * columns, (4 * span + 2 * tokens) * columns, 1),
        name="slot_grad",
    )(wide_t, *arrays)


def block_facts(block_adapter, block_length, adapter_slot, order, rows, per_owner, i):
    match = block_adapter[:, None] == jnp.arange(adapter_slot.shape[0], dtype=jnp.int32)[None, :]
    slots = jnp.sum(jnp.where(match, adapter_slot[None, :], 0), axis=1)[order]
    lengths = block_length[order]
    owned = slots // per_owner == i
    local_ids = slots % per_owner
    groups = order.shape[0]
    live = (lax.broadcasted_iota(jnp.int32, (groups, rows), 1) < lengths[:, None]).astype(jnp.float32)
    return owned, local_ids, live


def chosen(store, owned, local_ids):
    zero = jnp.zeros((), store.dtype)
    return [
        jnp.where(owned[q], lax.dynamic_index_in_dim(store, local_ids[q], 0, False), zero)
        for q in range(owned.shape[0])
    ]


def choose(block_adapter, block_length, adapter_slot, here, store):
    slots, rank, width = store.shape
    groups = block_adapter.shape[0]

    def block_of(step):
        return jnp.clip(jnp.where(step < 2, 2 * step + 1, 6 - 2 * step), 0, groups - 1)

    def slot_of(q, adapter_ref, slot_ref, here_ref):
        return slot_ref[adapter_ref[q ^ here_ref[0]]] - here_ref[0] * slots

    def kernel(adapter_ref, length_ref, slot_ref, here_ref, store_ref, near_ref, rest_ref, facts_ref):
        step = pl.program_id(0)

        @pl.when(step == 0)
        def _():
            for q in range(groups):
                at = slot_of(q, adapter_ref, slot_ref, here_ref)
                facts_ref[q] = jnp.where((at >= 0) & (at < slots), at, -1)
                facts_ref[groups + q] = length_ref[q ^ here_ref[0]]
            facts_ref[2 * groups] = here_ref[1]

        at = slot_of(block_of(step), adapter_ref, slot_ref, here_ref)
        value = store_ref[0] * ((at >= 0) & (at < slots)).astype(store_ref.dtype)

        @pl.when(step < 2)
        def _():
            near_ref[...] = value

        @pl.when(step >= 2)
        def _():
            rest_ref[...] = value

    def stored(step, adapter_ref, length_ref, slot_ref, here_ref):
        at = slot_of(block_of(step), adapter_ref, slot_ref, here_ref)
        return jnp.clip(at, 0, slots - 1), 0, 0

    return pl.pallas_call(
        kernel,
        grid_spec=pltpu.PrefetchScalarGridSpec(
            num_scalar_prefetch=4,
            grid=(groups,),
            in_specs=[pl.BlockSpec((1, rank, width), stored)],
            out_specs=[
                pl.BlockSpec((rank, width), lambda step, *refs: (jnp.minimum(step, 1), 0)),
                pl.BlockSpec((rank, width), lambda step, *refs: (jnp.maximum(step - 2, 0), 0)),
                pl.BlockSpec(memory_space=pltpu.SMEM),
            ],
        ),
        out_shape=[jax.ShapeDtypeStruct((2 * rank, width), store.dtype)] * 2
        + [jax.ShapeDtypeStruct((2 * groups + 1,), jnp.int32)],
        compiler_params=pltpu.CompilerParams(vmem_limit_bytes=VMEM),
        cost_estimate=cost(0, 8 * rank * width * groups),
        name="choose",
    )(block_adapter, block_length, adapter_slot, here, store)


def local_square(
    tokens, weight, adapter_down, adapter_up, cotangent, block_adapter, block_length, adapter_slot
):
    groups = shards = 4
    rows, width = tokens.shape
    depth, hidden = weight.shape
    per_owner, _, rank = adapter_down.shape
    span = per_owner * rank
    b16 = jnp.bfloat16
    i, j = lax.axis_index("dp"), lax.axis_index("tp")

    def swap(x, bit):
        return lax.ppermute(x, "dp", [(d, d ^ bit) for d in range(groups)])

    def along(x, bit):
        return lax.ppermute(x, "tp", [(z, z ^ bit) for z in range(shards)])

    place = [(c * groups + r, (r ^ c) * groups + c) for r in range(groups) for c in range(shards)]
    hop = [(d * groups + d, (d ^ 2) * groups + d) for d in range(groups)]
    hops = [(z * groups + d, (z ^ 1) * groups + d) for d in range(groups) for z in (d, d ^ 2)]

    def share(x, got, bit):
        return x + jnp.concatenate([got[:, (q ^ bit) * rows : ((q ^ bit) + 1) * rows] for q in range(groups)], axis=1)

    def both(x, pairs):
        return lax.ppermute(x, ("tp", "dp"), pairs)

    tok_x = swap(tokens, CHIP)
    cot_c = swap(cotangent, CORE)
    away = i ^ j
    here = jnp.stack([i, away]).astype(jnp.int32)
    down_t = jnp.swapaxes(adapter_down, 1, 2)
    near, rest, facts = choose(block_adapter, block_length, adapter_slot, here, down_t)
    up_flat = adapter_up.reshape(span, hidden)

    near = swap(near, CORE)
    even = jnp.concatenate([tokens, after(tok_x, facts)], axis=0)
    odd = swap(even, CORE)
    even_far = both(even, hop)
    cot_x = swap(after(cotangent, even), CHIP)
    grad01, parts, back01 = return_grad(facts, after(cotangent, odd), cot_c, weight, adapter_up, (0, 1))
    toks = [(even, 0), (odd, 0), (even, 1), (odd, 1)]
    inner = rank_inner(facts, down_t.reshape(span, width), [(after(x, grad01), n) for x, n in toks], rank)
    inner_near = along(inner, 1)
    odd_far = both(odd, hop)
    even_mid = jnp.where(away == 0, even, after(even_far, inner))
    even_all = both(even_mid, hops)
    inner = after(inner, even_mid) + inner_near
    cot_xc = swap(after(cot_x, inner), CORE)
    inner_far = along(inner, 2)
    down_x = swap(rest[:rank] + after(near, cot_x)[rank:], CHIP)
    grad23, parts, back23 = return_grad(
        facts, after(cot_x, inner), cot_xc, weight, adapter_up, (2, 3), (parts,)
    )
    odd_mid = jnp.where(away == 0, odd, after(odd_far, grad23))
    odd_all = both(odd_mid, hops)
    back = jnp.concatenate([back01, back23], axis=1)
    back_near = along(back, 1)
    all_even = jnp.where(away == 0, even, jnp.where(away == 2, even_far, after(even_all, odd_mid)))
    inner_wide, inner_rows, _ = spread(facts, after(inner, all_even), inner_far, per_owner, adapter_scale)
    cots = [([x], 0) for x in (cotangent, cot_c, cot_x, cot_xc)]
    up_wide = slot_grad(after(inner_wide, inner_rows), cots, hidden // 4)
    down_mine = both(rest[rank:] + near[:rank] + after(down_x, inner_rows), place)
    back = after(back, up_wide, down_mine) + back_near
    back_far = along(back, 2)
    all_odd = jnp.where(away == 0, odd, jnp.where(away == 2, odd_far, after(odd_all, back)))
    all_tokens = jnp.concatenate([all_even, all_odd], axis=0)
    back_wide, _, back_b = spread(facts, after(back, all_tokens), back_far, per_owner, 1.0)
    parts = lax.all_to_all(after(parts, back_b).reshape(shards, rows, depth), "tp", 0, 0, tiled=True)
    back_b = share(back_b, swap(back_b, CORE), CORE)

    def grad_block(q):
        low, high = [lax.dynamic_slice_in_dim(x, (q & 1) * rows, rows, 0) for x in (grad01, grad23)]
        return jnp.where(q < 2, low, high)

    block = 512
    steps = hidden // block
    pieces = 4
    edges = [(-(-steps * n // pieces)) * block for n in range(pieces + 1)]
    kept, sent, got_c, got_x, done = [], [], [], [], []

    def make(n, *points):
        keep, send = project(after(all_tokens, *points), inner_rows, weight, up_flat, edges[n], edges[n + 1], block)
        kept.append(keep)
        got_c.append(swap(send, CORE))
        return keep

    def cross(n, *points):
        summed = (after(kept[n], *points)[rows:] + got_c[n][rows:]).astype(b16)
        got_x.append(swap(summed, CHIP))
        return summed

    def finish(n, *points):
        own = after(kept[n], *points)[:rows] + got_c[n][:rows] + got_x[n].astype(jnp.float32)
        done.append(own.astype(b16))
        return done[-1]

    point = make(0, back_b)
    back_b = share(after(back_b, point), swap(back_b, CHIP), CHIP)
    point = make(1, point)
    point = cross(0, point)
    point = make(2, point, back_b)
    point = finish(0, point)
    point = cross(1, point)
    point = make(3, point)
    point = finish(1, point)
    point = cross(2, point)
    down_wide = slot_grad(after(back_wide, point), [([x], n) for x, n in toks], width // 2)
    back_mine = lax.dynamic_slice_in_dim(back_b, j * rows, rows, 1)
    total = grad_block(j)
    for m in range(1, shards):
        total = total + lax.dynamic_index_in_dim(after(parts, down_wide), j ^ m, 0, False).astype(jnp.float32)
    total = (total + dot(back_mine, down_mine, (0, 0))).astype(b16)
    tokens_grad = both(total, [(b, a) for a, b in place])
    point = cross(3, total)
    point = finish(2, point)
    finish(3, point)
    projected = jnp.concatenate(done, axis=1)
    up_grad = up_wide.reshape(per_owner, rank, hidden)
    down_grad = jnp.swapaxes(down_wide.reshape(per_owner, rank, width), 1, 2)
    return projected, tokens_grad, down_grad, up_grad


def local_any(
    groups, tokens, weight, adapter_down, adapter_up, cotangent, block_adapter, block_length, adapter_slot
):
    bits = [1 << n for n in range((groups - 1).bit_length())]

    def swap(x, bit):
        return lax.ppermute(x, "dp", [(d, d ^ bit) for d in range(groups)])

    def gather(x):
        blocks = {0: x}
        for bit in reversed(bits):
            blocks.update({q | bit: swap(block, bit) for q, block in blocks.items()})
        return jnp.stack([blocks[q] for q in range(groups)])

    def combine(parts):
        for bit in bits:
            parts = [a + swap(b, bit) for a, b in zip(parts[::2], parts[1::2])]
        return parts[0]

    rows, width = tokens.shape
    depth, hidden = weight.shape
    per_owner, _, rank = adapter_down.shape
    i = lax.axis_index("dp")
    order = jnp.arange(groups, dtype=jnp.int32) ^ i
    owned, local_ids, live = block_facts(
        block_adapter, block_length, adapter_slot, order, rows, per_owner, i
    )
    down_sel = chosen(adapter_down, owned, local_ids)
    up_sel = chosen(adapter_up, owned, local_ids)
    all_tokens = lax.all_gather(lax.all_gather(tokens, "dp", axis=0), "tp", axis=2, tiled=True)
    all_tokens = lax.dynamic_slice_in_dim(all_tokens, i * depth, depth, 2)[order]
    all_tokens = all_tokens.reshape(groups * rows, depth)
    toks, cots = gather(tokens), gather(cotangent)
    tok_all, cot_all = toks.reshape(-1, width), cots.reshape(-1, hidden)
    down_mine = combine(down_sel)
    inner = jnp.stack([dot(toks[q], down_sel[q], (1, 0)) for q in range(groups)])
    inner_b = (lax.psum(inner, "tp") * live[:, :, None]).astype(jnp.bfloat16)
    back = jnp.stack([dot(cots[q], up_sel[q], (1, 1)) for q in range(groups)])
    back = lax.psum(back[order], ("tp", "dp"))[order] * (adapter_scale * live)[:, :, None]
    back_b = back.astype(jnp.bfloat16)
    one_hot = (local_ids[:, None] == jnp.arange(per_owner, dtype=jnp.int32)[None, :]) & owned[:, None]

    def spread(x):
        wide = jnp.where(one_hot[:, None, :, None], x[:, :, None, :], jnp.zeros((), x.dtype))
        return wide.reshape(groups * rows, per_owner * rank)

    inner_wide = spread(inner_b) * jnp.bfloat16(adapter_scale)
    total = dot(cot_all, weight, (1, 1)).reshape(groups, rows, 1, depth)[order]
    placed = jnp.zeros((groups, rows, groups, depth), jnp.float32)
    placed = lax.dynamic_update_slice_in_dim(placed, total, i, 2)
    placed = lax.psum_scatter(placed, "dp", scatter_dimension=0, tiled=False)
    placed = placed.reshape(rows, groups * depth)
    placed = lax.psum_scatter(placed, "tp", scatter_dimension=1, tiled=True)
    tokens_grad = (placed + dot(back_b[0], down_mine, (1, 1))).astype(jnp.bfloat16)
    part = dot(all_tokens, weight, (1, 0)) + dot(inner_wide, adapter_up.reshape(-1, hidden), (1, 0))
    projected = combine(list(part.reshape(groups, rows, hidden))).astype(jnp.bfloat16)
    up_grad = dot(inner_wide, cot_all, (0, 0)).reshape(per_owner, rank, hidden)
    down_grad = dot(spread(back_b), tok_all, (0, 0)).reshape(per_owner, rank, width)
    return projected, tokens_grad, jnp.swapaxes(down_grad, 1, 2), up_grad


def solution(mesh):
    placed = (
        P(("grp", "dp"), "tp"),
        P("dp", "tp"),
        P("dp", "tp", None),
        P("dp", None, "tp"),
        P(("grp", "dp"), "tp"),
        P("grp"),
        P("grp"),
        P(),
    )
    groups, shards = mesh.shape["dp"], mesh.shape["tp"]
    square = groups == shards == 4
    return jax.shard_map(
        local_square if square else functools.partial(local_any, groups),
        mesh=mesh,
        in_specs=placed,
        out_specs=(
            P(("grp", "dp"), "tp"),
            P(("grp", "dp"), "tp"),
            P(("grp", "dp"), "tp", None),
            P(("grp", "dp"), None, "tp"),
        ),
        check_vma=False,
    )
```

```python
import functools

import jax
import jax.numpy as jnp
from jax import lax
from jax.experimental import pallas as pl
from jax.experimental.pallas import tpu as pltpu
from jax.sharding import PartitionSpec as P

SEGMENT_BLOCK = 128

adapter_scale = 2.0
CORE, CHIP = 1, 2
VMEM = 48 * 1024 * 1024


def dot(a, b, contract):
    return lax.dot_general(a, b, ((contract[:1], contract[1:]), ((), ())), preferred_element_type=jnp.float32)


def after(x, *others):
    return lax.optimization_barrier((x,) + others)[0]


def cost(flops, moved, share=64):
    return pl.CostEstimate(flops=flops // share, bytes_accessed=moved // share, transcendentals=0)


def project(tokens, wide, weight, up_flat, start, stop, block):
    rows, depth = tokens.shape
    span = wide.shape[1]
    base = start // block

    def kernel(tok_ref, wide_ref, w_ref, up_ref, keep_ref, send_ref):
        total = dot(tok_ref[...], w_ref[...], (1, 0)) + dot(wide_ref[...], up_ref[...], (1, 0))
        keep_ref[...] = total[: rows // 2]
        send_ref[...] = total[rows // 2 :]

    return pl.pallas_call(
        kernel,
        grid=((stop - start) // block,),
        in_specs=[
            pl.BlockSpec(memory_space=pltpu.VMEM),
            pl.BlockSpec(memory_space=pltpu.VMEM),
            pl.BlockSpec((depth, block), lambda n: (0, n + base)),
            pl.BlockSpec((span, block), lambda n: (0, n + base)),
        ],
        out_specs=[pl.BlockSpec((rows // 2, block), lambda n: (0, n))] * 2,
        out_shape=[jax.ShapeDtypeStruct((rows // 2, stop - start), jnp.float32)] * 2,
        compiler_params=pltpu.CompilerParams(vmem_limit_bytes=VMEM),
        cost_estimate=cost(2 * rows * (depth + span) * (stop - start), 2 * (depth + span + 2 * rows) * (stop - start)),
        name="project",
    )(tokens, wide, weight, up_flat)


def return_grad(facts, first, second, weight, store, places, sent=()):
    rows, hidden = first.shape
    depth, rank = weight.shape[0], store.shape[1]
    groups = facts.shape[0] // 2
    block = 256
    half = places[0] // 2

    def kernel(facts_ref, a_ref, b_ref, w_ref, up_a_ref, up_b_ref, *refs):
        out_ref, sent_ref, rank_ref, rhs = refs[len(sent) :]
        n = pl.program_id(0)

        @pl.when(n == 0)
        def _():
            rhs[:rows] = a_ref[...]
            rhs[rows:] = b_ref[...]

        total = dot(w_ref[...], rhs[...], (1, 1)).T
        out_ref[...] = total
        sent_ref[...] = total.astype(first.dtype)

        @pl.when(n == pl.num_programs(0) - 1)
        def _():
            ranks = dot(jnp.concatenate([up_a_ref[0], up_b_ref[0]], axis=0), rhs[...], (1, 1))
            for at, place in enumerate(places):
                value = ranks[at * rank : (at + 1) * rank, at * rows : (at + 1) * rows]
                alive = lax.broadcasted_iota(jnp.int32, (rank, rows), 1) < facts_ref[groups + place]
                alive = alive & (facts_ref[place] >= 0)
                rank_ref[:, at * rows : (at + 1) * rows] = jnp.where(alive, value * adapter_scale, 0.0)

    def chosen_slot(place):
        return lambda n, facts_ref: (jnp.maximum(facts_ref[place], 0), 0, 0)

    return pl.pallas_call(
        kernel,
        grid_spec=pltpu.PrefetchScalarGridSpec(
            num_scalar_prefetch=1,
            grid=(depth // block,),
            in_specs=[
                pl.BlockSpec(memory_space=pltpu.VMEM),
                pl.BlockSpec(memory_space=pltpu.VMEM),
                pl.BlockSpec((block, hidden), lambda n, facts_ref: (n, 0)),
                *[pl.BlockSpec((1, rank, hidden), chosen_slot(place)) for place in places],
                *[pl.BlockSpec(memory_space=pl.ANY)] * len(sent),
            ],
            out_specs=[
                pl.BlockSpec((2 * rows, block), lambda n, facts_ref: (0, n)),
                pl.BlockSpec((2 * rows, block), lambda n, facts_ref: (half, n)),
                pl.BlockSpec((rank, 2 * rows), lambda n, facts_ref: (0, 0)),
            ],
            scratch_shapes=[pltpu.VMEM((2 * rows, hidden), first.dtype)],
        ),
        out_shape=[
            jax.ShapeDtypeStruct((2 * rows, depth), jnp.float32),
            jax.ShapeDtypeStruct((4 * rows, depth), first.dtype),
            jax.ShapeDtypeStruct((rank, 2 * rows), jnp.float32),
        ],
        input_output_aliases={6: 1} if sent else {},
        compiler_params=pltpu.CompilerParams(vmem_limit_bytes=VMEM),
        cost_estimate=cost(4 * rows * hidden * depth, 2 * hidden * (depth + 2 * rows)),
        name="return_grad",
    )(facts, first, second, weight, store, store, *sent)


def rank_inner(facts, flat, blocks, rank):
    span, width = flat.shape
    arrays, places = [x for x, _ in blocks], [n for _, n in blocks]
    groups = len(blocks)
    rows = arrays[0].shape[0] // 2
    slots = span // rank

    def kernel(facts_ref, flat_ref, *refs):
        out_ref = refs[-1]
        total = dot(flat_ref[...], jnp.concatenate([r[...] for r in refs[:-1]], axis=0), (1, 1))
        for q in range(groups):
            acc = jnp.zeros((rank, rows), jnp.float32)
            for s in range(slots):
                acc = jnp.where(facts_ref[q] == s, total[s * rank : (s + 1) * rank, q * rows : (q + 1) * rows], acc)
            alive = lax.broadcasted_iota(jnp.int32, (rank, rows), 1) < facts_ref[groups + q]
            out_ref[:, q * rows : (q + 1) * rows] = jnp.where(alive, acc, 0.0)

    return pl.pallas_call(
        kernel,
        grid=(1,),
        in_specs=[pl.BlockSpec(memory_space=pltpu.SMEM), pl.BlockSpec((span, width), lambda n: (0, 0))]
        + [pl.BlockSpec((rows, width), lambda n, place=place: (place, 0)) for place in places],
        out_specs=pl.BlockSpec((rank, groups * rows), lambda n: (0, 0)),
        out_shape=jax.ShapeDtypeStruct((rank, groups * rows), jnp.float32),
        compiler_params=pltpu.CompilerParams(vmem_limit_bytes=VMEM),
        cost_estimate=cost(2 * span * groups * rows * width, 2 * width * (span + groups * rows)),
        name="rank_inner",
    )(facts, flat, *arrays)


def spread(facts, here, there, slots, scale):
    rank, tokens = here.shape
    groups = facts.shape[0] // 2
    rows = tokens // groups
    values = [here] if there is None else [here, there]

    def kernel(facts_ref, *refs):
        wide_ref, turned_ref, sum_ref = refs[-3:]
        x = sum(r[...] for r in refs[:-3]).astype(jnp.bfloat16)
        sum_ref[...] = x
        x = x.astype(jnp.float32) * scale
        for q in range(groups):
            part = x[:, q * rows : (q + 1) * rows]
            for s in range(slots):
                value = jnp.where(facts_ref[q] == s, part, 0.0)
                wide_ref[s * rank : (s + 1) * rank, q * rows : (q + 1) * rows] = value.astype(jnp.bfloat16)
        for n, q in enumerate((0, 2, 1, 3)):
            part = wide_ref[:, q * rows : (q + 1) * rows]
            turned_ref[n * rows : (n + 1) * rows] = part.astype(jnp.float32).T.astype(jnp.bfloat16)

    return pl.pallas_call(
        kernel,
        in_specs=[pl.BlockSpec(memory_space=pltpu.SMEM)] + [pl.BlockSpec(memory_space=pltpu.VMEM)] * len(values),
        out_specs=[pl.BlockSpec(memory_space=pltpu.VMEM)] * 3,
        out_shape=[
            jax.ShapeDtypeStruct((slots * rank, tokens), jnp.bfloat16),
            jax.ShapeDtypeStruct((tokens, slots * rank), jnp.bfloat16),
            jax.ShapeDtypeStruct((rank, tokens), jnp.bfloat16),
        ],
        compiler_params=pltpu.CompilerParams(vmem_limit_bytes=VMEM),
        cost_estimate=cost(0, 8 * slots * rank * tokens),
        name="spread",
    )(facts, *values)


def slot_grad(wide_t, blocks, block):
    span, tokens = wide_t.shape
    groups = len(blocks)
    rows = tokens // groups
    columns = sum(x.shape[1] for x in blocks[0][0])
    arrays, specs = [], []
    for parts, place in blocks:
        first = 0
        for x in parts:
            count = x.shape[1] // block
            specs.append(
                pl.BlockSpec((rows, block), lambda n, a=first, b=count - 1, place=place: (place, jnp.clip(n - a, 0, b)))
            )
            arrays.append(x)
            first += count

    def kernel(wide_ref, *refs):
        n = pl.program_id(0)
        values, at = [], 0
        for parts, _ in blocks:
            value, first = refs[at][...], parts[0].shape[1] // block
            for more, x in enumerate(parts[1:], 1):
                value = jnp.where(n >= first, refs[at + more][...], value)
                first += x.shape[1] // block
            values.append(value)
            at += len(parts)
        refs[-1][...] = dot(wide_ref[...], jnp.concatenate(values, axis=0), (1, 0))

    return pl.pallas_call(
        kernel,
        grid=(columns // block,),
        in_specs=[pl.BlockSpec((span, tokens), lambda n: (0, 0))] + specs,
        out_specs=pl.BlockSpec((span, block), lambda n: (0, n)),
        out_shape=jax.ShapeDtypeStruct((span, columns), jnp.float32),
        compiler_params=pltpu.CompilerParams(vmem_limit_bytes=VMEM),
        cost_estimate=cost(3 * 2 * span * tokens * columns, 3 * (4 * span + 2 * tokens) * columns, 1),
        name="slot_grad",
    )(wide_t, *arrays)


def block_facts(block_adapter, block_length, adapter_slot, order, rows, per_owner, i):
    match = block_adapter[:, None] == jnp.arange(adapter_slot.shape[0], dtype=jnp.int32)[None, :]
    slots = jnp.sum(jnp.where(match, adapter_slot[None, :], 0), axis=1)[order]
    lengths = block_length[order]
    owned = slots // per_owner == i
    local_ids = slots % per_owner
    groups = order.shape[0]
    live = (lax.broadcasted_iota(jnp.int32, (groups, rows), 1) < lengths[:, None]).astype(jnp.float32)
    return owned, local_ids, live


def chosen(store, owned, local_ids):
    zero = jnp.zeros((), store.dtype)
    return [
        jnp.where(owned[q], lax.dynamic_index_in_dim(store, local_ids[q], 0, False), zero)
        for q in range(owned.shape[0])
    ]


def choose(block_adapter, block_length, adapter_slot, here, store):
    slots, rank, width = store.shape
    groups = block_adapter.shape[0]

    def block_of(step):
        return jnp.clip(jnp.where(step < 2, 2 * step + 1, 6 - 2 * step), 0, groups - 1)

    def slot_of(q, adapter_ref, slot_ref, here_ref):
        return slot_ref[adapter_ref[q ^ here_ref[0]]] - here_ref[0] * slots

    def kernel(adapter_ref, length_ref, slot_ref, here_ref, store_ref, near_ref, rest_ref, facts_ref):
        step = pl.program_id(0)

        @pl.when(step == 0)
        def _():
            for q in range(groups):
                at = slot_of(q, adapter_ref, slot_ref, here_ref)
                facts_ref[q] = jnp.where((at >= 0) & (at < slots), at, -1)
                facts_ref[groups + q] = length_ref[q ^ here_ref[0]]
            facts_ref[2 * groups] = here_ref[1]

        at = slot_of(block_of(step), adapter_ref, slot_ref, here_ref)
        value = store_ref[0] * ((at >= 0) & (at < slots)).astype(store_ref.dtype)

        @pl.when(step < 2)
        def _():
            near_ref[...] = value

        @pl.when(step >= 2)
        def _():
            rest_ref[...] = value

    def stored(step, adapter_ref, length_ref, slot_ref, here_ref):
        at = slot_of(block_of(step), adapter_ref, slot_ref, here_ref)
        return jnp.clip(at, 0, slots - 1), 0, 0

    return pl.pallas_call(
        kernel,
        grid_spec=pltpu.PrefetchScalarGridSpec(
            num_scalar_prefetch=4,
            grid=(groups,),
            in_specs=[pl.BlockSpec((1, rank, width), stored)],
            out_specs=[
                pl.BlockSpec((rank, width), lambda step, *refs: (jnp.minimum(step, 1), 0)),
                pl.BlockSpec((rank, width), lambda step, *refs: (jnp.maximum(step - 2, 0), 0)),
                pl.BlockSpec(memory_space=pltpu.SMEM),
            ],
        ),
        out_shape=[jax.ShapeDtypeStruct((2 * rank, width), store.dtype)] * 2
        + [jax.ShapeDtypeStruct((2 * groups + 1,), jnp.int32)],
        compiler_params=pltpu.CompilerParams(vmem_limit_bytes=VMEM),
        cost_estimate=cost(0, 8 * rank * width * groups),
        name="choose",
    )(block_adapter, block_length, adapter_slot, here, store)


def local_square(
    tokens, weight, adapter_down, adapter_up, cotangent, block_adapter, block_length, adapter_slot
):
    groups = shards = 4
    rows, width = tokens.shape
    depth, hidden = weight.shape
    per_owner, _, rank = adapter_down.shape
    span = per_owner * rank
    b16 = jnp.bfloat16
    i, j = lax.axis_index("dp"), lax.axis_index("tp")

    def swap(x, bit):
        return lax.ppermute(x, "dp", [(d, d ^ bit) for d in range(groups)])

    def along(x, bit):
        return lax.ppermute(x, "tp", [(z, z ^ bit) for z in range(shards)])

    place = [(c * groups + r, (r ^ c) * groups + c) for r in range(groups) for c in range(shards)]
    hop = [(d * groups + d, (d ^ 2) * groups + d) for d in range(groups)]
    hops = [(z * groups + d, (z ^ 1) * groups + d) for d in range(groups) for z in (d, d ^ 2)]

    def share(x, got, bit):
        return x + jnp.concatenate([got[:, (q ^ bit) * rows : ((q ^ bit) + 1) * rows] for q in range(groups)], axis=1)

    def both(x, pairs):
        return lax.ppermute(x, ("tp", "dp"), pairs)

    tok_x = swap(tokens, CHIP)
    cot_c = swap(cotangent, CORE)
    away = i ^ j
    here = jnp.stack([i, away]).astype(jnp.int32)
    down_t = jnp.swapaxes(adapter_down, 1, 2)
    near, rest, facts = choose(block_adapter, block_length, adapter_slot, here, down_t)
    up_flat = adapter_up.reshape(span, hidden)

    near = swap(near, CORE)
    even = jnp.concatenate([tokens, after(tok_x, facts)], axis=0)
    odd = swap(even, CORE)
    even_far = both(even, hop)
    cot_x = swap(after(cotangent, even), CHIP)
    grad01, parts, back01 = return_grad(facts, after(cotangent, odd), cot_c, weight, adapter_up, (0, 1))
    toks = [(even, 0), (odd, 0), (even, 1), (odd, 1)]
    inner = rank_inner(facts, down_t.reshape(span, width), [(after(x, grad01), n) for x, n in toks], rank)
    inner_near = along(inner, 1)
    odd_far = both(odd, hop)
    even_mid = jnp.where(away == 0, even, after(even_far, inner))
    even_all = both(even_mid, hops)
    inner = after(inner, even_mid) + inner_near
    cot_xc = swap(after(cot_x, inner), CORE)
    inner_far = along(inner, 2)
    down_x = swap(rest[:rank] + after(near, cot_x)[rank:], CHIP)
    grad23, parts, back23 = return_grad(
        facts, after(cot_x, inner), cot_xc, weight, adapter_up, (2, 3), (parts,)
    )
    odd_mid = jnp.where(away == 0, odd, after(odd_far, grad23))
    odd_all = both(odd_mid, hops)
    back = jnp.concatenate([back01, back23], axis=1)
    back_near = along(back, 1)
    all_even = jnp.where(away == 0, even, jnp.where(away == 2, even_far, after(even_all, odd_mid)))
    inner_wide, inner_rows, _ = spread(facts, after(inner, all_even), inner_far, per_owner, adapter_scale)
    cots = [([x], 0) for x in (cotangent, cot_c, cot_x, cot_xc)]
    up_wide = slot_grad(after(inner_wide, inner_rows), cots, hidden // 4)
    down_mine = both(rest[rank:] + near[:rank] + after(down_x, inner_rows), place)
    back = after(back, up_wide, down_mine) + back_near
    back_far = along(back, 2)
    all_odd = jnp.where(away == 0, odd, jnp.where(away == 2, odd_far, after(odd_all, back)))
    all_tokens = jnp.concatenate([all_even, all_odd], axis=0)
    back_wide, _, back_b = spread(facts, after(back, all_tokens), back_far, per_owner, 1.0)
    parts = lax.all_to_all(after(parts, back_b).reshape(shards, rows, depth), "tp", 0, 0, tiled=True)
    back_b = share(back_b, swap(back_b, CORE), CORE)

    def grad_block(q):
        low, high = [lax.dynamic_slice_in_dim(x, (q & 1) * rows, rows, 0) for x in (grad01, grad23)]
        return jnp.where(q < 2, low, high)

    block = 512
    steps = hidden // block
    pieces = 4
    edges = [(-(-steps * n // pieces)) * block for n in range(pieces + 1)]
    kept, sent, got_c, got_x, done = [], [], [], [], []

    def make(n, *points):
        keep, send = project(after(all_tokens, *points), inner_rows, weight, up_flat, edges[n], edges[n + 1], block)
        kept.append(keep)
        got_c.append(swap(send, CORE))
        return keep

    def cross(n, *points):
        summed = (after(kept[n], *points)[rows:] + got_c[n][rows:]).astype(b16)
        got_x.append(swap(summed, CHIP))
        return summed

    def finish(n, *points):
        own = after(kept[n], *points)[:rows] + got_c[n][:rows] + got_x[n].astype(jnp.float32)
        done.append(own.astype(b16))
        return done[-1]

    point = make(0, back_b)
    back_b = share(after(back_b, point), swap(back_b, CHIP), CHIP)
    point = make(1, point)
    point = cross(0, point)
    point = make(2, point, back_b)
    point = finish(0, point)
    point = cross(1, point)
    point = make(3, point)
    point = finish(1, point)
    point = cross(2, point)
    down_wide = slot_grad(after(back_wide, point), [([x], n) for x, n in toks], width // 2)
    point = cross(3, down_wide, parts)
    back_mine = lax.dynamic_slice_in_dim(back_b, j * rows, rows, 1)
    total = grad_block(j)
    for m in range(1, shards):
        total = total + lax.dynamic_index_in_dim(after(parts, point), j ^ m, 0, False).astype(jnp.float32)
    total = (total + dot(back_mine, down_mine, (0, 0))).astype(b16)
    tokens_grad = both(total, [(b, a) for a, b in place])
    point = finish(2, total)
    finish(3, point)
    projected = jnp.concatenate(done, axis=1)
    up_grad = up_wide.reshape(per_owner, rank, hidden)
    down_grad = jnp.swapaxes(down_wide.reshape(per_owner, rank, width), 1, 2)
    return projected, tokens_grad, down_grad, up_grad


def local_any(
    groups, tokens, weight, adapter_down, adapter_up, cotangent, block_adapter, block_length, adapter_slot
):
    bits = [1 << n for n in range((groups - 1).bit_length())]

    def swap(x, bit):
        return lax.ppermute(x, "dp", [(d, d ^ bit) for d in range(groups)])

    def gather(x):
        blocks = {0: x}
        for bit in reversed(bits):
            blocks.update({q | bit: swap(block, bit) for q, block in blocks.items()})
        return jnp.stack([blocks[q] for q in range(groups)])

    def combine(parts):
        for bit in bits:
            parts = [a + swap(b, bit) for a, b in zip(parts[::2], parts[1::2])]
        return parts[0]

    rows, width = tokens.shape
    depth, hidden = weight.shape
    per_owner, _, rank = adapter_down.shape
    i = lax.axis_index("dp")
    order = jnp.arange(groups, dtype=jnp.int32) ^ i
    owned, local_ids, live = block_facts(
        block_adapter, block_length, adapter_slot, order, rows, per_owner, i
    )
    down_sel = chosen(adapter_down, owned, local_ids)
    up_sel = chosen(adapter_up, owned, local_ids)
    all_tokens = lax.all_gather(lax.all_gather(tokens, "dp", axis=0), "tp", axis=2, tiled=True)
    all_tokens = lax.dynamic_slice_in_dim(all_tokens, i * depth, depth, 2)[order]
    all_tokens = all_tokens.reshape(groups * rows, depth)
    toks, cots = gather(tokens), gather(cotangent)
    tok_all, cot_all = toks.reshape(-1, width), cots.reshape(-1, hidden)
    down_mine = combine(down_sel)
    inner = jnp.stack([dot(toks[q], down_sel[q], (1, 0)) for q in range(groups)])
    inner_b = (lax.psum(inner, "tp") * live[:, :, None]).astype(jnp.bfloat16)
    back = jnp.stack([dot(cots[q], up_sel[q], (1, 1)) for q in range(groups)])
    back = lax.psum(back[order], ("tp", "dp"))[order] * (adapter_scale * live)[:, :, None]
    back_b = back.astype(jnp.bfloat16)
    one_hot = (local_ids[:, None] == jnp.arange(per_owner, dtype=jnp.int32)[None, :]) & owned[:, None]

    def spread(x):
        wide = jnp.where(one_hot[:, None, :, None], x[:, :, None, :], jnp.zeros((), x.dtype))
        return wide.reshape(groups * rows, per_owner * rank)

    inner_wide = spread(inner_b) * jnp.bfloat16(adapter_scale)
    total = dot(cot_all, weight, (1, 1)).reshape(groups, rows, 1, depth)[order]
    placed = jnp.zeros((groups, rows, groups, depth), jnp.float32)
    placed = lax.dynamic_update_slice_in_dim(placed, total, i, 2)
    placed = lax.psum_scatter(placed, "dp", scatter_dimension=0, tiled=False)
    placed = placed.reshape(rows, groups * depth)
    placed = lax.psum_scatter(placed, "tp", scatter_dimension=1, tiled=True)
    tokens_grad = (placed + dot(back_b[0], down_mine, (1, 1))).astype(jnp.bfloat16)
    part = dot(all_tokens, weight, (1, 0)) + dot(inner_wide, adapter_up.reshape(-1, hidden), (1, 0))
    projected = combine(list(part.reshape(groups, rows, hidden))).astype(jnp.bfloat16)
    up_grad = dot(inner_wide, cot_all, (0, 0)).reshape(per_owner, rank, hidden)
    down_grad = dot(spread(back_b), tok_all, (0, 0)).reshape(per_owner, rank, width)
    return projected, tokens_grad, jnp.swapaxes(down_grad, 1, 2), up_grad


def solution(mesh):
    placed = (
        P(("grp", "dp"), "tp"),
        P("dp", "tp"),
        P("dp", "tp", None),
        P("dp", None, "tp"),
        P(("grp", "dp"), "tp"),
        P("grp"),
        P("grp"),
        P(),
    )
    groups, shards = mesh.shape["dp"], mesh.shape["tp"]
    square = groups == shards == 4
    return jax.shard_map(
        local_square if square else functools.partial(local_any, groups),
        mesh=mesh,
        in_specs=placed,
        out_specs=(
            P(("grp", "dp"), "tp"),
            P(("grp", "dp"), "tp"),
            P(("grp", "dp"), "tp", None),
            P(("grp", "dp"), None, "tp"),
        ),
        check_vma=False,
    )
```
